128 devices in a mesh: row: 4 (over x_lo, core), col: 32 (over x_hi, y, z).
Axes of the slice: x: 4 (x_hi: 2, x_lo: 2; x = x_hi * 2 + x_lo), y: 4, z: 4, core: 2. Of those that a mesh axis runs over, the one named last changes fastest.
Arguments:
- latent: bfloat16 [32, 8, 64, 1536], P(None, 'row', 'col'), may hold values from -6 to 6
- out_grad: bfloat16 [32, 8, 64, 1536], P(None, 'row', 'col'), may hold values from -6 to 6
- w_in: bfloat16 [1536, 1536], replicated, may hold values from -0.15625 to 0.15625
- w_out: bfloat16 [1536, 1536], replicated, may hold values from -0.15625 to 0.15625
- w_select: bfloat16 [1536, 128], replicated, may hold values from -0.15625 to 0.15625
- w_dt: bfloat16 [1536, 96], replicated, may hold values from -0.625 to 0.625
- dt_bias: float32 [1536], replicated, may hold values from -4 to -1
- a_log: float32 [1536, 16], replicated, may hold values from -3 to 1
- d_skip: float32 [1536], replicated, may hold values from 0.5 to 1.5
- w_mod: bfloat16 [3072, 256], replicated, may hold values from -0.375 to 0.375
- t_index: int32 [1], replicated, may hold values from 0 to 999
- frame_order: int32 [32], replicated, may hold values from 0 to 31, each once
- row_order: int32 [8], replicated, may hold values from 0 to 7, each once
- col_order: int32 [64], replicated, may hold values from 0 to 63, each once
Outputs:
- branch_out: bfloat16 [32, 8, 64, 1536], P(None, 'row', 'col')
- latent_grad: bfloat16 [32, 8, 64, 1536], P(None, 'row', 'col')
- grad_w_in: float32 [1536, 1536], P(('row', 'col'))
- grad_w_out: float32 [1536, 1536], P(('row', 'col'))
- grad_w_select: float32 [1536, 128], P(('row', 'col'))
- grad_w_dt: float32 [1536, 96], P(('row', 'col'))
- grad_dt_bias: float32 [1536], P(('row', 'col'))
- grad_a_log: float32 [1536, 16], P(('row', 'col'))
- grad_d_skip: float32 [1536], P(('row', 'col'))
- grad_w_mod: float32 [3072, 256], P(('row', 'col'))
The draws below stay inside these ranges and needn't reach their ends.
Inputs may be any that keep to these rules, and one draw needn't show every extreme that they name: `frame_order`: each frame index appears once. `row_order`: each row index appears once. `col_order`: each column index appears once.
All inputs are finite; a program needn't handle non-finite values.
Results may differ from the reference program's by a relative error of at most 0.015.
Values may be sent and summed in bfloat16 or wider, within the bound.
No kernel may reach another device: no remote copies, remote signals or barrier semaphores. Data moves between devices by JAX's collectives and lax.ppermute only.
A program may use at most 192 MiB of HBM per device.

```python
import math
import jax
import jax.numpy as jnp
from jax import lax

D = 1536
E = 1536
N = 16
R = 96
TS = 256
F = 32
H = 8
W = 64


def steps_of(rng, shape, cuts, low, high):
    factor_of = 1.0
    for axis_at, blocks in cuts:
        draws = jax.random.uniform(jax.random.fold_in(jax.random.fold_in(rng, 6), axis_at), (blocks,), jnp.float32, low / len(cuts), high / len(cuts))
        factor_of = factor_of * jnp.repeat(jnp.exp(draws), shape[axis_at] // blocks).reshape((-1,) + (1,) * (len(shape) - 1 - axis_at))
    return factor_of


def bell_draw(own_key, shape, scale, bound, cuts=(), kind=jnp.bfloat16):
    values = jax.random.normal(own_key, shape, jnp.float32) * scale
    if len(cuts) > 0:
        values = steps_of(own_key, shape, cuts, -0.22, 0.18) * values
    return jnp.clip(values, min=-bound, max=bound).astype(kind)


def setup_inputs(seed: int = 0) -> dict:
    seeds = jax.random.split(jax.random.key(seed), 15)
    latent = bell_draw(seeds[0], (F, H, W, D), 1.0, 6.0, ((1, 4), (2, 32)))
    out_grad = bell_draw(seeds[1], (F, H, W, D), 1.0, 6.0, ((1, 4), (2, 32)))
    w_in = bell_draw(seeds[2], (D, E), D ** -0.5, 0.15625)
    w_out = bell_draw(seeds[3], (E, D), E ** -0.5, 0.15625)
    w_select = bell_draw(seeds[4], (E, R + 2 * N), E ** -0.5, 0.15625)
    w_dt = bell_draw(seeds[5], (E, R), R ** -0.5, 0.625)
    dt_bias = jnp.clip(jax.random.uniform(seeds[6], (E,), jnp.float32, -4.0, -1.0), -4.0, -1.0)
    a_log = jnp.clip(jax.random.uniform(seeds[7], (E, N), jnp.float32, -3.0, 1.0), -3.0, 1.0)
    d_skip = jnp.clip(jax.random.uniform(seeds[8], (E,), jnp.float32, 0.5, 1.5), 0.5, 1.5)
    w_mod = bell_draw(seeds[9], (2 * D, TS), TS ** -0.5, 0.375)
    t_index = jax.random.randint(seeds[10], (1,), 0, 1000).astype(jnp.int32)
    frame_order = jax.random.permutation(seeds[11], F).astype(jnp.int32)
    row_order = jax.random.permutation(seeds[12], H).astype(jnp.int32)
    col_order = jax.random.permutation(seeds[13], W).astype(jnp.int32)
    return dict(latent=latent, out_grad=out_grad, w_in=w_in, w_out=w_out, w_select=w_select, w_dt=w_dt, dt_bias=dt_bias, a_log=a_log, d_skip=d_skip, w_mod=w_mod, t_index=t_index, frame_order=frame_order, row_order=row_order, col_order=col_order)


def time_features(step_index, width):
    halfway = width // 2
    frequency = jnp.exp(-math.log(10000.0) * jnp.arange(halfway, dtype=jnp.float32) / halfway)
    angles = step_index.astype(jnp.float32)[0] * frequency
    return jnp.concatenate([jnp.cos(angles), jnp.sin(angles)])

def modulate(inputs, shift_vec, scale_vec):
    widened = inputs.astype(jnp.float32)
    inverse = lax.rsqrt(lax.optimization_barrier(jnp.mean(widened * widened, axis=-1, keepdims=True)) + 1e-06)
    normed = widened * inverse
    return (normed, inverse, (normed * (1.0 + scale_vec) + shift_vec).astype(jnp.bfloat16))

def ssm_scan(values, spacing, input_map, output_map, rates):

    def advance(state, column):
        value_t, space_t, in_t, out_t = column
        state = jnp.exp(space_t[:, None, :] * rates) * state + (space_t * value_t)[:, None, :] * in_t[:, :, None]
        return (state, lax.optimization_barrier(jnp.sum(state * out_t[:, :, None], axis=1)))
    start = jnp.zeros((values.shape[1], rates.shape[0], values.shape[2]), jnp.float32)
    _, result = lax.scan(jax.checkpoint(advance), start, (values, spacing, input_map, output_map), unroll=8)
    return result

def scan_backward(values, spacing, input_map, output_map, rates, cotangent, blocks):

    def one_block(pieces):
        value_b, space_b, rate_b, cot_b = pieces
        result, pullback = jax.vjp(ssm_scan, value_b, space_b, input_map, output_map, rate_b)
        return (result,) + tuple(pullback(cot_b))
    if blocks == 1:
        return one_block((values, spacing, rates, cotangent))

    def split(array):
        return jnp.moveaxis(array.reshape(array.shape[:-1] + (blocks, array.shape[-1] // blocks)), -2, 0)

    def join(array):
        moved = jnp.moveaxis(array, 0, -2)
        return moved.reshape(moved.shape[:-2] + (-1,))
    stacked = lax.map(one_block, (split(values), split(spacing), split(rates), split(cotangent)))
    return (join(stacked[0]), join(stacked[1]), join(stacked[2]), lax.optimization_barrier(jnp.sum(stacked[3], axis=0)), lax.optimization_barrier(jnp.sum(stacked[4], axis=0)), join(stacked[5]))

def direction_pass(activ, cotangent, params, scan_axis, visit_order, blocks):
    w_select, w_dt, dt_bias, a_log = params
    length = activ.shape[scan_axis]
    inner = activ.shape[-1]
    rank = w_dt.shape[1]
    states = a_log.shape[1]
    positions = jnp.arange(length, dtype=jnp.int32)
    inverse_order = lax.optimization_barrier(jnp.sum(positions[None, :] * (visit_order[None, :] == positions[:, None]).astype(jnp.int32), axis=1)).astype(jnp.int32)

    def arrange(array):
        return jnp.moveaxis(jnp.take(array, visit_order, axis=scan_axis), scan_axis, 0)

    def restore(array, shape):
        return jnp.take(jnp.moveaxis(array.reshape(shape), 0, scan_axis), inverse_order, axis=scan_axis)
    ordered = arrange(activ)
    shape = ordered.shape
    flat = ordered.reshape(-1, inner)
    select_out = jnp.dot(flat, w_select, preferred_element_type=jnp.float32)
    low_rank = select_out[:, :rank].astype(jnp.bfloat16)
    spacing_pre = lax.dot_general(low_rank, w_dt, (((1,), (1,)), ((), ())), preferred_element_type=jnp.float32) + dt_bias.astype(jnp.float32)
    spacing = jax.nn.softplus(spacing_pre)
    rates = -jnp.exp(a_log.astype(jnp.float32)).T
    seq_shape = (length, flat.shape[0] // length)
    values = flat.astype(jnp.float32).reshape(seq_shape + (inner,))
    spaced = spacing.reshape(seq_shape + (inner,))
    in_seq = select_out[:, rank:rank + states].reshape(seq_shape + (states,))
    out_seq = select_out[:, rank + states:].reshape(seq_shape + (states,))
    if cotangent is None:
        result = ssm_scan(values, spaced, in_seq, out_seq, rates)
        return (restore(result.astype(jnp.bfloat16), shape), None, None)
    cot_seq = arrange(cotangent).astype(jnp.float32).reshape(seq_shape + (inner,))
    result, grad_values, grad_spacing, grad_in, grad_out_map, grad_rates = scan_backward(values, spaced, in_seq, out_seq, rates, cot_seq, blocks)
    grad_pre = grad_spacing.reshape(-1, inner) * jax.nn.sigmoid(spacing_pre)
    grad_bias = lax.optimization_barrier(jnp.sum(grad_pre, axis=0))
    grad_pre_b = grad_pre.astype(jnp.bfloat16)
    grad_dt = lax.dot_general(grad_pre_b, low_rank, (((0,), (0,)), ((), ())), preferred_element_type=jnp.float32)
    grad_low = jnp.dot(grad_pre_b, w_dt, preferred_element_type=jnp.float32)
    grad_select_out = jnp.concatenate([grad_low, grad_in.reshape(-1, states), grad_out_map.reshape(-1, states)], axis=1).astype(jnp.bfloat16)
    grad_select = lax.dot_general(flat, grad_select_out, (((0,), (0,)), ((), ())), preferred_element_type=jnp.float32)
    grad_flat = grad_values.reshape(-1, inner) + lax.dot_general(grad_select_out, w_select, (((1,), (1,)), ((), ())), preferred_element_type=jnp.float32)
    grad_alog = (grad_rates * rates).T
    return (restore(result.astype(jnp.bfloat16), shape), restore(grad_flat.astype(jnp.bfloat16), shape), (grad_select, grad_dt, grad_bias, grad_alog))

def reference(latent, out_grad, w_in, w_out, w_select, w_dt, dt_bias, a_log, d_skip, w_mod, t_index, frame_order, row_order, col_order):
    frames, rows, cols, width = latent.shape
    inner = w_in.shape[1]
    features = jax.nn.silu(time_features(t_index, w_mod.shape[1])).astype(jnp.bfloat16)
    modulation = jnp.dot(w_mod, features, preferred_element_type=jnp.float32)
    scale_vec = modulation[width:]
    normed, inverse, shifted = modulate(latent, modulation[:width], scale_vec)
    shifted_flat = shifted.reshape(-1, width)
    pre_act = jnp.dot(shifted_flat, w_in, preferred_element_type=jnp.float32)
    activ_flat = jax.nn.silu(pre_act).astype(jnp.bfloat16)
    activ = activ_flat.reshape(frames, rows, cols, inner)
    grad_flat = out_grad.reshape(-1, width)
    cot_flat = lax.dot_general(grad_flat, w_out, (((1,), (1,)), ((), ())), preferred_element_type=jnp.float32).astype(jnp.bfloat16)
    cot = cot_flat.reshape(frames, rows, cols, inner)
    params = (w_select, w_dt, dt_bias, a_log)
    blocks = max(inner // 128, 1)
    mixed_time, back_time, grads_time = direction_pass(activ, cot, params, 0, frame_order, blocks)
    mixed_tall, back_tall, grads_tall = direction_pass(activ, cot, params, 1, row_order, blocks)
    mixed_wide, back_wide, grads_wide = direction_pass(activ, cot, params, 2, col_order, blocks)
    skip = d_skip.astype(jnp.float32)
    activ_wide = activ_flat.astype(jnp.float32)
    mixed_sum = (mixed_time.astype(jnp.float32) + mixed_tall.astype(jnp.float32) + mixed_wide.astype(jnp.float32)).reshape(-1, inner) + skip * activ_wide
    mixed_flat = mixed_sum.astype(jnp.bfloat16)
    branch_out = jnp.dot(mixed_flat, w_out, preferred_element_type=jnp.float32).astype(jnp.bfloat16).reshape(latent.shape)
    grad_w_out = lax.dot_general(mixed_flat, grad_flat, (((0,), (0,)), ((), ())), preferred_element_type=jnp.float32)
    cot_wide = cot_flat.astype(jnp.float32)
    grad_d_skip = lax.optimization_barrier(jnp.sum(cot_wide * activ_wide, axis=0))
    back_sum = (back_time.astype(jnp.float32) + back_tall.astype(jnp.float32) + back_wide.astype(jnp.float32)).reshape(-1, inner) + skip * cot_wide
    sigmoid_pre = jax.nn.sigmoid(pre_act)
    grad_act = (back_sum * sigmoid_pre * (1.0 + pre_act * (1.0 - sigmoid_pre))).astype(jnp.bfloat16)
    grad_w_in = lax.dot_general(shifted_flat, grad_act, (((0,), (0,)), ((), ())), preferred_element_type=jnp.float32)
    grad_shifted = lax.dot_general(grad_act, w_in, (((1,), (1,)), ((), ())), preferred_element_type=jnp.float32)
    normed_flat = normed.reshape(-1, width)
    inverse_flat = inverse.reshape(-1, 1)
    grad_normed = grad_shifted * (1.0 + scale_vec)
    latent_grad = (inverse_flat * (grad_normed - normed_flat * lax.optimization_barrier(jnp.mean(grad_normed * normed_flat, axis=1, keepdims=True)))).astype(jnp.bfloat16).reshape(latent.shape)
    grad_mod_vec = jnp.concatenate([lax.optimization_barrier(jnp.sum(grad_shifted, axis=0)), lax.optimization_barrier(jnp.sum(grad_shifted * normed_flat, axis=0))])
    grad_w_mod = grad_mod_vec[:, None] * features.astype(jnp.float32)[None, :]
    summed = jax.tree.map(lambda first, second, third: first + second + third, grads_time, grads_tall, grads_wide)
    return (branch_out, latent_grad, grad_w_in, grad_w_out, summed[0], summed[1], summed[2], summed[3], grad_d_skip, grad_w_mod)
```

```python
import functools
import math

import jax
import jax.numpy as jnp
from jax import lax
from jax.experimental import pallas as pl
from jax.experimental.pallas import tpu as pltpu
from jax.sharding import Mesh
from jax.sharding import PartitionSpec as P

BF = jnp.bfloat16
F32 = jnp.float32
LANES = 128
GROUP = 4
LOG2E = math.log2(math.e)
MEGA = 1024 * 1024
AXES = ("xl", "core", "xh", "y", "z")
ROW = ("xl", "core")
COL = ("xh", "y", "z")
NEAR = ("y", "z")
FAR = ("xl", "core", "xh")
NT = (((1,), (1,)), ((), ()))
TN = (((0,), (0,)), ((), ()))


def time_features(step_index, width):
    halfway = width // 2
    frequency = jnp.exp(-math.log(10000.0) * jnp.arange(halfway, dtype=jnp.float32) / halfway)
    angles = step_index.astype(jnp.float32)[0] * frequency
    return jnp.concatenate([jnp.cos(angles), jnp.sin(angles)])


def total(terms):
    return functools.reduce(lambda a, b: a + b, terms)


def call(kernel, name, out_shape, scratch, vmem, args, smem=()):
    spaces = [
        pl.BlockSpec(memory_space=pltpu.SMEM if i in smem else pltpu.VMEM) for i in range(len(args))
    ]
    return pl.pallas_call(
        kernel,
        out_shape=tuple(jax.ShapeDtypeStruct(s, d) for s, d in out_shape),
        in_specs=spaces,
        out_specs=(pl.BlockSpec(memory_space=pltpu.VMEM),) * len(out_shape),
        scratch_shapes=[pltpu.VMEM(s, d) for s, d in scratch],
        compiler_params=pltpu.CompilerParams(vmem_limit_bytes=vmem * MEGA),
        name=name,
    )(*args)


def cut(j):
    return slice(LANES * j, LANES * j + LANES)


def to_flat(ref, j, value, tiles):
    ref[pl.ds(j, value.shape[0], stride=tiles), :] = value


def from_flat(ref, j, tokens, tiles):
    return ref[pl.ds(j, tokens, stride=tiles), :]


def normalise(latent):
    wide = latent.astype(F32)
    inverse = lax.rsqrt(jnp.mean(wide * wide, axis=-1, keepdims=True) + 1e-06)
    return wide * inverse, inverse


def pre_kernel(
    latent_ref,
    grad_ref,
    w_in_ref,
    w_out_ref,
    w_mod_ref,
    feature_ref,
    own_ref,
    tall_ref,
    wide_ref,
    shifted_ref,
    pre_ref,
    mod_ref,
    flat_ref,
):
    tokens, width = latent_ref.shape
    tiles = w_in_ref.shape[1] // LANES
    modulation = lax.dot_general(
        feature_ref[...], w_mod_ref[...], NT, preferred_element_type=F32
    )
    mod_ref[...] = modulation
    normed, _ = normalise(latent_ref[...])
    shifted = (normed * (1.0 + modulation[:1, width:]) + modulation[:1, :width]).astype(BF)
    shifted_ref[...] = shifted
    pre_act = jnp.dot(shifted, w_in_ref[...], preferred_element_type=F32)
    pre_ref[...] = pre_act
    activ = (pre_act * jax.nn.sigmoid(pre_act)).astype(BF)
    cot = lax.dot_general(grad_ref[...], w_out_ref[...], NT, preferred_element_type=F32).astype(BF)
    for which, value in enumerate((activ, cot)):
        wide = value.astype(F32)
        for j in range(tiles):
            to_flat(flat_ref, j, wide[:, cut(j)], tiles)
        flat = flat_ref[...].astype(BF)
        for ref in (own_ref, tall_ref, wide_ref):
            parts = ref.shape[0]
            ref[:, which] = flat.reshape(parts, flat.shape[0] // parts, LANES)


def scan_kernel(
    length,
    row_of,
    order_ref,
    data_ref,
    wsel_ref,
    wdt_ref,
    bias_ref,
    alog_ref,
    sel_in_ref,
    dt_in_ref,
    vec_in_ref,
    out_ref,
    gsel_ref,
    gdt_ref,
    gvec_ref,
    pre_ref,
    dt_ref,
    xf_ref,
    x_row_ref,
    dt_row_ref,
    dx_row_ref,
    dy_row_ref,
    bb_ref,
    cb_ref,
    gb_ref,
    gc_ref,
    hist_ref,
    y8_ref,
    u8_ref,
    v8_ref,
    rate2_ref,
    rate_ref,
):
    tokens, inner = xf_ref.shape
    tiles = inner // LANES
    lines = tokens // length
    states = alog_ref.shape[0]
    rank = LANES - 2 * states
    flat_shape = (tokens * tiles, LANES)
    x_row_ref[...] = data_ref[:, 0].reshape(flat_shape).astype(F32)
    dy_row_ref[...] = data_ref[:, 1].reshape(flat_shape).astype(F32)
    for j in range(tiles):
        xf_ref[:, cut(j)] = from_flat(x_row_ref, j, tokens, tiles)
    x = xf_ref[...].astype(BF)
    select = jnp.dot(x, wsel_ref[...], preferred_element_type=F32)
    lane = lax.broadcasted_iota(jnp.int32, (tokens, LANES), 1)
    low = jnp.where(lane < rank, select, 0.0).astype(BF)
    pre = lax.dot_general(low, wdt_ref[...], NT, preferred_element_type=F32) + bias_ref[...]
    pre_ref[...] = pre
    spacing = jnp.maximum(pre, 0.0) + jnp.log1p(jnp.exp(-jnp.abs(pre)))
    dt_ref[...] = spacing
    for j in range(tiles):
        to_flat(dt_row_ref, j, spacing[:, cut(j)], tiles)
    dx_row_ref[...] = dt_row_ref[...] * x_row_ref[...]
    rates = -jnp.exp(alog_ref[...])
    rate_ref[...] = rates
    rate2_ref[...] = rates * LOG2E
    turned = select.T
    for token in range(tokens):
        at = pl.ds(token * states, states)
        column = slice(token, token + 1)
        bb_ref[at, :] = jnp.broadcast_to(turned[rank : rank + states, column], (states, LANES))
        cb_ref[at, :] = jnp.broadcast_to(turned[rank + states :, column], (states, LANES))
    gb_ref[...] = jnp.zeros_like(gb_ref)
    gc_ref[...] = jnp.zeros_like(gc_ref)
    zero = jnp.zeros((states, LANES), F32)
    hist_ref[pl.ds(0, states), :] = jnp.zeros((states, GROUP * LANES), F32)
    unroll = min(length, 8)

    def fold(value):
        return value[:8] + value[8:]

    for group in range(tiles // GROUP):
        first = group * GROUP
        cuts = [cut(first + j) for j in range(GROUP)]
        rate2 = [rate2_ref[:, c] for c in cuts]
        rate1 = [rate_ref[:, c] for c in cuts]

        def one_line(line, grads):
            def places(step):
                row = row_of(order_ref[step], line)
                at = pl.ds(pl.multiple_of(row * states, states), states)
                slot = pl.ds(pl.multiple_of((step + 1) * states, states), states)
                return row * tiles + first, pl.multiple_of(row * 8, 8), at, slot

            def forward(step, carry):
                row, eight, at, slot = places(step)
                bb, cb = bb_ref[at, :], cb_ref[at, :]
                new = []
                for j in range(GROUP):
                    dt = dt_row_ref[pl.ds(row + j, 1), :]
                    dx = dx_row_ref[pl.ds(row + j, 1), :]
                    h = jnp.exp2(rate2[j] * dt) * carry[j] + bb * dx
                    hist_ref[slot, cut(j)] = h
                    y8_ref[pl.ds(eight + 8 * tokens * j, 8), :] = fold(h * cb)
                    new.append(h)
                return tuple(new)

            lax.fori_loop(0, length, forward, (zero,) * GROUP, unroll=unroll)

            def backward(back_step, carry):
                step = length - 1 - back_step
                row, eight, at, slot = places(step)
                prev = pl.ds(pl.multiple_of(step * states, states), states)
                bb, cb = bb_ref[at, :], cb_ref[at, :]
                pend, acc = carry
                gb = gb_ref[at, :]
                gc = gc_ref[at, :]
                new, acc_new = [], []
                for j in range(GROUP):
                    dt = dt_row_ref[pl.ds(row + j, 1), :]
                    dx = dx_row_ref[pl.ds(row + j, 1), :]
                    dy = dy_row_ref[pl.ds(row + j, 1), :]
                    g = pend[j] + cb * dy
                    gc = gc + hist_ref[slot, cut(j)] * dy
                    u8_ref[pl.ds(eight + 8 * tokens * j, 8), :] = fold(g * bb)
                    gb = gb + g * dx
                    p = jnp.exp2(rate2[j] * dt) * g
                    w = p * hist_ref[prev, cut(j)]
                    v8_ref[pl.ds(eight + 8 * tokens * j, 8), :] = fold(w * rate1[j])
                    acc_new.append(acc[j] + w * dt)
                    new.append(p)
                gb_ref[at, :] = gb
                gc_ref[at, :] = gc
                return tuple(new), tuple(acc_new)

            start = ((zero,) * GROUP, grads)
            return lax.fori_loop(0, length, backward, start, unroll=unroll)[1]

        grads = lax.fori_loop(0, lines, one_line, (zero,) * GROUP)
        for j in range(GROUP):
            gvec_ref[:states, cuts[j]] = vec_in_ref[:states, cuts[j]] + grads[j] * rate1[j]

        def gather(block, carry):
            rows = pl.ds(pl.multiple_of(block * 8, 8), 8)

            def summed(ref, j):
                begin = block * 64 + 8 * tokens * j
                return total([ref[pl.ds(begin + r, 8, stride=8), :] for r in range(8)])

            for j in range(GROUP):
                c = cuts[j]
                u = summed(u8_ref, j)
                x_row_ref[pl.ds(block * 8 * tiles + first + j, 8, stride=tiles), :] = summed(y8_ref, j)
                grad_spacing = summed(v8_ref, j) + xf_ref[rows, c] * u
                pre_ref[rows, c] = grad_spacing * jax.nn.sigmoid(pre_ref[rows, c])
                dt_ref[rows, c] = dt_ref[rows, c] * u
            return carry

        lax.fori_loop(0, tokens // 8, gather, 0, unroll=2)

    out_shape = (out_ref.shape[0], out_ref.shape[2], LANES)
    out_ref[:, 0] = x_row_ref[...].astype(BF).reshape(out_shape)
    grad_pre = pre_ref[...]
    gvec_ref[states:, :] = vec_in_ref[states:, :]
    gvec_ref[states : states + 1, :] += jnp.sum(grad_pre, axis=0, keepdims=True)
    grad_pre_b = grad_pre.astype(BF)
    ones = jnp.ones((LANES, LANES), BF)

    def lane_total(ref):
        value = ref[...]
        top = value.astype(BF)
        rest = (value - top.astype(F32)).astype(BF)
        return jnp.dot(top, ones, preferred_element_type=F32) + jnp.dot(
            rest, ones, preferred_element_type=F32
        )

    shape = (tokens * states, LANES)
    state_at = lax.broadcasted_iota(jnp.int32, shape, 0) % states
    lane_at = lax.broadcasted_iota(jnp.int32, shape, 1)
    gb_ref[...] = jnp.where(lane_at == state_at + rank, lane_total(gb_ref), 0.0) + jnp.where(
        lane_at == state_at + rank + states, lane_total(gc_ref), 0.0
    )
    grad_maps = total([gb_ref[pl.ds(n, tokens, stride=states), :] for n in range(states)])
    grad_low = jnp.dot(grad_pre_b, wdt_ref[...], preferred_element_type=F32)
    grad_select_out = (grad_low + grad_maps).astype(BF)
    back = dt_ref[...] + lax.dot_general(
        grad_select_out, wsel_ref[...], NT, preferred_element_type=F32
    )
    for j in range(tiles):
        to_flat(x_row_ref, j, back[:, cut(j)], tiles)
    out_ref[:, 1] = x_row_ref[...].astype(BF).reshape(out_shape)
    gsel_ref[...] = sel_in_ref[...] + lax.dot_general(
        x, grad_select_out, TN, preferred_element_type=F32
    )
    gdt_ref[...] = dt_in_ref[...] + lax.dot_general(
        grad_pre_b, low, TN, preferred_element_type=F32
    )


def direction(name, length, row_of, order, data, params, grads):
    inner = params[0].shape[0]
    tiles = inner // LANES
    tokens = data.shape[0] * data.shape[2] // tiles
    states = params[3].shape[0]
    plane = ((tokens, inner), F32)
    flat = ((tokens * tiles, LANES), F32)
    maps = ((tokens * states, LANES), F32)
    eights = ((tokens * 8 * GROUP, LANES), F32)
    out, *grads = call(
        functools.partial(scan_kernel, length, row_of),
        name,
        [(data.shape, BF)] + [(g.shape, F32) for g in grads],
        [plane] * 3
        + [flat] * 4
        + [maps] * 4
        + [(((length + 1) * states, GROUP * LANES), F32)]
        + [eights] * 3
        + [((states, inner), F32)] * 2,
        40,
        (order, data, *params, *grads),
        smem=(0,),
    )
    return out, grads


def post_kernel(
    own_ref,
    time_ref,
    tall_ref,
    wide_ref,
    pre_ref,
    latent_ref,
    mod_ref,
    skip_ref,
    w_in_ref,
    w_out_ref,
    gsel_ref,
    gdt_ref,
    gvec_ref,
    branch_ref,
    latent_grad_ref,
    send_ref,
    sum_ref,
    own_row_ref,
    mixed_ref,
    back_ref,
    turned_ref,
    first_ref,
    second_ref,
):
    tokens, width = latent_ref.shape
    inner = w_in_ref.shape[1]
    tiles = inner // LANES
    flat_shape = (tokens * tiles, LANES)
    near, _, near_rows, _ = send_ref.shape
    far = inner // (near * 12)
    states = gvec_ref.shape[0] - 8
    rank = LANES - 2 * states
    grad_skip = []
    for which, target in ((0, mixed_ref), (1, back_ref)):
        sum_ref[...] = total(
            [ref[:, which].reshape(flat_shape).astype(F32) for ref in (time_ref, tall_ref, wide_ref)]
        )
        own_row_ref[which] = own_ref[0, which].astype(F32)
        for j in range(tiles):
            mine = own_row_ref[which, pl.ds(j, tokens, stride=tiles), :]
            target[:, cut(j)] = from_flat(sum_ref, j, tokens, tiles) + skip_ref[:, cut(j)] * mine
            if which:
                other = own_row_ref[0, pl.ds(j, tokens, stride=tiles), :]
                grad_skip.append(jnp.sum(mine * other, axis=0, keepdims=True))
    mixed = mixed_ref[...].astype(BF)
    branch_ref[...] = jnp.dot(mixed, w_out_ref[...], preferred_element_type=F32).astype(BF)
    pre_act = pre_ref[...]
    gate = jax.nn.sigmoid(pre_act)
    grad_act = (back_ref[...] * gate * (1.0 + pre_act * (1.0 - gate))).astype(BF)
    grad_shifted = lax.dot_general(grad_act, w_in_ref[...], NT, preferred_element_type=F32)
    normed, inverse = normalise(latent_ref[...])
    grad_normed = grad_shifted * (1.0 + mod_ref[:1, width:])
    product = jnp.mean(grad_normed * normed, axis=1, keepdims=True)
    latent_grad_ref[...] = (inverse * (grad_normed - normed * product)).astype(BF)
    grad_vec = jnp.concatenate(
        [
            jnp.sum(grad_shifted, axis=0, keepdims=True),
            jnp.sum(grad_shifted * normed, axis=0, keepdims=True),
        ],
        axis=1,
    )
    turned_ref[0] = mixed.astype(F32).T
    turned_ref[1] = grad_act.astype(F32).T
    turned_ref[2] = gsel_ref[...]
    row_at = lax.broadcasted_iota(jnp.int32, (LANES, 2 * width), 0)
    spread = jnp.broadcast_to(grad_vec, (LANES, 2 * width))
    first_ref[...] = jnp.where(row_at == LANES - 14, spread, 0.0).T
    second_ref[...] = jnp.where(row_at == LANES - 13, spread, 0.0).T
    at = lax.broadcasted_iota(jnp.int32, (LANES, inner), 0)
    skips = jnp.concatenate(grad_skip, axis=1)
    vectors = jnp.concatenate(
        [
            jnp.zeros((rank, inner), F32),
            gvec_ref[...],
            jnp.zeros((states - 8, inner), F32),
        ],
        axis=0,
    )
    vectors = vectors + jnp.where(at == rank + states + 1, jnp.broadcast_to(skips, at.shape), 0.0)
    turned_ref[3] = gdt_ref[...] + vectors.T
    for m in range(near):
        send_ref[m, 1] = turned_ref[1, pl.ds(m * near_rows, near_rows), :].astype(BF)
        for which in (0, 2, 3):
            pieces = []
            for i in range(12):
                piece = turned_ref[which, pl.ds(m * 12 + i, far, stride=near * 12), :]
                if which == 3:
                    begin = m * 24 + i
                    piece = (
                        piece
                        + first_ref[pl.ds(begin, far, stride=near * 24), :]
                        + second_ref[pl.ds(begin + 12, far, stride=near * 24), :]
                    )
                pieces.append(piece)
            send_ref[m, which] = jnp.concatenate(pieces, axis=0).astype(BF)


def middle_kernel(recv_ref, grad_ref, shifted_ref, send_ref, left_ref, out_ref, half_ref):
    near, _, rows, tokens = recv_ref.shape
    far = send_ref.shape[0]
    width = grad_ref.shape[1]
    tiles = width // LANES
    chunk = width // far
    own = rows // far
    for s in range(near):
        left_ref[:, cut(s)] = recv_ref[s, 0]
    product = jnp.dot(left_ref[...], grad_ref[...], preferred_element_type=F32)
    for j in range(tiles):
        half_ref[...] = product[:, cut(j)]
        for o in range(far):
            out_ref[o, pl.ds(j, own, stride=tiles), :] = half_ref[pl.ds(o, own, stride=far), :]
    base = own * tiles
    for which in (2, 3):
        half_ref[...] = total([recv_ref[s, which].astype(F32) for s in range(near)])
        for o in range(far):
            out_ref[o, pl.ds(base, own), :] = half_ref[pl.ds(o, own, stride=far), :]
        base += own
    for s in range(near):
        left_ref[:, cut(s)] = recv_ref[s, 1]
    product = jnp.dot(left_ref[...], shifted_ref[...], preferred_element_type=F32)
    turned = jnp.concatenate([product, jnp.zeros((LANES - rows, width), F32)], axis=0).T
    for o in range(far):
        out_ref[o, pl.ds(base, chunk), :] = turned[o * chunk : (o + 1) * chunk]
    base += chunk
    rest = out_ref.shape[1] - base
    for o in range(far):
        out_ref[o, pl.ds(base, rest), :] = jnp.zeros((rest, LANES), F32)
    send_ref[...] = out_ref[...].astype(BF)


def last_kernel(recv_ref, feature_ref, gwo_ref, gsel_ref, small_ref, gmod_ref, send_ref, sum_ref):
    far = recv_ref.shape[0]
    near = send_ref.shape[0]
    own, width = gwo_ref.shape
    tiles = width // LANES
    sum_ref[...] = total([recv_ref[o].astype(F32) for o in range(far)])
    for j in range(tiles):
        gwo_ref[:, cut(j)] = sum_ref[pl.ds(j, own, stride=tiles), :]
    base = own * tiles
    gsel_ref[...] = sum_ref[pl.ds(base, own), :]
    small = sum_ref[pl.ds(base + own, own), :]
    small_ref[...] = small
    features = feature_ref[:1, :].astype(F32)
    gmod_ref[:own, :] = small[:, LANES - 14 : LANES - 13] * features
    gmod_ref[own:, :] = small[:, LANES - 13 : LANES - 12] * features
    base += 2 * own
    for m in range(near):
        send_ref[m, :own] = sum_ref[pl.ds(base + m * own, own), :]
        send_ref[m, own:] = jnp.zeros((send_ref.shape[1] - own, LANES), F32)


def join_kernel(recv_ref, gwi_ref):
    near = recv_ref.shape[0]
    own, width = gwi_ref.shape
    part = width // near
    for m in range(near):
        gwi_ref[:, part * m : part * (m + 1)] = recv_ref[m, :own, :part]


def exchange(value, axes):
    return lax.all_to_all(value, axes, split_axis=0, concat_axis=0, tiled=True)


def local(
    latent,
    out_grad,
    w_in,
    w_out,
    w_select,
    w_dt,
    dt_bias,
    a_log,
    d_skip,
    w_mod,
    t_index,
    frame_order,
    row_order,
    col_order,
):
    frames, rows, cols, width = latent.shape
    inner = w_in.shape[1]
    tokens = frames * rows * cols
    tiles = inner // LANES
    states = a_log.shape[1]
    n_row, n_col = lax.axis_size(ROW), lax.axis_size(COL)
    near, far = lax.axis_size(NEAR), lax.axis_size(FAR)
    own = width // (near * far)
    flat_latent = latent.reshape(tokens, width)
    flat_grad = out_grad.reshape(tokens, width)
    features = jax.nn.silu(time_features(t_index, w_mod.shape[1])).astype(BF)
    feature_rows = jnp.broadcast_to(features[None, :], (8, features.shape[0]))

    def packed(parts):
        return ((parts, 2, tokens * tiles // parts, LANES), BF)

    grad_near = lax.all_gather(flat_grad, NEAR, axis=0, tiled=True)
    data_own, data_tall, data_wide, shifted, pre_act, modulation = call(
        pre_kernel,
        "norm_project",
        [
            packed(1),
            packed(n_row),
            packed(n_col),
            ((tokens, width), BF),
            ((tokens, inner), F32),
            ((8, 2 * width), F32),
        ],
        [((tokens * tiles, LANES), F32)],
        48,
        (flat_latent, flat_grad, w_in, w_out, w_mod, feature_rows),
    )
    data_wide = exchange(data_wide, COL)
    data_tall = exchange(data_tall, ROW)
    shifted_near = lax.all_gather(shifted, NEAR, axis=0, tiled=True)
    params = (
        w_select,
        jnp.pad(w_dt, ((0, 0), (0, LANES - w_dt.shape[1]))),
        dt_bias[None, :],
        a_log.T,
    )
    grads = [
        jnp.zeros((inner, LANES), F32),
        jnp.zeros((inner, LANES), F32),
        jnp.zeros((states + 8, inner), F32),
    ]
    area = rows * cols

    def time_row(at, line):
        return at * area + line

    def wide_row(at, line):
        chunk = frames // n_col * area
        return (
            lax.div(at, cols) * chunk
            + lax.rem(at, cols)
            + lax.div(line, rows) * area
            + lax.rem(line, rows) * cols
        )

    def tall_row(at, line):
        chunk = frames // n_row * area
        return (
            lax.div(at, rows) * chunk
            + lax.rem(at, rows) * cols
            + lax.div(line, cols) * area
            + lax.rem(line, cols)
        )

    out_time, grads = direction(
        "scan_time", frames, time_row, frame_order, data_own, params, grads
    )
    out_wide, grads = direction(
        "scan_width", cols * n_col, wide_row, col_order, data_wide, params, grads
    )
    out_wide = exchange(out_wide, COL)
    out_tall, grads = direction(
        "scan_height", rows * n_row, tall_row, row_order, data_tall, params, grads
    )
    out_tall = exchange(out_tall, ROW)
    branch, latent_grad, near_send = call(
        post_kernel,
        "sum_project",
        [
            ((tokens, width), BF),
            ((tokens, width), BF),
            ((near, 4, inner // near, LANES), BF),
        ],
        [
            ((tokens * tiles, LANES), F32),
            ((2, tokens * tiles, LANES), F32),
            ((tokens, inner), F32),
            ((tokens, inner), F32),
            ((4, inner, LANES), F32),
            ((2 * width, LANES), F32),
            ((2 * width, LANES), F32),
        ],
        48,
        (
            data_own,
            out_time,
            out_tall,
            out_wide,
            pre_act,
            flat_latent,
            modulation,
            d_skip[None, :],
            w_in,
            w_out,
            *grads,
        ),
    )
    near_recv = exchange(near_send, NEAR)
    piece = own * tiles + 2 * own + width // far
    piece = -(-piece // 16) * 16
    far_send = call(
        middle_kernel,
        "weight_grads",
        [((far, piece, LANES), BF)],
        [
            ((inner // near, near * tokens), BF),
            ((far, piece, LANES), F32),
            ((inner // near, LANES), F32),
        ],
        48,
        (near_recv, grad_near, shifted_near),
    )[0]
    far_recv = exchange(far_send, FAR)
    grad_w_out, grad_select, small, grad_mod, last_send = call(
        last_kernel,
        "weight_sums",
        [
            ((own, width), F32),
            ((own, LANES), F32),
            ((own, LANES), F32),
            ((2 * own, features.shape[0]), F32),
            ((near, 16, LANES), F32),
        ],
        [((piece, LANES), F32)],
        16,
        (far_recv, feature_rows),
    )
    last_recv = exchange(last_send, NEAR)
    grad_w_in = call(join_kernel, "weight_rows", [((own, width), F32)], [], 16, (last_recv,))[0]
    rank = w_dt.shape[1]
    return (
        branch.reshape(latent.shape),
        latent_grad.reshape(latent.shape),
        grad_w_in,
        grad_w_out,
        grad_select,
        small[:, :rank],
        small[:, rank + states],
        small[:, rank : rank + states],
        small[:, rank + states + 1],
        grad_mod,
    )


def solution(mesh):
    n_row, n_col = mesh.shape["row"], mesh.shape["col"]
    split = Mesh(mesh.devices.reshape(n_row // 2, 2, 2, 4, n_col // 8), AXES)
    tokens = P(None, ROW, COL, None)
    matrix = P(ROW + COL, None)
    vector = P(ROW + COL)
    return jax.shard_map(
        local,
        mesh=split,
        in_specs=(tokens, tokens) + (P(),) * 12,
        out_specs=(
            tokens,
            tokens,
            matrix,
            matrix,
            matrix,
            matrix,
            vector,
            matrix,
            vector,
            matrix,
        ),
        check_vma=False,
    )
```

```python
import functools
import math

import jax
import jax.numpy as jnp
from jax import lax
from jax.experimental import pallas as pl
from jax.experimental.pallas import tpu as pltpu
from jax.sharding import Mesh
from jax.sharding import PartitionSpec as P

BF = jnp.bfloat16
F32 = jnp.float32
LANES = 128
GROUP = 4
LOG2E = math.log2(math.e)
MEGA = 1024 * 1024
VMEM_ALL = 63
PIECES = 4
SLOT = 16
AXES = ("xl", "core", "xh", "y", "z")
ROW = ("xl", "core")
COL = ("xh", "y", "z")
NEAR = ("y", "z")
FAR = ("xl", "core", "xh")
FAR_SIZE = 8
NT = (((1,), (1,)), ((), ()))
TN = (((0,), (0,)), ((), ()))


def time_features(step_index, width):
    halfway = width // 2
    frequency = jnp.exp(-math.log(10000.0) * jnp.arange(halfway, dtype=jnp.float32) / halfway)
    angles = step_index.astype(jnp.float32)[0] * frequency
    return jnp.concatenate([jnp.cos(angles), jnp.sin(angles)])


def total(terms):
    return functools.reduce(lambda a, b: a + b, terms)


def call(kernel, name, out_shape, scratch, vmem, flops, args, smem=(), late=(), pieces=None, choose=None):
    moved = [i for i in range(len(args)) if i not in smem]
    pieces, choose = pieces or {}, choose or {}
    held_shape = {
        i: args[i].shape[:1] + args[i].shape[2:] if i in choose else args[i].shape for i in moved
    }
    cuts = []
    for i in moved:
        size = args[i].shape[0] // pieces.get(i, 1)
        cuts += [(i, n, pl.ds(n * size, size)) for n in range(pieces.get(i, 1))]

    def body(*refs):
        given, out = refs[: len(args)], refs[len(args) : len(args) + len(out_shape)]
        rest = refs[len(args) + len(out_shape) :]
        held, rest = rest[: len(moved)], rest[len(moved) :]
        made, rest = rest[: len(out_shape)], rest[len(out_shape) :]
        in_sem, out_sem = rest[-2:]
        views = [given[i] if i in smem else held[moved.index(i)] for i in range(len(args))]
        copies = {
            (i, n): pltpu.make_async_copy(
                given[i].at[at, choose[i]] if i in choose else given[i].at[at],
                views[i].at[at],
                in_sem.at[place],
            )
            for place, (i, n, at) in enumerate(cuts)
        }
        for copy in copies.values():
            copy.start()
        for (i, _), copy in copies.items():
            if i not in late:
                copy.wait()
        waits = (lambda i, n=0: copies[i, n].wait(),) if late else ()
        kernel(*waits, *views, *made, *rest[:-2])
        sent = [
            pltpu.make_async_copy(made[n], out[n], out_sem.at[n]) for n in range(len(out_shape))
        ]
        for copy in sent:
            copy.start()
        for copy in sent:
            copy.wait()

    spaces = [
        pl.BlockSpec(memory_space=pltpu.SMEM if i in smem else pltpu.HBM) for i in range(len(args))
    ]
    return pl.pallas_call(
        body,
        out_shape=tuple(jax.ShapeDtypeStruct(s, d) for s, d in out_shape),
        in_specs=spaces,
        out_specs=(pl.BlockSpec(memory_space=pltpu.HBM),) * len(out_shape),
        scratch_shapes=[pltpu.VMEM(held_shape[i], args[i].dtype) for i in moved]
        + [pltpu.VMEM(s, d) for s, d in out_shape]
        + [pltpu.VMEM(s, d) for s, d in scratch]
        + [pltpu.SemaphoreType.DMA((len(cuts),)), pltpu.SemaphoreType.DMA((len(out_shape),))],
        compiler_params=pltpu.CompilerParams(vmem_limit_bytes=vmem * MEGA),
        cost_estimate=cost(flops, args),
        name=name,
    )(*args)


def cost(flops, args):
    return pl.CostEstimate(
        flops=int(flops),
        bytes_accessed=sum(a.size * a.dtype.itemsize for a in args),
        transcendentals=0,
    )


def plain_call(kernel, name, out_shape, scratch, vmem, flops, args, smem=()):
    spaces = [
        pl.BlockSpec(memory_space=pltpu.SMEM if i in smem else pltpu.VMEM) for i in range(len(args))
    ]
    return pl.pallas_call(
        kernel,
        out_shape=tuple(jax.ShapeDtypeStruct(s, d) for s, d in out_shape),
        in_specs=spaces,
        out_specs=(pl.BlockSpec(memory_space=pltpu.VMEM),) * len(out_shape),
        scratch_shapes=[pltpu.VMEM(s, d) for s, d in scratch],
        compiler_params=pltpu.CompilerParams(vmem_limit_bytes=vmem * MEGA),
        cost_estimate=cost(flops, args),
        name=name,
    )(*args)


def cut(j):
    return slice(LANES * j, LANES * j + LANES)


def to_flat(ref, j, value, tiles):
    ref[pl.ds(j, value.shape[0], stride=tiles), :] = value


def from_flat(ref, j, tokens, tiles):
    return ref[pl.ds(j, tokens, stride=tiles), :]


def normalise(latent):
    wide = latent.astype(F32)
    inverse = lax.rsqrt(jnp.mean(wide * wide, axis=-1, keepdims=True) + 1e-06)
    return wide * inverse, inverse


def pre_kernel(
    wait,
    latent_ref,
    grad_ref,
    w_in_ref,
    w_out_ref,
    w_mod_ref,
    feature_ref,
    place_ref,
    own_ref,
    wide_ref,
    slot_0_ref,
    slot_1_ref,
    slot_2_ref,
    slot_3_ref,
    both_ref,
    pre_ref,
    mod_ref,
    flat_ref,
):
    tokens, width = latent_ref.shape
    tiles = w_in_ref.shape[1] // LANES
    modulation = lax.dot_general(
        feature_ref[...], w_mod_ref[...], NT, preferred_element_type=F32
    )
    mod_ref[...] = modulation
    normed, _ = normalise(latent_ref[...])
    shifted = (normed * (1.0 + modulation[:1, width:]) + modulation[:1, :width]).astype(BF)
    both_ref[0] = shifted
    both_ref[1] = grad_ref[...]
    wait(2)
    pre_act = jnp.dot(shifted, w_in_ref[...], preferred_element_type=F32)
    pre_ref[...] = pre_act
    activ = (pre_act * jax.nn.sigmoid(pre_act)).astype(BF)
    wait(3)
    cot = lax.dot_general(grad_ref[...], w_out_ref[...], NT, preferred_element_type=F32).astype(BF)
    for which, value in enumerate((activ, cot)):
        wide = value.astype(F32)
        for j in range(tiles):
            to_flat(flat_ref, j, wide[:, cut(j)], tiles)
        flat = flat_ref[...].astype(BF)
        own_ref[0, which] = flat
        wide_ref[:, which] = flat.reshape(wide_ref.shape[0], wide_ref.shape[2], LANES)
        for k, ref in enumerate((slot_0_ref, slot_1_ref, slot_2_ref, slot_3_ref)):
            chunk = ref.shape[2]
            begin = pl.multiple_of((place_ref[0] ^ k) * chunk, chunk)
            ref[0, which] = flat_ref[pl.ds(begin, chunk), :].astype(BF)


def parts_of(refs):
    begin, found = 0, []
    for ref in refs:
        size = ref.shape[0] * ref.shape[2]
        found.append((ref, slice(begin, begin + size)))
        begin += size
    return found


def read_part(ref, which):
    return ref[:, which].reshape(ref.shape[0] * ref.shape[2], LANES).astype(F32)


def write_part(ref, which, value):
    ref[:, which] = value.astype(BF).reshape(ref.shape[0], ref.shape[2], LANES)


def scan_kernel(
    length,
    row_of,
    pieces,
    order_ref,
    place_ref,
    *refs,
):
    data_refs, out_refs = refs[:pieces], refs[pieces + 4 : 2 * pieces + 4]
    scan_steps(
        length,
        row_of,
        order_ref,
        place_ref,
        data_refs,
        *refs[pieces : pieces + 4],
        out_refs,
        *refs[2 * pieces + 4 :],
    )


def scan_steps(
    length,
    row_of,
    order_ref,
    place_ref,
    data_refs,
    wsel_ref,
    wdt_ref,
    bias_ref,
    alog_ref,
    out_refs,
    x_ref,
    grad_pre_ref,
    low_ref,
    grad_low_ref,
    gvec_ref,
    pre_ref,
    dt_ref,
    xf_ref,
    x_row_ref,
    dt_row_ref,
    dx_row_ref,
    dy_row_ref,
    bb_ref,
    cb_ref,
    gb_ref,
    gc_ref,
    hist_ref,
    y8_ref,
    u8_ref,
    v8_ref,
    rate2_ref,
    rate_ref,
):
    tokens, inner = xf_ref.shape
    tiles = inner // LANES
    lines = tokens // length
    states = alog_ref.shape[0]
    rank = LANES - 2 * states
    for ref, at in parts_of(data_refs):
        x_row_ref[at, :] = read_part(ref, 0)
        dy_row_ref[at, :] = read_part(ref, 1)
    for j in range(tiles):
        xf_ref[:, cut(j)] = from_flat(x_row_ref, j, tokens, tiles)
    x = xf_ref[...].astype(BF)
    x_ref[...] = x
    select = jnp.dot(x, wsel_ref[...], preferred_element_type=F32)
    lane = lax.broadcasted_iota(jnp.int32, (tokens, LANES), 1)
    low = jnp.where(lane < rank, select, 0.0).astype(BF)
    low_ref[...] = low
    w_dt = jnp.concatenate([wdt_ref[...], jnp.zeros((2 * states, inner), BF)], axis=0)
    pre = jnp.dot(low, w_dt, preferred_element_type=F32) + bias_ref[...]
    pre_ref[...] = pre
    spacing = jnp.maximum(pre, 0.0) + jnp.log1p(jnp.exp(-jnp.abs(pre)))
    dt_ref[...] = spacing
    for j in range(tiles):
        to_flat(dt_row_ref, j, spacing[:, cut(j)], tiles)
    dx_row_ref[...] = dt_row_ref[...] * x_row_ref[...]
    rates = -jnp.exp(alog_ref[...])
    rate_ref[...] = rates
    rate2_ref[...] = rates * LOG2E
    turned = select.T
    for token in range(tokens):
        at = pl.ds(token * states, states)
        column = slice(token, token + 1)
        bb_ref[at, :] = jnp.broadcast_to(turned[rank : rank + states, column], (states, LANES))
        cb_ref[at, :] = jnp.broadcast_to(turned[rank + states :, column], (states, LANES))
    gb_ref[...] = jnp.zeros_like(gb_ref)
    gc_ref[...] = jnp.zeros_like(gc_ref)
    zero = jnp.zeros((states, LANES), F32)
    hist_ref[pl.ds(0, states), :] = jnp.zeros((states, GROUP * LANES), F32)
    unroll = min(length, 8)

    def fold(value):
        return value[:8] + value[8:]

    for group in range(tiles // GROUP):
        first = group * GROUP
        cuts = [cut(first + j) for j in range(GROUP)]
        rate2 = [rate2_ref[:, c] for c in cuts]
        rate1 = [rate_ref[:, c] for c in cuts]

        def one_line(line, grads):
            def places(step):
                row = row_of(order_ref[step], line, place_ref[0])
                at = pl.ds(pl.multiple_of(row * states, states), states)
                slot = pl.ds(pl.multiple_of((step + 1) * states, states), states)
                return row * tiles + first, pl.multiple_of(row * 8, 8), at, slot

            def forward(step, carry):
                row, at_8, at, slot = places(step)
                bb, cb = bb_ref[at, :], cb_ref[at, :]
                new = []
                for j in range(GROUP):
                    dt = dt_row_ref[pl.ds(row + j, 1), :]
                    dx = dx_row_ref[pl.ds(row + j, 1), :]
                    h = jnp.exp2(rate2[j] * dt) * carry[j] + bb * dx
                    hist_ref[slot, cut(j)] = h
                    y8_ref[pl.ds(at_8 + 8 * tokens * j, 8), :] = fold(h * cb)
                    new.append(h)
                return tuple(new)

            lax.fori_loop(0, length, forward, (zero,) * GROUP, unroll=unroll)

            def backward(back_step, carry):
                step = length - 1 - back_step
                row, at_8, at, slot = places(step)
                prev = pl.ds(pl.multiple_of(step * states, states), states)
                bb, cb = bb_ref[at, :], cb_ref[at, :]
                pend, acc = carry
                gb = gb_ref[at, :]
                gc = gc_ref[at, :]
                new, acc_new = [], []
                for j in range(GROUP):
                    dt = dt_row_ref[pl.ds(row + j, 1), :]
                    dx = dx_row_ref[pl.ds(row + j, 1), :]
                    dy = dy_row_ref[pl.ds(row + j, 1), :]
                    g = pend[j] + cb * dy
                    gc = gc + hist_ref[slot, cut(j)] * dy
                    u8_ref[pl.ds(at_8 + 8 * tokens * j, 8), :] = fold(g * bb)
                    gb = gb + g * dx
                    p = jnp.exp2(rate2[j] * dt) * g
                    w = p * hist_ref[prev, cut(j)]
                    v8_ref[pl.ds(at_8 + 8 * tokens * j, 8), :] = fold(w * rate1[j])
                    acc_new.append(acc[j] + w * dt)
                    new.append(p)
                gb_ref[at, :] = gb
                gc_ref[at, :] = gc
                return tuple(new), tuple(acc_new)

            start = ((zero,) * GROUP, grads)
            return lax.fori_loop(0, length, backward, start, unroll=unroll)[1]

        grads = lax.fori_loop(0, lines, one_line, (zero,) * GROUP)
        for j in range(GROUP):
            gvec_ref[:states, cuts[j]] = grads[j] * rate1[j]

        def gather(block, carry):
            rows = pl.ds(pl.multiple_of(block * 8, 8), 8)

            def summed(ref, j):
                begin = block * 64 + 8 * tokens * j
                return total([ref[pl.ds(begin + r, 8, stride=8), :] for r in range(8)])

            for j in range(GROUP):
                c = cuts[j]
                u = summed(u8_ref, j)
                x_row_ref[pl.ds(block * 8 * tiles + first + j, 8, stride=tiles), :] = summed(y8_ref, j)
                grad_spacing = summed(v8_ref, j) + xf_ref[rows, c] * u
                pre_ref[rows, c] = grad_spacing * jax.nn.sigmoid(pre_ref[rows, c])
                dt_ref[rows, c] = dt_ref[rows, c] * u
            return carry

        lax.fori_loop(0, tokens // 8, gather, 0, unroll=2)

    for ref, at in parts_of(out_refs):
        write_part(ref, 0, x_row_ref[at, :])
    grad_pre = pre_ref[...]
    gvec_ref[states:, :] = jnp.broadcast_to(
        jnp.sum(grad_pre, axis=0, keepdims=True), (8, inner)
    )
    grad_pre_b = grad_pre.astype(BF)
    grad_pre_ref[...] = grad_pre_b
    ones = jnp.ones((LANES, LANES), BF)

    def lane_total(ref):
        value = ref[...]
        top = value.astype(BF)
        rest = (value - top.astype(F32)).astype(BF)
        return jnp.dot(top, ones, preferred_element_type=F32) + jnp.dot(
            rest, ones, preferred_element_type=F32
        )

    shape = (tokens * states, LANES)
    state_at = lax.broadcasted_iota(jnp.int32, shape, 0) % states
    lane_at = lax.broadcasted_iota(jnp.int32, shape, 1)
    gb_ref[...] = jnp.where(lane_at == state_at + rank, lane_total(gb_ref), 0.0) + jnp.where(
        lane_at == state_at + rank + states, lane_total(gc_ref), 0.0
    )
    grad_maps = total([gb_ref[pl.ds(n, tokens, stride=states), :] for n in range(states)])
    grad_low = lax.dot_general(grad_pre_b, w_dt, NT, preferred_element_type=F32)
    grad_select_out = (grad_low + grad_maps).astype(BF)
    grad_low_ref[...] = grad_select_out
    back = dt_ref[...] + lax.dot_general(
        grad_select_out, wsel_ref[...], NT, preferred_element_type=F32
    )
    for j in range(tiles):
        to_flat(x_row_ref, j, back[:, cut(j)], tiles)
    for ref, at in parts_of(out_refs):
        write_part(ref, 1, x_row_ref[at, :])


def direction(name, length, row_of, order, place, data, params):
    inner = params[0].shape[0]
    tiles = inner // LANES
    tokens = sum(d.shape[0] * d.shape[2] for d in data) // tiles
    states = params[3].shape[0]
    plane = ((tokens, inner), F32)
    flat = ((tokens * tiles, LANES), F32)
    maps = ((tokens * states, LANES), F32)
    eights = ((tokens * 8 * GROUP, LANES), F32)
    results = call(
        functools.partial(scan_kernel, length, row_of, len(data)),
        name,
        [(d.shape, BF) for d in data]
        + [((tokens, inner), BF)] * 2
        + [((tokens, LANES), BF)] * 2
        + [((states + 8, inner), F32)],
        [plane] * 3
        + [flat] * 4
        + [maps] * 4
        + [(((length + 1) * states, GROUP * LANES), F32)]
        + [eights] * 3
        + [((states, inner), F32)] * 2,
        VMEM_ALL,
        2e10,
        (order, place, *data, *params),
        smem=(0, 1),
    )
    return results[: len(data)], results[len(data) :]


def small_kernel(own_ref, *refs):
    found, refs = [refs[5 * d : 5 * d + 5] for d in range(3)], refs[15:]
    send_ref, row_ref, turned_ref = refs
    inner = found[0][0].shape[1]
    tiles = inner // LANES
    tokens = own_ref.shape[2] // tiles
    own = inner // send_ref.shape[0]
    states = found[0][4].shape[0] - 8
    rank = LANES - 2 * states
    row_ref[...] = own_ref[0, 0].astype(F32) * own_ref[0, 1].astype(F32)
    skips = jnp.concatenate(
        [
            jnp.sum(from_flat(row_ref, j, tokens, tiles), axis=0, keepdims=True)
            for j in range(tiles)
        ],
        axis=1,
    )
    x, grad_pre, low, grad_low = [
        jnp.concatenate([d[i][...] for d in found], axis=0) for i in range(4)
    ]
    summed = total([d[4][...] for d in found])
    at = lax.broadcasted_iota(jnp.int32, (LANES, inner), 0)
    vectors = jnp.concatenate(
        [jnp.zeros((rank, inner), F32), summed, jnp.zeros((states - 8, inner), F32)], axis=0
    )
    vectors = jnp.where(at > rank + states, 0.0, vectors) + jnp.where(
        at == rank + states + 1, jnp.broadcast_to(skips, at.shape), 0.0
    )
    turned_ref[0, :inner] = lax.dot_general(x, grad_low, TN, preferred_element_type=F32)
    turned_ref[1, :inner] = vectors.T + lax.dot_general(
        grad_pre, low, TN, preferred_element_type=F32
    )
    turned_ref[:, inner:] = jnp.zeros((2, SLOT - own, LANES), F32)
    for d in range(send_ref.shape[0]):
        for which in (0, 1):
            send_ref[d, which * SLOT : (which + 1) * SLOT] = turned_ref[
                which, d * own : d * own + SLOT
            ].astype(BF)


def spread_rows(ref, which, m, own, near):
    return jnp.concatenate(
        [ref[which, pl.ds(m * own + i, FAR_SIZE, stride=near * own), :] for i in range(own)],
        axis=0,
    ).astype(BF)


def post_kernel(
    wait,
    place_ref,
    own_ref,
    time_ref,
    wide_ref,
    slot_0_ref,
    slot_1_ref,
    slot_2_ref,
    slot_3_ref,
    pre_ref,
    latent_ref,
    mod_ref,
    skip_ref,
    w_in_ref,
    mixed_out_ref,
    normed_grad_ref,
    send_ref,
    sum_ref,
    own_row_ref,
    plane_ref,
    turned_ref,
    vec_ref,
):
    tokens, width = latent_ref.shape
    inner = w_in_ref.shape[1]
    tiles = inner // LANES
    flat_shape = (tokens * tiles, LANES)
    near = send_ref.shape[0]
    near_rows = inner // near
    own = near_rows // FAR_SIZE

    def summed(which):
        sum_ref[...] = time_ref[0, which].astype(F32) + wide_ref[:, which].reshape(
            flat_shape
        ).astype(F32)
        for k, ref in enumerate((slot_0_ref, slot_1_ref, slot_2_ref, slot_3_ref)):
            chunk = ref.shape[2]
            at = pl.ds(pl.multiple_of((place_ref[0] ^ k) * chunk, chunk), chunk)
            sum_ref[at, :] += ref[0, which].astype(F32)
        own_row_ref[...] = own_ref[0, which].astype(F32)
        for j in range(tiles):
            mine = from_flat(own_row_ref, j, tokens, tiles)
            plane_ref[:, cut(j)] = from_flat(sum_ref, j, tokens, tiles) + skip_ref[:, cut(j)] * mine

    summed(1)
    pre_act = pre_ref[...]
    gate = jax.nn.sigmoid(pre_act)
    grad_act = (plane_ref[...] * gate * (1.0 + pre_act * (1.0 - gate))).astype(BF)
    summed(0)
    mixed = plane_ref[...].astype(BF)
    mixed_out_ref[...] = mixed
    wait(12)
    grad_shifted = lax.dot_general(grad_act, w_in_ref[...], NT, preferred_element_type=F32)
    normed, _ = normalise(latent_ref[...])
    normed_grad_ref[...] = grad_shifted * (1.0 + mod_ref[:1, width:])
    grad_vec = jnp.concatenate(
        [
            jnp.sum(grad_shifted, axis=0, keepdims=True),
            jnp.sum(grad_shifted * normed, axis=0, keepdims=True),
        ],
        axis=1,
    )
    devices = near * FAR_SIZE
    part = 2 * own
    shape = (devices, 2 * width)
    block_at = lax.broadcasted_iota(jnp.int32, shape, 0) * part
    column_at = lax.broadcasted_iota(jnp.int32, shape, 1)
    mine = (column_at >= block_at) & (column_at < block_at + part)
    chosen = jnp.where(mine, jnp.broadcast_to(grad_vec, shape), 0.0)
    top = chosen.astype(BF)
    rest = (chosen - top.astype(F32)).astype(BF)
    lane_at = lax.broadcasted_iota(jnp.int32, (2 * width, LANES), 1)
    place = lax.broadcasted_iota(jnp.int32, (2 * width, LANES), 0) % part
    choose = jnp.where(lane_at == place, 1.0, 0.0).astype(BF)
    vec_ref[...] = jnp.dot(top, choose, preferred_element_type=F32) + jnp.dot(
        rest, choose, preferred_element_type=F32
    )
    turned_ref[0] = mixed.astype(F32).T
    turned_ref[1] = grad_act.astype(F32).T
    for m in range(near):
        send_ref[m, :near_rows] = spread_rows(turned_ref, 0, m, own, near)
        send_ref[m, near_rows : 2 * near_rows] = turned_ref[
            1, pl.ds(m * near_rows, near_rows), :
        ].astype(BF)
        send_ref[m, 2 * near_rows :] = jnp.concatenate(
            [vec_ref[pl.ds(m, FAR_SIZE, stride=near), :], jnp.zeros((8, LANES), F32)], axis=0
        ).astype(BF)


def finish_kernel(
    mixed_ref, normed_grad_ref, latent_ref, w_out_ref, branch_ref, latent_grad_ref
):
    branch_ref[...] = jnp.dot(
        mixed_ref[...], w_out_ref[...], preferred_element_type=F32
    ).astype(BF)
    normed, inverse = normalise(latent_ref[...])
    grad_normed = normed_grad_ref[...]
    product = jnp.mean(grad_normed * normed, axis=1, keepdims=True)
    latent_grad_ref[...] = (inverse * (grad_normed - normed * product)).astype(BF)


def long_product(wait, at, left, right_ref):
    size = right_ref.shape[0] // PIECES
    tokens, width = right_ref.shape[1:]
    terms = []
    for n in range(PIECES):
        wait(at, n)
        rows = slice(n * size * tokens, (n + 1) * size * tokens)
        right = right_ref[n * size : (n + 1) * size].reshape(size * tokens, width)
        terms.append(jnp.dot(left[:, rows], right, preferred_element_type=F32))
    return total(terms)


def in_grad_kernel(wait, recv_ref, both_ref, small_ref, all_ref, right_ref, rows_ref):
    near = recv_ref.shape[0]
    rows = right_ref.shape[0]
    width = both_ref.shape[2]
    own = rows // FAR_SIZE
    for s in range(near):
        right_ref[:, cut(s)] = recv_ref[s, rows : 2 * rows]
    all_ref[:, SLOT:] = small_ref[...]
    product = long_product(wait, 1, right_ref, both_ref)
    turned = jnp.concatenate([product, jnp.zeros((LANES - rows, width), F32)], axis=0).T
    rows_ref[:width] = turned
    rows_ref[width:] = jnp.zeros((rows_ref.shape[0] - width, LANES), F32)
    for d in range(all_ref.shape[0]):
        all_ref[d, :SLOT] = rows_ref[pl.ds(d * own, SLOT), :].astype(BF)


def out_grad_kernel(wait, place_ref, recv_ref, both_ref, *refs):
    far_refs = refs[:FAR_SIZE]
    left_ref, out_ref, half_ref = refs[FAR_SIZE:]
    near = recv_ref.shape[0]
    rows = left_ref.shape[0]
    far = FAR_SIZE
    tiles = both_ref.shape[2] // LANES
    own = rows // far
    for s in range(near):
        left_ref[:, cut(s)] = recv_ref[s, :rows]
    vec = total([recv_ref[s, 2 * rows :].astype(F32) for s in range(near)])
    base = own * tiles
    for o in range(far):
        out_ref[o, base:, :] = jnp.broadcast_to(vec[o : o + 1], (SLOT, LANES))
    product = long_product(wait, 2, left_ref, both_ref)
    for j in range(tiles):
        half_ref[...] = product[:, cut(j)]
        for o in range(far):
            out_ref[o, pl.ds(j, own, stride=tiles), :] = half_ref[pl.ds(o, own, stride=far), :]
    for k, ref in enumerate(far_refs):
        ref[...] = out_ref[place_ref[0] ^ k].astype(BF)


def last_kernel(all_ref, feature_ref, *refs):
    far_refs = refs[:FAR_SIZE]
    gwo_ref, gwi_ref, gsel_ref, small_ref, gmod_ref, sum_ref, rest_ref = refs[FAR_SIZE:]
    far = FAR_SIZE
    own, width = gwo_ref.shape
    tiles = width // LANES
    near = all_ref.shape[0] // far
    part = width // near
    sum_ref[...] = total([ref[...].astype(F32) for ref in far_refs])
    for j in range(tiles):
        gwo_ref[:, cut(j)] = sum_ref[pl.ds(j, own, stride=tiles), :]
    vec = sum_ref[own * tiles : own * tiles + 8, :].T
    gmod_ref[...] = vec[: 2 * own, :1] * feature_ref[:1, :].astype(F32)
    rest = []
    for m in range(near):
        block = total([all_ref[o * near + m].astype(F32) for o in range(far)])
        gwi_ref[:, part * m : part * (m + 1)] = block[:own, :part]
        rest.append(block[SLOT:])
    rest_ref[...] = total(rest)
    gsel_ref[...] = rest_ref[:own, :]
    small_ref[...] = rest_ref[SLOT : SLOT + own, :]


def permute(value, axes, k):
    if k == 0:
        return value
    return lax.ppermute(value, axes, [(i, i ^ k) for i in range(lax.axis_size(axes))])


def exchange(value, axes):
    return lax.all_to_all(value, axes, split_axis=0, concat_axis=0, tiled=True)


def local(
    latent,
    out_grad,
    w_in,
    w_out,
    w_select,
    w_dt,
    dt_bias,
    a_log,
    d_skip,
    w_mod,
    t_index,
    frame_order,
    row_order,
    col_order,
):
    frames, rows, cols, width = latent.shape
    inner = w_in.shape[1]
    tokens = frames * rows * cols
    tiles = inner // LANES
    states = a_log.shape[1]
    n_row, n_col = lax.axis_size(ROW), lax.axis_size(COL)
    near, far = lax.axis_size(NEAR), lax.axis_size(FAR)
    own = width // (near * far)
    flat_latent = latent.reshape(tokens, width)
    flat_grad = out_grad.reshape(tokens, width)
    features = jax.nn.silu(time_features(t_index, w_mod.shape[1])).astype(BF)
    feature_rows = jnp.broadcast_to(features[None, :], (8, features.shape[0]))

    def packed(parts):
        return ((parts, 2, tokens * tiles // parts, LANES), BF)

    slot = ((1, 2, tokens * tiles // n_row, LANES), BF)
    place = lax.axis_index(ROW).astype(jnp.int32)[None]
    far_place = lax.axis_index(FAR).astype(jnp.int32)[None]
    data_own, data_wide, *slots, both, pre_act, modulation = call(
        pre_kernel,
        "norm_project",
        [
            packed(1),
            packed(n_col),
            slot,
            slot,
            slot,
            slot,
            ((2, tokens, width), BF),
            ((tokens, inner), F32),
            ((8, 2 * width), F32),
        ],
        [((tokens * tiles, LANES), F32)],
        VMEM_ALL,
        7e9,
        (flat_latent, flat_grad, w_in, w_out, w_mod, feature_rows, place),
        smem=(6,),
        late=(2, 3),
    )
    data_wide = exchange(data_wide, COL)
    slots = [permute(value, ROW, k) for k, value in enumerate(slots)]
    both_near = lax.all_gather(both, NEAR, axis=0, tiled=False)
    params = (
        w_select,
        w_dt.T,
        dt_bias[None, :],
        a_log.T,
    )
    area = rows * cols

    def time_row(at, line, place):
        return at * area + line

    def wide_row(at, line, place):
        chunk = frames // n_col * area
        return (
            lax.div(at, cols) * chunk
            + lax.rem(at, cols)
            + lax.div(line, rows) * area
            + lax.rem(line, rows) * cols
        )

    def tall_row(at, line, place):
        chunk = frames // n_row * area
        return (
            (lax.div(at, rows) ^ place) * chunk
            + lax.rem(at, rows) * cols
            + lax.div(line, cols) * area
            + lax.rem(line, cols)
        )

    out_tall, grads_tall = direction(
        "scan_height", rows * n_row, tall_row, row_order, place, slots, params
    )
    out_slots = [permute(value, ROW, k) for k, value in enumerate(out_tall)]
    data_wide, _ = lax.optimization_barrier((data_wide, out_tall))
    (out_wide,), grads_wide = direction(
        "scan_width", cols * n_col, wide_row, col_order, place, [data_wide], params
    )
    data_time, out_slots, _ = lax.optimization_barrier((data_own, out_slots, out_wide))
    out_wide = exchange(out_wide, COL)
    (out_time,), grads_time = direction(
        "scan_time", frames, time_row, frame_order, place, [data_time], params
    )
    mixed, normed_grad, near_send = call(
        post_kernel,
        "sum_project",
        [
            ((tokens, inner), BF),
            ((tokens, width), F32),
            ((near, 2 * inner // near + 16, LANES), BF),
        ],
        [
            ((tokens * tiles, LANES), F32),
            ((tokens * tiles, LANES), F32),
            ((tokens, inner), F32),
            ((2, inner, LANES), F32),
            ((near * far, LANES), F32),
        ],
        VMEM_ALL,
        8e9,
        (
            place,
            data_own,
            out_time,
            out_wide,
            *out_slots,
            pre_act,
            flat_latent,
            modulation,
            d_skip[None, :],
            w_in,
        ),
        smem=(0,),
        late=(12,),
    )
    near_recv = exchange(near_send, NEAR)
    data_own, _ = lax.optimization_barrier((data_own, near_send))
    small_send = call(
        small_kernel,
        "small_sums",
        [((near * far, 2 * SLOT, LANES), BF)],
        [((tokens * tiles, LANES), F32), ((2, inner + SLOT - own, LANES), F32)],
        VMEM_ALL,
        3e9,
        (data_own, *grads_time, *grads_wide, *grads_tall),
    )[0]
    branch, latent_grad = plain_call(
        finish_kernel,
        "out_project",
        [((tokens, width), BF), ((tokens, width), BF)],
        [],
        24,
        2e9,
        (mixed, normed_grad, flat_latent, w_out),
    )
    piece = own * tiles + SLOT
    all_send = call(
        in_grad_kernel,
        "in_weight_grad",
        [((near * far, 3 * SLOT, LANES), BF)],
        [((inner // near, near * tokens), BF), ((width + SLOT - own, LANES), F32)],
        VMEM_ALL,
        3e9,
        (near_recv, both_near, small_send),
        late=(1,),
        pieces={1: PIECES},
        choose={1: 0},
    )[0]
    all_recv = exchange(all_send, FAR + NEAR)
    far_send = call(
        out_grad_kernel,
        "out_weight_grad",
        [((piece, LANES), BF)] * far,
        [
            ((inner // near, near * tokens), BF),
            ((far, piece, LANES), F32),
            ((inner // near, LANES), F32),
        ],
        VMEM_ALL,
        4e9,
        (far_place, near_recv, both_near),
        smem=(0,),
        late=(2,),
        pieces={2: PIECES},
        choose={2: 1},
    )
    far_recv = [permute(value, FAR, k) for k, value in enumerate(far_send)]
    grad_w_out, grad_w_in, grad_select, small, grad_mod = plain_call(
        last_kernel,
        "weight_sums",
        [
            ((own, width), F32),
            ((own, width), F32),
            ((own, LANES), F32),
            ((own, LANES), F32),
            ((2 * own, features.shape[0]), F32),
        ],
        [((piece, LANES), F32), ((2 * SLOT, LANES), F32)],
        16,
        1e9,
        (all_recv, feature_rows, *far_recv),
    )
    rank = w_dt.shape[1]
    return (
        branch.reshape(latent.shape),
        latent_grad.reshape(latent.shape),
        grad_w_in,
        grad_w_out,
        grad_select,
        small[:, :rank],
        small[:, rank + states],
        small[:, rank : rank + states],
        small[:, rank + states + 1],
        grad_mod,
    )


def solution(mesh):
    n_row, n_col = mesh.shape["row"], mesh.shape["col"]
    split = Mesh(mesh.devices.reshape(n_row // 2, 2, 2, 4, n_col // 8), AXES)
    tokens = P(None, ROW, COL, None)
    matrix = P(ROW + COL, None)
    vector = P(ROW + COL)
    return jax.shard_map(
        local,
        mesh=split,
        in_specs=(tokens, tokens) + (P(),) * 12,
        out_specs=(
            tokens,
            tokens,
            matrix,
            matrix,
            matrix,
            matrix,
            vector,
            matrix,
            vector,
            matrix,
        ),
        check_vma=False,
    )
```

```python
import functools
import math

import jax
import jax.numpy as jnp
from jax import lax
from jax.experimental import pallas as pl
from jax.experimental.pallas import tpu as pltpu
from jax.sharding import Mesh
from jax.sharding import PartitionSpec as P

BF = jnp.bfloat16
F32 = jnp.float32
LANES = 128
GROUP = 6
EIGHT = 9
LOG2E = math.log2(math.e)
MEGA = 1024 * 1024
VMEM_ALL = 63
PIECES = 4
SLOT = 16
AXES = ("xl", "core", "xh", "y", "z")
ROW = ("xl", "core")
COL = ("xh", "y", "z")
NEAR = ("y", "z")
FAR = ("xl", "core", "xh")
FAR_SIZE = 8
NT = (((1,), (1,)), ((), ()))
TN = (((0,), (0,)), ((), ()))


def time_features(step_index, width):
    halfway = width // 2
    frequency = jnp.exp(-math.log(10000.0) * jnp.arange(halfway, dtype=jnp.float32) / halfway)
    angles = step_index.astype(jnp.float32)[0] * frequency
    return jnp.concatenate([jnp.cos(angles), jnp.sin(angles)])


def total(terms):
    return functools.reduce(lambda a, b: a + b, terms)


def call(kernel, name, out_shape, scratch, vmem, flops, args, smem=(), late=(), pieces=None, choose=None, early=()):
    moved = [i for i in range(len(args)) if i not in smem]
    pieces, choose = pieces or {}, choose or {}
    held_shape = {
        i: args[i].shape[:1] + args[i].shape[2:] if i in choose else args[i].shape for i in moved
    }
    cuts = []
    for i in moved:
        size = args[i].shape[0] // pieces.get(i, 1)
        cuts += [(i, n, pl.ds(n * size, size)) for n in range(pieces.get(i, 1))]

    def body(*refs):
        given, out = refs[: len(args)], refs[len(args) : len(args) + len(out_shape)]
        rest = refs[len(args) + len(out_shape) :]
        held, rest = rest[: len(moved)], rest[len(moved) :]
        made, rest = rest[: len(out_shape)], rest[len(out_shape) :]
        in_sem, out_sem = rest[-2:]
        views = [given[i] if i in smem else held[moved.index(i)] for i in range(len(args))]
        copies = {
            (i, n): pltpu.make_async_copy(
                given[i].at[at, choose[i]] if i in choose else given[i].at[at],
                views[i].at[at],
                in_sem.at[place],
            )
            for place, (i, n, at) in enumerate(cuts)
        }
        for copy in copies.values():
            copy.start()
        for (i, _), copy in copies.items():
            if i not in late:
                copy.wait()
        waits = (lambda i, n=0: copies[i, n].wait(),) if late else ()
        sent = []

        def send(n, plane=None):
            at = (slice(None), plane) if plane is not None else (slice(None),)
            place = 2 * n + (plane or 0)
            copy = pltpu.make_async_copy(made[n].at[at], out[n].at[at], out_sem.at[place])
            copy.start()
            sent.append(copy)

        kernel(*waits, *((send,) if early else ()), *views, *made, *rest[:-2])
        for n in range(len(out_shape)):
            if n not in early:
                send(n)
        for copy in sent:
            copy.wait()

    spaces = [
        pl.BlockSpec(memory_space=pltpu.SMEM if i in smem else pltpu.HBM) for i in range(len(args))
    ]
    return pl.pallas_call(
        body,
        out_shape=tuple(jax.ShapeDtypeStruct(s, d) for s, d in out_shape),
        in_specs=spaces,
        out_specs=(pl.BlockSpec(memory_space=pltpu.HBM),) * len(out_shape),
        scratch_shapes=[pltpu.VMEM(held_shape[i], args[i].dtype) for i in moved]
        + [pltpu.VMEM(s, d) for s, d in out_shape]
        + [pltpu.VMEM(s, d) for s, d in scratch]
        + [pltpu.SemaphoreType.DMA((len(cuts),)), pltpu.SemaphoreType.DMA((2 * len(out_shape),))],
        compiler_params=pltpu.CompilerParams(vmem_limit_bytes=vmem * MEGA),
        cost_estimate=cost(flops, args),
        name=name,
    )(*args)


def cost(flops, args):
    return pl.CostEstimate(
        flops=int(flops),
        bytes_accessed=sum(a.size * a.dtype.itemsize for a in args),
        transcendentals=0,
    )


def plain_call(kernel, name, out_shape, scratch, vmem, flops, args, smem=()):
    spaces = [
        pl.BlockSpec(memory_space=pltpu.SMEM if i in smem else pltpu.VMEM) for i in range(len(args))
    ]
    return pl.pallas_call(
        kernel,
        out_shape=tuple(jax.ShapeDtypeStruct(s, d) for s, d in out_shape),
        in_specs=spaces,
        out_specs=(pl.BlockSpec(memory_space=pltpu.VMEM),) * len(out_shape),
        scratch_shapes=[pltpu.VMEM(s, d) for s, d in scratch],
        compiler_params=pltpu.CompilerParams(vmem_limit_bytes=vmem * MEGA),
        cost_estimate=cost(flops, args),
        name=name,
    )(*args)


def cut(j):
    return slice(LANES * j, LANES * j + LANES)


def to_flat(ref, j, value, tiles):
    ref[pl.ds(j, value.shape[0], stride=tiles), :] = value


def from_flat(ref, j, tokens, tiles):
    return ref[pl.ds(j, tokens, stride=tiles), :]


def normalise(latent):
    wide = latent.astype(F32)
    inverse = lax.rsqrt(jnp.mean(wide * wide, axis=-1, keepdims=True) + 1e-06)
    return wide * inverse, inverse


def pre_kernel(
    wait,
    send,
    latent_ref,
    grad_ref,
    w_in_ref,
    w_out_ref,
    w_mod_ref,
    feature_ref,
    place_ref,
    own_ref,
    wide_ref,
    slot_0_ref,
    slot_1_ref,
    slot_2_ref,
    slot_3_ref,
    both_ref,
    pre_ref,
    mod_ref,
    cot_ref,
    flat_ref,
):
    tokens, width = latent_ref.shape
    tiles = w_in_ref.shape[1] // LANES
    modulation = lax.dot_general(
        feature_ref[...], w_mod_ref[...], NT, preferred_element_type=F32
    )
    mod_ref[...] = modulation
    send(8)
    normed, _ = normalise(latent_ref[...])
    shifted = (normed * (1.0 + modulation[:1, width:]) + modulation[:1, :width]).astype(BF)
    both_ref[0] = shifted
    wait(1)
    both_ref[1] = grad_ref[...]
    send(6)
    wait(2)
    pre_act = jnp.dot(shifted, w_in_ref[...], preferred_element_type=F32)
    pre_ref[...] = pre_act
    send(7)
    activ = (pre_act * jax.nn.sigmoid(pre_act)).astype(BF)

    def pack(which, value):
        wide = value.astype(F32)
        for j in range(tiles):
            to_flat(flat_ref, j, wide[:, cut(j)], tiles)
        flat = flat_ref[...].astype(BF)
        own_ref[0, which] = flat
        wide_ref[:, which] = flat.reshape(wide_ref.shape[0], wide_ref.shape[2], LANES)
        for k, ref in enumerate((slot_0_ref, slot_1_ref, slot_2_ref, slot_3_ref)):
            chunk = ref.shape[2]
            begin = pl.multiple_of((place_ref[0] ^ k) * chunk, chunk)
            ref[0, which] = flat_ref[pl.ds(begin, chunk), :].astype(BF)
        for n in range(6):
            send(n, which)

    pack(0, activ)
    wait(3)
    cot = lax.dot_general(grad_ref[...], w_out_ref[...], NT, preferred_element_type=F32).astype(BF)
    cot_ref[...] = cot
    send(9)
    pack(1, cot)


def parts_of(refs):
    begin, found = 0, []
    for ref in refs:
        size = ref.shape[0] * ref.shape[2]
        found.append((ref, slice(begin, begin + size)))
        begin += size
    return found


def read_part(ref, which):
    return ref[:, which].reshape(ref.shape[0] * ref.shape[2], LANES).astype(F32)


def write_part(ref, which, value):
    ref[:, which] = value.astype(BF).reshape(ref.shape[0], ref.shape[2], LANES)


def scan_kernel(
    length,
    row_of,
    pieces,
    wait,
    send,
    order_ref,
    place_ref,
    *refs,
):
    data_refs, out_refs = refs[:pieces], refs[pieces + 4 : 2 * pieces + 4]
    scan_steps(
        length,
        row_of,
        order_ref,
        place_ref,
        data_refs,
        *refs[pieces : pieces + 4],
        out_refs,
        *refs[2 * pieces + 4 :],
        functools.partial(wait_for, wait, 2 + pieces),
        functools.partial(send_from, send, pieces),
    )


def wait_for(wait, first, n):
    wait(first + n)


def send_from(send, pieces, n):
    if n < 2:
        for k in range(pieces):
            send(k, n)
    else:
        send(pieces + n - 2)


def scan_steps(
    length,
    row_of,
    order_ref,
    place_ref,
    data_refs,
    wsel_ref,
    wdt_ref,
    bias_ref,
    alog_ref,
    out_refs,
    x_ref,
    grad_pre_ref,
    low_ref,
    grad_low_ref,
    gvec_ref,
    pre_ref,
    dt_ref,
    xf_ref,
    x_row_ref,
    dt_row_ref,
    dx_row_ref,
    dy_row_ref,
    bb_ref,
    cb_ref,
    gb_ref,
    gc_ref,
    hist_ref,
    keep_ref,
    y8_ref,
    u8_ref,
    v8_ref,
    rate2_ref,
    rate_ref,
    wait,
    send,
):
    tokens, inner = xf_ref.shape
    tiles = inner // LANES
    lines = tokens // length
    states = alog_ref.shape[0]
    rank = LANES - 2 * states
    for ref, at in parts_of(data_refs):
        x_row_ref[at, :] = read_part(ref, 0)
        dy_row_ref[at, :] = read_part(ref, 1)
    for j in range(tiles):
        xf_ref[:, cut(j)] = from_flat(x_row_ref, j, tokens, tiles)
    x = xf_ref[...].astype(BF)
    x_ref[...] = x
    send(2)
    wait(0)
    select = jnp.dot(x, wsel_ref[...], preferred_element_type=F32)
    lane = lax.broadcasted_iota(jnp.int32, (tokens, LANES), 1)
    low = jnp.where(lane < rank, select, 0.0).astype(BF)
    low_ref[...] = low
    send(4)
    wait(1)
    w_dt = jnp.concatenate([wdt_ref[...], jnp.zeros((2 * states, inner), BF)], axis=0)
    pre = jnp.dot(low, w_dt, preferred_element_type=F32) + bias_ref[:1, :]
    pre_ref[...] = pre
    spacing = jnp.maximum(pre, 0.0) + jnp.log1p(jnp.exp(-jnp.abs(pre)))
    dt_ref[...] = spacing
    for j in range(tiles):
        at = slice(j * tokens, (j + 1) * tokens)
        dt_row_ref[at, :] = spacing[:, cut(j)]
        dx_row_ref[at, :] = spacing[:, cut(j)] * xf_ref[:, cut(j)]
    rates = -jnp.exp(alog_ref[...])
    rate_ref[...] = rates
    rate2_ref[...] = rates * LOG2E
    turned = select.T
    for token in range(tokens):
        at = pl.ds(token * states, states)
        column = slice(token, token + 1)
        bb_ref[at, :] = jnp.broadcast_to(turned[rank : rank + states, column], (states, LANES))
        cb_ref[at, :] = jnp.broadcast_to(turned[rank + states :, column], (states, LANES))
    gb_ref[...] = jnp.zeros_like(gb_ref)
    gc_ref[...] = jnp.zeros_like(gc_ref)
    zero = jnp.zeros((states, LANES), F32)
    hist_ref[pl.ds(0, states), :] = jnp.zeros((states, GROUP * LANES), F32)
    unroll = min(length, 8)

    def fold(value):
        return value[:8] + value[8:]

    for group in range(tiles // GROUP):
        first = group * GROUP
        cuts = [cut(first + j) for j in range(GROUP)]
        rate2 = [rate2_ref[:, c] for c in cuts]
        rate1 = [rate_ref[:, c] for c in cuts]

        def one_line(line, grads):
            def places(step):
                row = row_of(order_ref[step], line, place_ref[0])
                at = pl.ds(pl.multiple_of(row * states, states), states)
                slot = pl.ds(pl.multiple_of((step + 1) * states, states), states)
                return row, row * EIGHT, at, slot

            def forward(step, carry):
                row, at_8, at, slot = places(step)
                bb, cb = bb_ref[at, :], cb_ref[at, :]
                new = []
                for j in range(GROUP):
                    dt = dt_row_ref[pl.ds(row + (first + j) * tokens, 1), :]
                    dx = dx_row_ref[pl.ds(row + (first + j) * tokens, 1), :]
                    decay = jnp.exp2(rate2[j] * dt)
                    keep_ref[slot, cut(j)] = decay
                    h = decay * carry[j] + bb * dx
                    hist_ref[slot, cut(j)] = h
                    y8_ref[pl.ds(at_8 + EIGHT * tokens * j, 8), :] = fold(h * cb)
                    new.append(h)
                return tuple(new)

            lax.fori_loop(0, length, forward, (zero,) * GROUP, unroll=unroll)

            def backward(back_step, carry):
                step = length - 1 - back_step
                row, at_8, at, slot = places(step)
                prev = pl.ds(pl.multiple_of(step * states, states), states)
                bb, cb = bb_ref[at, :], cb_ref[at, :]
                pend, acc = carry
                gb = gb_ref[at, :]
                gc = gc_ref[at, :]
                new, acc_new = [], []
                for j in range(GROUP):
                    dt = dt_row_ref[pl.ds(row + (first + j) * tokens, 1), :]
                    dx = dx_row_ref[pl.ds(row + (first + j) * tokens, 1), :]
                    dy = dy_row_ref[pl.ds(row * tiles + first + j, 1), :]
                    g = pend[j] + cb * dy
                    gc = gc + hist_ref[slot, cut(j)] * dy
                    u8_ref[pl.ds(at_8 + EIGHT * tokens * j, 8), :] = fold(g * bb)
                    gb = gb + g * dx
                    p = keep_ref[slot, cut(j)] * g
                    w = p * hist_ref[prev, cut(j)]
                    v8_ref[pl.ds(at_8 + EIGHT * tokens * j, 8), :] = fold(w * rate1[j])
                    acc_new.append(acc[j] + w * dt)
                    new.append(p)
                gb_ref[at, :] = gb
                gc_ref[at, :] = gc
                return tuple(new), tuple(acc_new)

            start = ((zero,) * GROUP, grads)
            return lax.fori_loop(0, length, backward, start, unroll=unroll)[1]

        grads = lax.fori_loop(0, lines, one_line, (zero,) * GROUP)
        for j in range(GROUP):
            gvec_ref[:states, cuts[j]] = grads[j] * rate1[j]

        def gather(block, carry):
            rows = pl.ds(pl.multiple_of(block * 8, 8), 8)

            def summed(ref, j):
                begin = block * (8 * EIGHT) + EIGHT * tokens * j
                return total([ref[pl.ds(begin + r, 8, stride=EIGHT), :] for r in range(8)])

            for j in range(GROUP):
                c = cuts[j]
                u = summed(u8_ref, j)
                x_row_ref[pl.ds(block * 8 * tiles + first + j, 8, stride=tiles), :] = summed(y8_ref, j)
                grad_spacing = summed(v8_ref, j) + xf_ref[rows, c] * u
                pre_ref[rows, c] = grad_spacing * jax.nn.sigmoid(pre_ref[rows, c])
                dt_ref[rows, c] = dt_ref[rows, c] * u
            return carry

        lax.fori_loop(0, tokens // 8, gather, 0, unroll=2)

    for ref, at in parts_of(out_refs):
        write_part(ref, 0, x_row_ref[at, :])
    send(0)
    grad_pre = pre_ref[...]
    gvec_ref[states:, :] = jnp.broadcast_to(
        jnp.sum(grad_pre, axis=0, keepdims=True), (8, inner)
    )
    send(6)
    grad_pre_b = grad_pre.astype(BF)
    grad_pre_ref[...] = grad_pre_b
    send(3)
    shape = (2 * LANES, LANES)
    half = lax.broadcasted_iota(jnp.int32, shape, 0) // LANES
    lane_at = lax.broadcasted_iota(jnp.int32, shape, 1)
    spread = jnp.where((lane_at - rank) // states == half, 1.0, 0.0).astype(BF)
    shape = (tokens * states, LANES)
    state_at = lax.broadcasted_iota(jnp.int32, shape, 0) % states
    lane_at = lax.broadcasted_iota(jnp.int32, shape, 1)
    both = jnp.concatenate([gb_ref[...], gc_ref[...]], axis=1)
    lanes = halves_product(both, spread, False)
    kept = jnp.where((lane_at >= rank) & ((lane_at - rank) % states == state_at), lanes, 0.0)
    shape = (tokens, tokens * states)
    collect = lax.broadcasted_iota(jnp.int32, shape, 1) // states == lax.broadcasted_iota(
        jnp.int32, shape, 0
    )
    grad_maps = halves_product(kept, jnp.where(collect, 1.0, 0.0).astype(BF), True)
    grad_low = lax.dot_general(grad_pre_b, w_dt, NT, preferred_element_type=F32)
    grad_select_out = (grad_low + grad_maps).astype(BF)
    grad_low_ref[...] = grad_select_out
    send(5)
    back = dt_ref[...] + lax.dot_general(
        grad_select_out, wsel_ref[...], NT, preferred_element_type=F32
    )
    for j in range(tiles):
        to_flat(dy_row_ref, j, back[:, cut(j)], tiles)
    for ref, at in parts_of(out_refs):
        write_part(ref, 1, dy_row_ref[at, :])
    send(1)


def halves_product(value, other, other_first):
    top = value.astype(BF)
    rest = (value - top.astype(F32)).astype(BF)
    if other_first:
        return jnp.dot(other, top, preferred_element_type=F32) + jnp.dot(
            other, rest, preferred_element_type=F32
        )
    return jnp.dot(top, other, preferred_element_type=F32) + jnp.dot(
        rest, other, preferred_element_type=F32
    )


def direction(name, length, row_of, order, place, data, params):
    inner = params[0].shape[0]
    tiles = inner // LANES
    tokens = sum(d.shape[0] * d.shape[2] for d in data) // tiles
    states = params[3].shape[0]
    plane = ((tokens, inner), F32)
    flat = ((tokens * tiles, LANES), F32)
    maps = ((tokens * states, LANES), F32)
    eights = ((tokens * EIGHT * GROUP, LANES), F32)
    results = call(
        functools.partial(scan_kernel, length, row_of, len(data)),
        name,
        [(d.shape, BF) for d in data]
        + [((tokens, inner), BF)] * 2
        + [((tokens, LANES), BF)] * 2
        + [((states + 8, inner), F32)],
        [plane] * 3
        + [flat] * 4
        + [maps] * 4
        + [(((length + 1) * states, GROUP * LANES), F32)] * 2
        + [eights] * 3
        + [((states, inner), F32)] * 2,
        VMEM_ALL,
        2e10,
        (order, place, *data, *params),
        smem=(0, 1),
        late=tuple(2 + len(data) + i for i in (0, 1)),
        early=tuple(range(len(data) + 5)),
    )
    return results[: len(data)], results[len(data) :]


def small_kernel(own_ref, *refs):
    found, refs = [refs[5 * d : 5 * d + 5] for d in range(3)], refs[15:]
    send_ref, row_ref, turned_ref, held_ref = refs
    inner = found[0][0].shape[1]
    tiles = inner // LANES
    tokens = own_ref.shape[2] // tiles
    own = inner // send_ref.shape[0]
    states = found[0][4].shape[0] - 8
    rank = LANES - 2 * states
    row_ref[...] = own_ref[0, 0].astype(F32) * own_ref[0, 1].astype(F32)
    skips = jnp.concatenate(
        [
            jnp.sum(from_flat(row_ref, j, tokens, tiles), axis=0, keepdims=True)
            for j in range(tiles)
        ],
        axis=1,
    )
    x, grad_pre, low, grad_low = [
        jnp.concatenate([d[i][...] for d in found], axis=0) for i in range(4)
    ]
    summed = total([d[4][...] for d in found])
    at = lax.broadcasted_iota(jnp.int32, (LANES, inner), 0)
    vectors = jnp.concatenate(
        [jnp.zeros((rank, inner), F32), summed, jnp.zeros((states - 8, inner), F32)], axis=0
    )
    vectors = jnp.where(at > rank + states, 0.0, vectors) + jnp.where(
        at == rank + states + 1, jnp.broadcast_to(skips, at.shape), 0.0
    )
    turned_ref[0] = lax.dot_general(x, grad_low, TN, preferred_element_type=F32)
    turned_ref[1] = vectors.T + lax.dot_general(
        grad_pre, low, TN, preferred_element_type=F32
    )
    for d in range(send_ref.shape[0]):
        for which in (0, 1):
            begin = (2 * d + which) * own
            held_ref[begin : begin + own, :] = turned_ref[which, d * own : (d + 1) * own, :]
    send_ref[...] = held_ref[...].reshape(send_ref.shape).astype(BF)


def spread_rows(ref, which, own, near, held_ref):
    for m in range(near):
        for o in range(FAR_SIZE):
            begin = (o * near + m) * own
            at = (m * FAR_SIZE + o) * own
            held_ref[at : at + own, :] = ref[which, begin : begin + own, :]
    return held_ref[...].reshape(near, FAR_SIZE * own, LANES).astype(BF)


def post_kernel(
    send,
    place_ref,
    activ_ref,
    cot_ref,
    time_ref,
    wide_ref,
    slot_0_ref,
    slot_1_ref,
    slot_2_ref,
    slot_3_ref,
    pre_ref,
    skip_ref,
    mixed_out_ref,
    grad_act_ref,
    send_ref,
    sum_ref,
    turned_ref,
    held_ref,
):
    tokens, inner = pre_ref.shape
    tiles = inner // LANES
    flat_shape = (tokens * tiles, LANES)
    near = send_ref.shape[0]
    near_rows = inner // near
    own = near_rows // FAR_SIZE

    def summed(which, own_ref):
        sum_ref[...] = time_ref[0, which].astype(F32) + wide_ref[:, which].reshape(
            flat_shape
        ).astype(F32)
        for k, ref in enumerate((slot_0_ref, slot_1_ref, slot_2_ref, slot_3_ref)):
            chunk = ref.shape[2]
            at = pl.ds(pl.multiple_of((place_ref[0] ^ k) * chunk, chunk), chunk)
            sum_ref[at, :] += ref[0, which].astype(F32)
        scans = jnp.concatenate([from_flat(sum_ref, j, tokens, tiles) for j in range(tiles)], axis=1)
        return scans + skip_ref[1:, :] * own_ref[...].astype(F32)

    back = summed(1, cot_ref)
    pre_act = pre_ref[...]
    gate = jax.nn.sigmoid(pre_act)
    grad_act = (back * gate * (1.0 + pre_act * (1.0 - gate))).astype(BF)
    grad_act_ref[...] = grad_act
    send(1)
    turned_ref[1] = grad_act.astype(F32).T
    mixed = summed(0, activ_ref).astype(BF)
    mixed_out_ref[...] = mixed
    send(0)
    turned_ref[0] = mixed.astype(F32).T
    send_ref[:, :near_rows] = spread_rows(turned_ref, 0, own, near, held_ref)
    for m in range(near):
        send_ref[m, near_rows:] = turned_ref[1, pl.ds(m * near_rows, near_rows), :].astype(BF)


def finish_kernel(
    wait,
    mixed_ref,
    grad_act_ref,
    latent_ref,
    mod_ref,
    w_in_ref,
    w_out_ref,
    branch_ref,
    latent_grad_ref,
    vec_ref,
):
    tokens, width = latent_ref.shape
    normed, inverse = normalise(latent_ref[...])
    wait(4)
    grad_shifted = lax.dot_general(
        grad_act_ref[...], w_in_ref[...], NT, preferred_element_type=F32
    )
    grad_vec = jnp.concatenate(
        [
            jnp.sum(grad_shifted, axis=0, keepdims=True),
            jnp.sum(grad_shifted * normed, axis=0, keepdims=True),
        ],
        axis=1,
    )
    devices = vec_ref.shape[0]
    part = 2 * width // devices
    shape = (devices, 2 * width)
    block_at = lax.broadcasted_iota(jnp.int32, shape, 0) * part
    column_at = lax.broadcasted_iota(jnp.int32, shape, 1)
    mine = (column_at >= block_at) & (column_at < block_at + part)
    chosen = jnp.where(mine, jnp.broadcast_to(grad_vec, shape), 0.0)
    lane_at = lax.broadcasted_iota(jnp.int32, (2 * width, LANES), 1)
    place = lax.broadcasted_iota(jnp.int32, (2 * width, LANES), 0) % part
    choose = jnp.where(lane_at == place, 1.0, 0.0).astype(BF)
    vec_ref[...] = halves_product(chosen, choose, False)
    grad_normed = grad_shifted * (1.0 + mod_ref[:1, width:])
    product = jnp.mean(grad_normed * normed, axis=1, keepdims=True)
    latent_grad_ref[...] = (inverse * (grad_normed - normed * product)).astype(BF)
    wait(5)
    branch_ref[...] = jnp.dot(
        mixed_ref[...], w_out_ref[...], preferred_element_type=F32
    ).astype(BF)


def long_product(wait, at, left, right_ref):
    size = right_ref.shape[0] // PIECES
    tokens, width = right_ref.shape[1:]
    terms = []
    for n in range(PIECES):
        wait(at, n)
        rows = slice(n * size * tokens, (n + 1) * size * tokens)
        right = right_ref[n * size : (n + 1) * size].reshape(size * tokens, width)
        terms.append(jnp.dot(left[:, rows], right, preferred_element_type=F32))
    return total(terms)


def in_grad_kernel(wait, recv_ref, both_ref, small_ref, vec_ref, all_ref, right_ref, rows_ref):
    near = recv_ref.shape[0]
    rows = right_ref.shape[0]
    width = both_ref.shape[2]
    devices = all_ref.shape[0]
    own = rows // FAR_SIZE
    for s in range(near):
        right_ref[:, cut(s)] = recv_ref[s, rows:]
    all_ref[:, SLOT:] = small_ref[...]
    product = long_product(wait, 1, right_ref, both_ref)
    turned = jnp.concatenate([product, jnp.zeros((LANES - rows, width), F32)], axis=0).T
    for d in range(devices):
        rows_ref[d * SLOT : d * SLOT + own, :] = turned[d * own : (d + 1) * own]
    for n in range(own, SLOT):
        rows_ref[pl.ds(n, devices, stride=SLOT), :] = vec_ref[...]
    all_ref[:, :SLOT] = rows_ref[...].reshape(devices, SLOT, LANES).astype(BF)


def out_grad_kernel(wait, place_ref, recv_ref, both_ref, *refs):
    far_refs = refs[:FAR_SIZE]
    left_ref, out_ref, half_ref = refs[FAR_SIZE:]
    near = recv_ref.shape[0]
    rows = left_ref.shape[0]
    far = FAR_SIZE
    tiles = both_ref.shape[2] // LANES
    own = rows // far
    for s in range(near):
        left_ref[:, cut(s)] = recv_ref[s, :rows]
    product = long_product(wait, 2, left_ref, both_ref)
    for j in range(tiles):
        half_ref[...] = product[:, cut(j)]
        for o in range(far):
            out_ref[o, pl.ds(j, own, stride=tiles), :] = half_ref[o * own : (o + 1) * own, :]
    for k, ref in enumerate(far_refs):
        ref[...] = out_ref[place_ref[0] ^ k].astype(BF)


def last_kernel(all_ref, feature_ref, *refs):
    far_refs = refs[:FAR_SIZE]
    gwo_ref, gwi_ref, gsel_ref, gdt_ref, galog_ref, gvec_ref, gmod_ref, sum_ref, rest_ref = refs[
        FAR_SIZE:
    ]
    far = FAR_SIZE
    own, width = gwo_ref.shape
    tiles = width // LANES
    near = all_ref.shape[0] // far
    part = width // near
    sum_ref[...] = total([ref[...].astype(F32) for ref in far_refs])
    for j in range(tiles):
        gwo_ref[:, cut(j)] = sum_ref[pl.ds(j, own, stride=tiles), :]
    rest = []
    for m in range(near):
        block = total([all_ref[o * near + m].astype(F32) for o in range(far)])
        gwi_ref[:, part * m : part * (m + 1)] = block[:own, :part]
        rest.append(block)
    rest_ref[...] = total(rest)
    vec = rest_ref[own : own + 1, :]
    turned = jnp.broadcast_to(vec, (LANES, LANES)).T
    gmod_ref[...] = turned[: 2 * own, :1] * feature_ref[:1, :].astype(F32)
    gsel_ref[...] = rest_ref[SLOT : SLOT + own, :]
    rank, states = gdt_ref.shape[1], galog_ref.shape[1]
    base = SLOT + own
    gdt_ref[...] = rest_ref[base : base + own, :rank]
    galog_ref[...] = rest_ref[base : base + own, rank : rank + states]
    turned = jnp.concatenate([rest_ref[base : base + own, :], jnp.zeros((LANES - own, LANES), F32)])
    gvec_ref[...] = turned.T[rank + states : rank + states + 8, :own]


def permute(value, axes, k):
    if k == 0:
        return value
    return lax.ppermute(value, axes, [(i, i ^ k) for i in range(lax.axis_size(axes))])


def exchange(value, axes):
    return lax.all_to_all(value, axes, split_axis=0, concat_axis=0, tiled=True)


def local(
    latent,
    out_grad,
    w_in,
    w_out,
    w_select,
    w_dt,
    dt_bias,
    a_log,
    d_skip,
    w_mod,
    t_index,
    frame_order,
    row_order,
    col_order,
):
    frames, rows, cols, width = latent.shape
    inner = w_in.shape[1]
    tokens = frames * rows * cols
    tiles = inner // LANES
    states = a_log.shape[1]
    n_row, n_col = lax.axis_size(ROW), lax.axis_size(COL)
    near, far = lax.axis_size(NEAR), lax.axis_size(FAR)
    own = width // (near * far)
    flat_latent = latent.reshape(tokens, width)
    flat_grad = out_grad.reshape(tokens, width)
    features = jax.nn.silu(time_features(t_index, w_mod.shape[1])).astype(BF)
    feature_rows = jnp.broadcast_to(features[None, :], (8, features.shape[0]))

    def packed(parts):
        return ((parts, 2, tokens * tiles // parts, LANES), BF)

    slot = ((1, 2, tokens * tiles // n_row, LANES), BF)
    place = lax.axis_index(ROW).astype(jnp.int32)[None]
    far_place = lax.axis_index(FAR).astype(jnp.int32)[None]
    data_own, data_wide, *slots, both, pre_act, modulation, cot = call(
        pre_kernel,
        "norm_project",
        [
            packed(1),
            packed(n_col),
            slot,
            slot,
            slot,
            slot,
            ((2, tokens, width), BF),
            ((tokens, inner), F32),
            ((8, 2 * width), F32),
            ((tokens, inner), BF),
        ],
        [((tokens * tiles, LANES), F32)],
        VMEM_ALL,
        7e9,
        (flat_latent, flat_grad, w_in, w_out, w_mod, feature_rows, place),
        smem=(6,),
        late=(1, 2, 3),
        early=tuple(range(10)),
    )
    data_wide = exchange(data_wide, COL)
    slots = [permute(value, ROW, k) for k, value in enumerate(slots)]
    both_near = lax.all_gather(both, NEAR, axis=0, tiled=False)
    vectors = jnp.stack([dt_bias, d_skip])
    params = (
        w_select,
        w_dt.T,
        vectors,
        a_log.T,
    )
    area = rows * cols

    def time_row(at, line, place):
        return at * area + line

    def wide_row(at, line, place):
        chunk = frames // n_col * area
        return (
            lax.div(at, cols) * chunk
            + lax.rem(at, cols)
            + lax.div(line, rows) * area
            + lax.rem(line, rows) * cols
        )

    def tall_row(at, line, place):
        chunk = frames // n_row * area
        return (
            (lax.div(at, rows) ^ place) * chunk
            + lax.rem(at, rows) * cols
            + lax.div(line, cols) * area
            + lax.rem(line, cols)
        )

    out_tall, grads_tall = direction(
        "scan_height", rows * n_row, tall_row, row_order, place, slots, params
    )
    out_slots = [permute(value, ROW, k) for k, value in enumerate(out_tall)]
    data_wide, _ = lax.optimization_barrier((data_wide, out_tall))
    (out_wide,), grads_wide = direction(
        "scan_width", cols * n_col, wide_row, col_order, place, [data_wide], params
    )
    data_time, out_slots, _ = lax.optimization_barrier((data_own, out_slots, out_wide))
    out_wide = exchange(out_wide, COL)
    (out_time,), grads_time = direction(
        "scan_time", frames, time_row, frame_order, place, [data_time], params
    )
    mixed, grad_act, near_send = call(
        post_kernel,
        "sum_directions",
        [
            ((tokens, inner), BF),
            ((tokens, inner), BF),
            ((near, 2 * inner // near, LANES), BF),
        ],
        [
            ((tokens * tiles, LANES), F32),
            ((2, inner, LANES), F32),
            ((inner, LANES), F32),
        ],
        VMEM_ALL,
        6e9,
        (place, grads_time[0], cot, out_time, out_wide, *out_slots, pre_act, vectors),
        smem=(0,),
        early=(0, 1),
    )
    near_recv = exchange(near_send, NEAR)
    data_own, _ = lax.optimization_barrier((data_own, near_send))
    small_send = call(
        small_kernel,
        "small_sums",
        [((near * far, 2 * own, LANES), BF)],
        [
            ((tokens * tiles, LANES), F32),
            ((2, inner, LANES), F32),
            ((2 * inner, LANES), F32),
        ],
        VMEM_ALL,
        3e9,
        (data_own, *grads_time, *grads_wide, *grads_tall),
    )[0]
    branch, latent_grad, vec = call(
        finish_kernel,
        "out_projections",
        [((tokens, width), BF), ((tokens, width), BF), ((near * far, LANES), F32)],
        [],
        VMEM_ALL,
        6e9,
        (mixed, grad_act, flat_latent, modulation, w_in, w_out),
        late=(4, 5),
    )
    near_recv, vec, small_send = lax.optimization_barrier((near_recv, vec, small_send))
    piece = own * tiles
    all_send = call(
        in_grad_kernel,
        "in_weight_grad",
        [((near * far, SLOT + 2 * own, LANES), BF)],
        [((inner // near, near * tokens), BF), ((near * far * SLOT, LANES), F32)],
        VMEM_ALL,
        3e9,
        (near_recv, both_near, small_send, vec),
        late=(1,),
        pieces={1: PIECES},
        choose={1: 0},
    )[0]
    all_recv = exchange(all_send, FAR + NEAR)
    far_send = call(
        out_grad_kernel,
        "out_weight_grad",
        [((piece, LANES), BF)] * far,
        [
            ((inner // near, near * tokens), BF),
            ((far, piece, LANES), F32),
            ((inner // near, LANES), F32),
        ],
        VMEM_ALL,
        4e9,
        (far_place, near_recv, both_near),
        smem=(0,),
        late=(2,),
        pieces={2: PIECES},
        choose={2: 1},
    )
    far_recv = [permute(value, FAR, k) for k, value in enumerate(far_send)]
    rank = w_dt.shape[1]
    grad_w_out, grad_w_in, grad_select, grad_dt, grad_alog, grad_vec, grad_mod = plain_call(
        last_kernel,
        "weight_sums",
        [
            ((own, width), F32),
            ((own, width), F32),
            ((own, LANES), F32),
            ((own, rank), F32),
            ((own, states), F32),
            ((8, own), F32),
            ((2 * own, features.shape[0]), F32),
        ],
        [((piece, LANES), F32), ((SLOT + 2 * own, LANES), F32)],
        16,
        1e9,
        (all_recv, feature_rows, *far_recv),
    )
    return (
        branch.reshape(latent.shape),
        latent_grad.reshape(latent.shape),
        grad_w_in,
        grad_w_out,
        grad_select,
        grad_dt,
        grad_vec[0],
        grad_alog,
        grad_vec[1],
        grad_mod,
    )


def solution(mesh):
    n_row, n_col = mesh.shape["row"], mesh.shape["col"]
    split = Mesh(mesh.devices.reshape(n_row // 2, 2, 2, 4, n_col // 8), AXES)
    tokens = P(None, ROW, COL, None)
    matrix = P(ROW + COL, None)
    vector = P(ROW + COL)
    return jax.shard_map(
        local,
        mesh=split,
        in_specs=(tokens, tokens) + (P(),) * 12,
        out_specs=(
            tokens,
            tokens,
            matrix,
            matrix,
            matrix,
            matrix,
            vector,
            matrix,
            vector,
            matrix,
        ),
        check_vma=False,
    )
```

```python
import functools
import math

import jax
import jax.numpy as jnp
from jax import lax
from jax.experimental import pallas as pl
from jax.experimental.pallas import tpu as pltpu
from jax.sharding import Mesh
from jax.sharding import PartitionSpec as P

BF = jnp.bfloat16
F32 = jnp.float32
LANES = 128
GROUP = 6
EIGHT = 9
LOG2E = math.log2(math.e)
MEGA = 1024 * 1024
VMEM_ALL = 63
PIECES = 4
SLOT = 16
AXES = ("xl", "core", "xh", "y", "z")
ROW = ("xl", "core")
COL = ("xh", "y", "z")
NEAR = ("y", "z")
FAR = ("xl", "core", "xh")
FAR_SIZE = 8
NT = (((1,), (1,)), ((), ()))
TN = (((0,), (0,)), ((), ()))


def time_features(step_index, width):
    halfway = width // 2
    frequency = jnp.exp(-math.log(10000.0) * jnp.arange(halfway, dtype=jnp.float32) / halfway)
    angles = step_index.astype(jnp.float32)[0] * frequency
    return jnp.concatenate([jnp.cos(angles), jnp.sin(angles)])


def total(terms):
    return functools.reduce(lambda a, b: a + b, terms)


def call(kernel, name, out_shape, scratch, vmem, flops, args, smem=(), late=(), pieces=None, choose=None, early=()):
    moved = [i for i in range(len(args)) if i not in smem]
    pieces, choose = pieces or {}, choose or {}
    held_shape = {
        i: args[i].shape[:1] + args[i].shape[2:] if i in choose else args[i].shape for i in moved
    }
    cuts = []
    for i in moved:
        size = args[i].shape[0] // pieces.get(i, 1)
        cuts += [(i, n, pl.ds(n * size, size)) for n in range(pieces.get(i, 1))]

    def body(*refs):
        given, out = refs[: len(args)], refs[len(args) : len(args) + len(out_shape)]
        rest = refs[len(args) + len(out_shape) :]
        held, rest = rest[: len(moved)], rest[len(moved) :]
        made, rest = rest[: len(out_shape)], rest[len(out_shape) :]
        in_sem, out_sem = rest[-2:]
        views = [given[i] if i in smem else held[moved.index(i)] for i in range(len(args))]
        copies = {
            (i, n): pltpu.make_async_copy(
                given[i].at[at, choose[i]] if i in choose else given[i].at[at],
                views[i].at[at],
                in_sem.at[place],
            )
            for place, (i, n, at) in enumerate(cuts)
        }
        for copy in copies.values():
            copy.start()
        for (i, _), copy in copies.items():
            if i not in late:
                copy.wait()
        waits = (lambda i, n=0: copies[i, n].wait(),) if late else ()
        sent = []

        def send(n, plane=None):
            at = (slice(None), plane) if plane is not None else (slice(None),)
            place = 2 * n + (plane or 0)
            copy = pltpu.make_async_copy(made[n].at[at], out[n].at[at], out_sem.at[place])
            copy.start()
            sent.append(copy)

        kernel(*waits, *((send,) if early else ()), *views, *made, *rest[:-2])
        for n in range(len(out_shape)):
            if n not in early:
                send(n)
        for copy in sent:
            copy.wait()

    spaces = [
        pl.BlockSpec(memory_space=pltpu.SMEM if i in smem else pltpu.HBM) for i in range(len(args))
    ]
    return pl.pallas_call(
        body,
        out_shape=tuple(jax.ShapeDtypeStruct(s, d) for s, d in out_shape),
        in_specs=spaces,
        out_specs=(pl.BlockSpec(memory_space=pltpu.HBM),) * len(out_shape),
        scratch_shapes=[pltpu.VMEM(held_shape[i], args[i].dtype) for i in moved]
        + [pltpu.VMEM(s, d) for s, d in out_shape]
        + [pltpu.VMEM(s, d) for s, d in scratch]
        + [pltpu.SemaphoreType.DMA((len(cuts),)), pltpu.SemaphoreType.DMA((2 * len(out_shape),))],
        compiler_params=pltpu.CompilerParams(vmem_limit_bytes=vmem * MEGA),
        cost_estimate=cost(flops, args),
        name=name,
    )(*args)


def cost(flops, args):
    return pl.CostEstimate(
        flops=int(flops),
        bytes_accessed=sum(a.size * a.dtype.itemsize for a in args),
        transcendentals=0,
    )


def plain_call(kernel, name, out_shape, scratch, vmem, flops, args, smem=()):
    spaces = [
        pl.BlockSpec(memory_space=pltpu.SMEM if i in smem else pltpu.VMEM) for i in range(len(args))
    ]
    return pl.pallas_call(
        kernel,
        out_shape=tuple(jax.ShapeDtypeStruct(s, d) for s, d in out_shape),
        in_specs=spaces,
        out_specs=(pl.BlockSpec(memory_space=pltpu.VMEM),) * len(out_shape),
        scratch_shapes=[pltpu.VMEM(s, d) for s, d in scratch],
        compiler_params=pltpu.CompilerParams(vmem_limit_bytes=vmem * MEGA),
        cost_estimate=cost(flops, args),
        name=name,
    )(*args)


def cut(j):
    return slice(LANES * j, LANES * j + LANES)


def to_flat(ref, j, value, tiles):
    ref[pl.ds(j, value.shape[0], stride=tiles), :] = value


def from_flat(ref, j, tokens, tiles):
    return ref[pl.ds(j, tokens, stride=tiles), :]


def normalise(latent):
    wide = latent.astype(F32)
    inverse = lax.rsqrt(jnp.mean(wide * wide, axis=-1, keepdims=True) + 1e-06)
    return wide * inverse, inverse


def pre_kernel(
    wait,
    send,
    latent_ref,
    grad_ref,
    w_in_ref,
    w_out_ref,
    w_mod_ref,
    feature_ref,
    place_ref,
    own_ref,
    wide_ref,
    slot_0_ref,
    slot_1_ref,
    slot_2_ref,
    slot_3_ref,
    both_ref,
    pre_ref,
    mod_ref,
    cot_ref,
    rows_ref,
    flat_ref,
):
    tokens, width = rows_ref.shape
    tiles = w_in_ref.shape[1] // LANES
    modulation = lax.dot_general(
        feature_ref[...], w_mod_ref[...], NT, preferred_element_type=F32
    )
    mod_ref[...] = modulation
    send(8)
    latent = latent_ref[...].astype(F32).reshape(tokens, width)
    rows_ref[...] = latent.astype(BF)
    send(10)
    normed, _ = normalise(latent)
    shifted = (normed * (1.0 + modulation[:1, width:]) + modulation[:1, :width]).astype(BF)
    both_ref[0] = shifted
    wait(1)
    both_ref[1] = grad_ref[...].astype(F32).reshape(tokens, width).astype(BF)
    send(6)
    wait(2)
    pre_act = jnp.dot(shifted, w_in_ref[...], preferred_element_type=F32)
    pre_ref[...] = pre_act
    send(7)
    activ = (pre_act * jax.nn.sigmoid(pre_act)).astype(BF)

    def pack(which, value):
        wide = value.astype(F32)
        for j in range(tiles):
            to_flat(flat_ref, j, wide[:, cut(j)], tiles)
        flat = flat_ref[...].astype(BF)
        own_ref[0, which] = flat
        wide_ref[:, which] = flat.reshape(wide_ref.shape[0], wide_ref.shape[2], LANES)
        for k, ref in enumerate((slot_0_ref, slot_1_ref, slot_2_ref, slot_3_ref)):
            chunk = ref.shape[2]
            begin = pl.multiple_of((place_ref[0] ^ k) * chunk, chunk)
            ref[0, which] = flat_ref[pl.ds(begin, chunk), :].astype(BF)
        for n in range(6):
            send(n, which)

    pack(0, activ)
    wait(3)
    cot = lax.dot_general(both_ref[1], w_out_ref[...], NT, preferred_element_type=F32).astype(BF)
    cot_ref[...] = cot
    send(9)
    pack(1, cot)


def parts_of(refs):
    begin, found = 0, []
    for ref in refs:
        size = ref.shape[0] * ref.shape[2]
        found.append((ref, slice(begin, begin + size)))
        begin += size
    return found


def read_part(ref, which):
    return ref[:, which].reshape(ref.shape[0] * ref.shape[2], LANES).astype(F32)


def write_part(ref, which, value):
    ref[:, which] = value.astype(BF).reshape(ref.shape[0], ref.shape[2], LANES)


def scan_kernel(
    length,
    row_of,
    pieces,
    wait,
    send,
    order_ref,
    place_ref,
    *refs,
):
    data_refs, out_refs = refs[:pieces], refs[pieces + 4 : 2 * pieces + 4]
    scan_steps(
        length,
        row_of,
        order_ref,
        place_ref,
        data_refs,
        *refs[pieces : pieces + 4],
        out_refs,
        *refs[2 * pieces + 4 :],
        functools.partial(wait_for, wait, 2 + pieces),
        functools.partial(send_from, send, pieces),
    )


def wait_for(wait, first, n):
    wait(first + n)


def send_from(send, pieces, n):
    if n < 2:
        for k in range(pieces):
            send(k, n)
    else:
        send(pieces + n - 2)


def scan_steps(
    length,
    row_of,
    order_ref,
    place_ref,
    data_refs,
    wsel_ref,
    wdt_ref,
    bias_ref,
    alog_ref,
    out_refs,
    x_ref,
    grad_pre_ref,
    low_ref,
    grad_low_ref,
    gvec_ref,
    pre_ref,
    dt_ref,
    xf_ref,
    x_row_ref,
    dt_row_ref,
    dx_row_ref,
    dy_row_ref,
    bb_ref,
    cb_ref,
    gb_ref,
    gc_ref,
    hist_ref,
    keep_ref,
    y8_ref,
    u8_ref,
    v8_ref,
    rate2_ref,
    rate_ref,
    wait,
    send,
):
    tokens, inner = xf_ref.shape
    tiles = inner // LANES
    lines = tokens // length
    states = alog_ref.shape[0]
    rank = LANES - 2 * states
    for ref, at in parts_of(data_refs):
        x_row_ref[at, :] = read_part(ref, 0)
        dy_row_ref[at, :] = read_part(ref, 1)
    for j in range(tiles):
        xf_ref[:, cut(j)] = from_flat(x_row_ref, j, tokens, tiles)
    x = xf_ref[...].astype(BF)
    x_ref[...] = x
    send(2)
    wait(0)
    select = jnp.dot(x, wsel_ref[...], preferred_element_type=F32)
    lane = lax.broadcasted_iota(jnp.int32, (tokens, LANES), 1)
    low = jnp.where(lane < rank, select, 0.0).astype(BF)
    low_ref[...] = low
    send(4)
    wait(1)
    w_dt = jnp.concatenate([wdt_ref[...], jnp.zeros((2 * states, inner), BF)], axis=0)
    pre = jnp.dot(low, w_dt, preferred_element_type=F32) + bias_ref[:1, :]
    pre_ref[...] = pre
    spacing = jnp.maximum(pre, 0.0) + jnp.log1p(jnp.exp(-jnp.abs(pre)))
    dt_ref[...] = spacing
    for j in range(tiles):
        at = slice(j * tokens, (j + 1) * tokens)
        dt_row_ref[at, :] = spacing[:, cut(j)]
        dx_row_ref[at, :] = spacing[:, cut(j)] * xf_ref[:, cut(j)]
    rates = -jnp.exp(alog_ref[...])
    rate_ref[...] = rates
    rate2_ref[...] = rates * LOG2E
    turned = select.T
    for token in range(tokens):
        at = pl.ds(token * states, states)
        column = slice(token, token + 1)
        bb_ref[at, :] = jnp.broadcast_to(turned[rank : rank + states, column], (states, LANES))
        cb_ref[at, :] = jnp.broadcast_to(turned[rank + states :, column], (states, LANES))
    gb_ref[...] = jnp.zeros_like(gb_ref)
    gc_ref[...] = jnp.zeros_like(gc_ref)
    zero = jnp.zeros((states, LANES), F32)
    hist_ref[pl.ds(0, states), :] = jnp.zeros((states, GROUP * LANES), F32)
    unroll = min(length, 8)

    def fold(value):
        return value[:8] + value[8:]

    for group in range(tiles // GROUP):
        first = group * GROUP
        cuts = [cut(first + j) for j in range(GROUP)]
        rate2 = [rate2_ref[:, c] for c in cuts]
        rate1 = [rate_ref[:, c] for c in cuts]

        def one_line(line, grads):
            def places(step):
                row = row_of(order_ref[step], line, place_ref[0])
                at = pl.ds(pl.multiple_of(row * states, states), states)
                slot = pl.ds(pl.multiple_of((step + 1) * states, states), states)
                return row, row * EIGHT, at, slot

            def forward(step, carry):
                row, at_8, at, slot = places(step)
                bb, cb = bb_ref[at, :], cb_ref[at, :]
                new = []
                for j in range(GROUP):
                    dt = dt_row_ref[pl.ds(row + (first + j) * tokens, 1), :]
                    dx = dx_row_ref[pl.ds(row + (first + j) * tokens, 1), :]
                    decay = jnp.exp2(rate2[j] * dt)
                    keep_ref[slot, cut(j)] = decay
                    h = decay * carry[j] + bb * dx
                    hist_ref[slot, cut(j)] = h
                    y8_ref[pl.ds(at_8 + EIGHT * tokens * j, 8), :] = fold(h * cb)
                    new.append(h)
                return tuple(new)

            lax.fori_loop(0, length, forward, (zero,) * GROUP, unroll=unroll)

            def backward(back_step, carry):
                step = length - 1 - back_step
                row, at_8, at, slot = places(step)
                prev = pl.ds(pl.multiple_of(step * states, states), states)
                bb, cb = bb_ref[at, :], cb_ref[at, :]
                pend, acc = carry
                gb = gb_ref[at, :]
                gc = gc_ref[at, :]
                new, acc_new = [], []
                for j in range(GROUP):
                    dt = dt_row_ref[pl.ds(row + (first + j) * tokens, 1), :]
                    dx = dx_row_ref[pl.ds(row + (first + j) * tokens, 1), :]
                    dy = dy_row_ref[pl.ds(row * tiles + first + j, 1), :]
                    g = pend[j] + cb * dy
                    gc = gc + hist_ref[slot, cut(j)] * dy
                    u8_ref[pl.ds(at_8 + EIGHT * tokens * j, 8), :] = fold(g * bb)
                    gb = gb + g * dx
                    p = keep_ref[slot, cut(j)] * g
                    w = p * hist_ref[prev, cut(j)]
                    v8_ref[pl.ds(at_8 + EIGHT * tokens * j, 8), :] = fold(w * rate1[j])
                    acc_new.append(acc[j] + w * dt)
                    new.append(p)
                gb_ref[at, :] = gb
                gc_ref[at, :] = gc
                return tuple(new), tuple(acc_new)

            start = ((zero,) * GROUP, grads)
            return lax.fori_loop(0, length, backward, start, unroll=unroll)[1]

        grads = lax.fori_loop(0, lines, one_line, (zero,) * GROUP)
        for j in range(GROUP):
            gvec_ref[:states, cuts[j]] = grads[j] * rate1[j]

        def gather(block, carry):
            rows = pl.ds(pl.multiple_of(block * 8, 8), 8)

            def summed(ref, j):
                begin = block * (8 * EIGHT) + EIGHT * tokens * j
                return total([ref[pl.ds(begin + r, 8, stride=EIGHT), :] for r in range(8)])

            for j in range(GROUP):
                c = cuts[j]
                u = summed(u8_ref, j)
                x_row_ref[pl.ds(block * 8 * tiles + first + j, 8, stride=tiles), :] = summed(y8_ref, j)
                grad_spacing = summed(v8_ref, j) + xf_ref[rows, c] * u
                pre_ref[rows, c] = grad_spacing * jax.nn.sigmoid(pre_ref[rows, c])
                dt_ref[rows, c] = dt_ref[rows, c] * u
            return carry

        lax.fori_loop(0, tokens // 8, gather, 0, unroll=2)

    for ref, at in parts_of(out_refs):
        write_part(ref, 0, x_row_ref[at, :])
    send(0)
    grad_pre = pre_ref[...]
    gvec_ref[states:, :] = jnp.broadcast_to(
        jnp.sum(grad_pre, axis=0, keepdims=True), (8, inner)
    )
    send(6)
    grad_pre_b = grad_pre.astype(BF)
    grad_pre_ref[...] = grad_pre_b
    send(3)
    shape = (2 * LANES, LANES)
    half = lax.broadcasted_iota(jnp.int32, shape, 0) // LANES
    lane_at = lax.broadcasted_iota(jnp.int32, shape, 1)
    spread = jnp.where((lane_at - rank) // states == half, 1.0, 0.0).astype(BF)
    shape = (tokens * states, LANES)
    state_at = lax.broadcasted_iota(jnp.int32, shape, 0) % states
    lane_at = lax.broadcasted_iota(jnp.int32, shape, 1)
    both = jnp.concatenate([gb_ref[...], gc_ref[...]], axis=1)
    lanes = halves_product(both, spread, False)
    kept = jnp.where((lane_at >= rank) & ((lane_at - rank) % states == state_at), lanes, 0.0)
    shape = (tokens, tokens * states)
    collect = lax.broadcasted_iota(jnp.int32, shape, 1) // states == lax.broadcasted_iota(
        jnp.int32, shape, 0
    )
    grad_maps = halves_product(kept, jnp.where(collect, 1.0, 0.0).astype(BF), True)
    grad_low = lax.dot_general(grad_pre_b, w_dt, NT, preferred_element_type=F32)
    grad_select_out = (grad_low + grad_maps).astype(BF)
    grad_low_ref[...] = grad_select_out
    send(5)
    back = dt_ref[...] + lax.dot_general(
        grad_select_out, wsel_ref[...], NT, preferred_element_type=F32
    )
    for j in range(tiles):
        to_flat(dy_row_ref, j, back[:, cut(j)], tiles)
    for ref, at in parts_of(out_refs):
        write_part(ref, 1, dy_row_ref[at, :])
    send(1)


def halves_product(value, other, other_first):
    top = value.astype(BF)
    rest = (value - top.astype(F32)).astype(BF)
    if other_first:
        return jnp.dot(other, top, preferred_element_type=F32) + jnp.dot(
            other, rest, preferred_element_type=F32
        )
    return jnp.dot(top, other, preferred_element_type=F32) + jnp.dot(
        rest, other, preferred_element_type=F32
    )


def direction(name, length, row_of, order, place, data, params):
    inner = params[0].shape[0]
    tiles = inner // LANES
    tokens = sum(d.shape[0] * d.shape[2] for d in data) // tiles
    states = params[3].shape[0]
    plane = ((tokens, inner), F32)
    flat = ((tokens * tiles, LANES), F32)
    maps = ((tokens * states, LANES), F32)
    eights = ((tokens * EIGHT * GROUP, LANES), F32)
    results = call(
        functools.partial(scan_kernel, length, row_of, len(data)),
        name,
        [(d.shape, BF) for d in data]
        + [((tokens, inner), BF)] * 2
        + [((tokens, LANES), BF)] * 2
        + [((states + 8, inner), F32)],
        [plane] * 3
        + [flat] * 4
        + [maps] * 4
        + [(((length + 1) * states, GROUP * LANES), F32)] * 2
        + [eights] * 3
        + [((states, inner), F32)] * 2,
        VMEM_ALL,
        2e10,
        (order, place, *data, *params),
        smem=(0, 1),
        late=tuple(2 + len(data) + i for i in (0, 1)),
        early=tuple(range(len(data) + 5)),
    )
    return results[: len(data)], results[len(data) :]


def small_kernel(own_ref, *refs):
    found, refs = [refs[5 * d : 5 * d + 5] for d in range(3)], refs[15:]
    send_ref, row_ref, turned_ref, held_ref = refs
    inner = found[0][0].shape[1]
    tiles = inner // LANES
    tokens = own_ref.shape[2] // tiles
    own = inner // send_ref.shape[0]
    states = found[0][4].shape[0] - 8
    rank = LANES - 2 * states
    row_ref[...] = own_ref[0, 0].astype(F32) * own_ref[0, 1].astype(F32)
    skips = jnp.concatenate(
        [
            jnp.sum(from_flat(row_ref, j, tokens, tiles), axis=0, keepdims=True)
            for j in range(tiles)
        ],
        axis=1,
    )
    x, grad_pre, low, grad_low = [
        jnp.concatenate([d[i][...] for d in found], axis=0) for i in range(4)
    ]
    summed = total([d[4][...] for d in found])
    at = lax.broadcasted_iota(jnp.int32, (LANES, inner), 0)
    vectors = jnp.concatenate(
        [jnp.zeros((rank, inner), F32), summed, jnp.zeros((states - 8, inner), F32)], axis=0
    )
    vectors = jnp.where(at > rank + states, 0.0, vectors) + jnp.where(
        at == rank + states + 1, jnp.broadcast_to(skips, at.shape), 0.0
    )
    turned_ref[0] = lax.dot_general(x, grad_low, TN, preferred_element_type=F32)
    turned_ref[1] = vectors.T + lax.dot_general(
        grad_pre, low, TN, preferred_element_type=F32
    )
    for d in range(send_ref.shape[0]):
        for which in (0, 1):
            begin = (2 * d + which) * own
            held_ref[begin : begin + own, :] = turned_ref[which, d * own : (d + 1) * own, :]
    send_ref[...] = held_ref[...].reshape(send_ref.shape).astype(BF)


def spread_rows(ref, which, own, near, held_ref):
    for m in range(near):
        for o in range(FAR_SIZE):
            begin = (o * near + m) * own
            at = (m * FAR_SIZE + o) * own
            held_ref[at : at + own, :] = ref[which, begin : begin + own, :]
    return held_ref[...].reshape(near, FAR_SIZE * own, LANES).astype(BF)


def post_kernel(
    send,
    place_ref,
    activ_ref,
    cot_ref,
    time_ref,
    wide_ref,
    slot_0_ref,
    slot_1_ref,
    slot_2_ref,
    slot_3_ref,
    pre_ref,
    skip_ref,
    mixed_out_ref,
    grad_act_ref,
    send_ref,
    sum_ref,
    turned_ref,
    held_ref,
):
    tokens, inner = pre_ref.shape
    tiles = inner // LANES
    flat_shape = (tokens * tiles, LANES)
    near = send_ref.shape[0]
    near_rows = inner // near
    own = near_rows // FAR_SIZE

    def summed(which, own_ref):
        sum_ref[...] = time_ref[0, which].astype(F32) + wide_ref[:, which].reshape(
            flat_shape
        ).astype(F32)
        for k, ref in enumerate((slot_0_ref, slot_1_ref, slot_2_ref, slot_3_ref)):
            chunk = ref.shape[2]
            at = pl.ds(pl.multiple_of((place_ref[0] ^ k) * chunk, chunk), chunk)
            sum_ref[at, :] += ref[0, which].astype(F32)
        scans = jnp.concatenate([from_flat(sum_ref, j, tokens, tiles) for j in range(tiles)], axis=1)
        return scans + skip_ref[1:, :] * own_ref[...].astype(F32)

    back = summed(1, cot_ref)
    pre_act = pre_ref[...]
    gate = jax.nn.sigmoid(pre_act)
    grad_act = (back * gate * (1.0 + pre_act * (1.0 - gate))).astype(BF)
    grad_act_ref[...] = grad_act
    send(1)
    turned_ref[1] = grad_act.astype(F32).T
    mixed = summed(0, activ_ref).astype(BF)
    mixed_out_ref[...] = mixed
    send(0)
    turned_ref[0] = mixed.astype(F32).T
    send_ref[:, :near_rows] = spread_rows(turned_ref, 0, own, near, held_ref)
    for m in range(near):
        send_ref[m, near_rows:] = turned_ref[1, pl.ds(m * near_rows, near_rows), :].astype(BF)


def finish_kernel(
    wait,
    mixed_ref,
    grad_act_ref,
    latent_ref,
    mod_ref,
    w_in_ref,
    w_out_ref,
    branch_ref,
    latent_grad_ref,
    vec_ref,
):
    tokens, width = latent_ref.shape
    normed, inverse = normalise(latent_ref[...])
    wait(4)
    grad_shifted = lax.dot_general(
        grad_act_ref[...], w_in_ref[...], NT, preferred_element_type=F32
    )
    grad_vec = jnp.concatenate(
        [
            jnp.sum(grad_shifted, axis=0, keepdims=True),
            jnp.sum(grad_shifted * normed, axis=0, keepdims=True),
        ],
        axis=1,
    )
    devices = vec_ref.shape[0]
    part = 2 * width // devices
    shape = (devices, 2 * width)
    block_at = lax.broadcasted_iota(jnp.int32, shape, 0) * part
    column_at = lax.broadcasted_iota(jnp.int32, shape, 1)
    mine = (column_at >= block_at) & (column_at < block_at + part)
    chosen = jnp.where(mine, jnp.broadcast_to(grad_vec, shape), 0.0)
    lane_at = lax.broadcasted_iota(jnp.int32, (2 * width, LANES), 1)
    place = lax.broadcasted_iota(jnp.int32, (2 * width, LANES), 0) % part
    choose = jnp.where(lane_at == place, 1.0, 0.0).astype(BF)
    vec_ref[...] = halves_product(chosen, choose, False)
    grad_normed = grad_shifted * (1.0 + mod_ref[:1, width:])
    product = jnp.mean(grad_normed * normed, axis=1, keepdims=True)
    latent_grad_ref[...] = (inverse * (grad_normed - normed * product)).astype(BF)
    wait(5)
    branch_ref[...] = jnp.dot(
        mixed_ref[...], w_out_ref[...], preferred_element_type=F32
    ).astype(BF)


def long_product(wait, at, left, right_ref):
    size = right_ref.shape[0] // PIECES
    tokens, width = right_ref.shape[1:]
    terms = []
    for n in range(PIECES):
        wait(at, n)
        rows = slice(n * size * tokens, (n + 1) * size * tokens)
        right = right_ref[n * size : (n + 1) * size].reshape(size * tokens, width)
        terms.append(jnp.dot(left[:, rows], right, preferred_element_type=F32))
    return total(terms)


def in_grad_kernel(wait, recv_ref, both_ref, small_ref, vec_ref, all_ref, right_ref, rows_ref):
    near = recv_ref.shape[0]
    rows = right_ref.shape[0]
    width = both_ref.shape[2]
    devices = all_ref.shape[0]
    own = rows // FAR_SIZE
    for s in range(near):
        right_ref[:, cut(s)] = recv_ref[s, rows:]
    all_ref[:, SLOT:] = small_ref[...]
    product = long_product(wait, 1, right_ref, both_ref)
    turned = jnp.concatenate([product, jnp.zeros((LANES - rows, width), F32)], axis=0).T
    for d in range(devices):
        rows_ref[d * SLOT : d * SLOT + own, :] = turned[d * own : (d + 1) * own]
    for n in range(own, SLOT):
        rows_ref[pl.ds(n, devices, stride=SLOT), :] = vec_ref[...]
    all_ref[:, :SLOT] = rows_ref[...].reshape(devices, SLOT, LANES).astype(BF)


def pair_place(place, core_flip, slot):
    return place ^ ((slot // 2) * 4 + core_flip * 2 + slot % 2)


def out_grad_kernel(
    wait, place_ref, recv_ref, both_ref, mine_ref, other_ref, left_ref, out_ref, half_ref
):
    near = recv_ref.shape[0]
    rows = left_ref.shape[0]
    far = FAR_SIZE
    tiles = both_ref.shape[2] // LANES
    own = rows // far
    for s in range(near):
        left_ref[:, cut(s)] = recv_ref[s, :rows]
    product = long_product(wait, 2, left_ref, both_ref)
    for j in range(tiles):
        half_ref[...] = product[:, cut(j)]
        for o in range(far):
            out_ref[o, pl.ds(j, own, stride=tiles), :] = half_ref[o * own : (o + 1) * own, :]
    for slot in range(far // 2):
        mine_ref[slot] = out_ref[pair_place(place_ref[0], 0, slot)]
        other_ref[slot] = out_ref[pair_place(place_ref[0], 1, slot)].astype(BF)


def pair_sum_kernel(mine_ref, other_ref, kept_ref, *slot_refs):
    kept_ref[...] = mine_ref[0] + other_ref[0].astype(F32)
    for slot, ref in enumerate(slot_refs, 1):
        ref[...] = (mine_ref[slot] + other_ref[slot].astype(F32)).astype(BF)


def last_kernel(all_ref, feature_ref, *refs):
    far_refs = refs[: FAR_SIZE // 2]
    gwo_ref, gwi_ref, gsel_ref, gdt_ref, galog_ref, gvec_ref, gmod_ref, sum_ref, rest_ref = refs[
        FAR_SIZE // 2 :
    ]
    far = FAR_SIZE
    own, width = gwo_ref.shape
    tiles = width // LANES
    near = all_ref.shape[0] // far
    part = width // near
    sum_ref[...] = total([ref[...].astype(F32) for ref in far_refs])
    for j in range(tiles):
        gwo_ref[:, cut(j)] = sum_ref[pl.ds(j, own, stride=tiles), :]
    rest = []
    for m in range(near):
        block = total([all_ref[o * near + m].astype(F32) for o in range(far)])
        gwi_ref[:, part * m : part * (m + 1)] = block[:own, :part]
        rest.append(block)
    rest_ref[...] = total(rest)
    vec = rest_ref[own : own + 1, :]
    turned = jnp.broadcast_to(vec, (LANES, LANES)).T
    gmod_ref[...] = turned[: 2 * own, :1] * feature_ref[:1, :].astype(F32)
    gsel_ref[...] = rest_ref[SLOT : SLOT + own, :]
    rank, states = gdt_ref.shape[1], galog_ref.shape[1]
    base = SLOT + own
    gdt_ref[...] = rest_ref[base : base + own, :rank]
    galog_ref[...] = rest_ref[base : base + own, rank : rank + states]
    turned = jnp.concatenate([rest_ref[base : base + own, :], jnp.zeros((LANES - own, LANES), F32)])
    gvec_ref[...] = turned.T[rank + states : rank + states + 8, :own]


def permute(value, axes, k):
    if k == 0:
        return value
    return lax.ppermute(value, axes, [(i, i ^ k) for i in range(lax.axis_size(axes))])


def exchange(value, axes):
    return lax.all_to_all(value, axes, split_axis=0, concat_axis=0, tiled=True)


def local(
    latent,
    out_grad,
    w_in,
    w_out,
    w_select,
    w_dt,
    dt_bias,
    a_log,
    d_skip,
    w_mod,
    t_index,
    frame_order,
    row_order,
    col_order,
):
    frames, rows, cols, width = latent.shape
    inner = w_in.shape[1]
    tokens = frames * rows * cols
    tiles = inner // LANES
    states = a_log.shape[1]
    n_row, n_col = lax.axis_size(ROW), lax.axis_size(COL)
    near, far = lax.axis_size(NEAR), lax.axis_size(FAR)
    own = width // (near * far)
    features = jax.nn.silu(time_features(t_index, w_mod.shape[1])).astype(BF)
    feature_rows = jnp.broadcast_to(features[None, :], (8, features.shape[0]))

    def packed(parts):
        return ((parts, 2, tokens * tiles // parts, LANES), BF)

    slot = ((1, 2, tokens * tiles // n_row, LANES), BF)
    place = lax.axis_index(ROW).astype(jnp.int32)[None]
    far_place = lax.axis_index(FAR).astype(jnp.int32)[None]
    data_own, data_wide, *slots, both, pre_act, modulation, cot, flat_latent = call(
        pre_kernel,
        "norm_project",
        [
            packed(1),
            packed(n_col),
            slot,
            slot,
            slot,
            slot,
            ((2, tokens, width), BF),
            ((tokens, inner), F32),
            ((8, 2 * width), F32),
            ((tokens, inner), BF),
            ((tokens, width), BF),
        ],
        [((tokens * tiles, LANES), F32)],
        VMEM_ALL,
        7e9,
        (latent, out_grad, w_in, w_out, w_mod, feature_rows, place),
        smem=(6,),
        late=(1, 2, 3),
        early=tuple(range(11)),
    )
    data_wide = exchange(data_wide, COL)
    slots = [permute(value, ROW, k) for k, value in enumerate(slots)]
    both_near = lax.all_gather(both, NEAR, axis=0, tiled=False)
    vectors = jnp.stack([dt_bias, d_skip])
    params = (
        w_select,
        w_dt.T,
        vectors,
        a_log.T,
    )
    area = rows * cols

    def time_row(at, line, place):
        return at * area + line

    def wide_row(at, line, place):
        chunk = frames // n_col * area
        return (
            lax.div(at, cols) * chunk
            + lax.rem(at, cols)
            + lax.div(line, rows) * area
            + lax.rem(line, rows) * cols
        )

    def tall_row(at, line, place):
        chunk = frames // n_row * area
        return (
            (lax.div(at, rows) ^ place) * chunk
            + lax.rem(at, rows) * cols
            + lax.div(line, cols) * area
            + lax.rem(line, cols)
        )

    out_tall, grads_tall = direction(
        "scan_height", rows * n_row, tall_row, row_order, place, slots, params
    )
    out_slots = [permute(value, ROW, k) for k, value in enumerate(out_tall)]
    data_wide, _ = lax.optimization_barrier((data_wide, out_tall))
    (out_wide,), grads_wide = direction(
        "scan_width", cols * n_col, wide_row, col_order, place, [data_wide], params
    )
    data_time, out_slots, _ = lax.optimization_barrier((data_own, out_slots, out_wide))
    out_wide = exchange(out_wide, COL)
    (out_time,), grads_time = direction(
        "scan_time", frames, time_row, frame_order, place, [data_time], params
    )
    mixed, grad_act, near_send = call(
        post_kernel,
        "sum_directions",
        [
            ((tokens, inner), BF),
            ((tokens, inner), BF),
            ((near, 2 * inner // near, LANES), BF),
        ],
        [
            ((tokens * tiles, LANES), F32),
            ((2, inner, LANES), F32),
            ((inner, LANES), F32),
        ],
        VMEM_ALL,
        6e9,
        (place, grads_time[0], cot, out_time, out_wide, *out_slots, pre_act, vectors),
        smem=(0,),
        early=(0, 1),
    )
    near_recv = exchange(near_send, NEAR)
    data_own, _ = lax.optimization_barrier((data_own, near_send))
    small_send = call(
        small_kernel,
        "small_sums",
        [((near * far, 2 * own, LANES), BF)],
        [
            ((tokens * tiles, LANES), F32),
            ((2, inner, LANES), F32),
            ((2 * inner, LANES), F32),
        ],
        VMEM_ALL,
        3e9,
        (data_own, *grads_time, *grads_wide, *grads_tall),
    )[0]
    branch, latent_grad, vec = call(
        finish_kernel,
        "out_projections",
        [((tokens, width), BF), ((tokens, width), BF), ((near * far, LANES), F32)],
        [],
        VMEM_ALL,
        6e9,
        (mixed, grad_act, flat_latent, modulation, w_in, w_out),
        late=(4, 5),
    )
    near_recv, vec, small_send = lax.optimization_barrier((near_recv, vec, small_send))
    piece = own * tiles
    all_send = call(
        in_grad_kernel,
        "in_weight_grad",
        [((near * far, SLOT + 2 * own, LANES), BF)],
        [((inner // near, near * tokens), BF), ((near * far * SLOT, LANES), F32)],
        VMEM_ALL,
        3e9,
        (near_recv, both_near, small_send, vec),
        late=(1,),
        pieces={1: PIECES},
        choose={1: 0},
    )[0]
    all_recv = exchange(all_send, FAR + NEAR)
    mine, other = call(
        out_grad_kernel,
        "out_weight_grad",
        [((far // 2, piece, LANES), F32), ((far // 2, piece, LANES), BF)],
        [
            ((inner // near, near * tokens), BF),
            ((far, piece, LANES), F32),
            ((inner // near, LANES), F32),
        ],
        VMEM_ALL,
        4e9,
        (far_place, near_recv, both_near),
        smem=(0,),
        late=(2,),
        pieces={2: PIECES},
        choose={2: 1},
    )
    other = permute(other, FAR, 2)
    far_send = plain_call(
        pair_sum_kernel,
        "pair_sums",
        [((piece, LANES), F32)] + [((piece, LANES), BF)] * (far // 2 - 1),
        [],
        8,
        1e9,
        (mine, other),
    )
    far_recv = [permute(value, FAR, (0, 1, 4, 5)[slot]) for slot, value in enumerate(far_send)]
    rank = w_dt.shape[1]
    grad_w_out, grad_w_in, grad_select, grad_dt, grad_alog, grad_vec, grad_mod = plain_call(
        last_kernel,
        "weight_sums",
        [
            ((own, width), F32),
            ((own, width), F32),
            ((own, LANES), F32),
            ((own, rank), F32),
            ((own, states), F32),
            ((8, own), F32),
            ((2 * own, features.shape[0]), F32),
        ],
        [((piece, LANES), F32), ((SLOT + 2 * own, LANES), F32)],
        16,
        1e9,
        (all_recv, feature_rows, *far_recv),
    )
    return (
        branch.reshape(latent.shape),
        latent_grad.reshape(latent.shape),
        grad_w_in,
        grad_w_out,
        grad_select,
        grad_dt,
        grad_vec[0],
        grad_alog,
        grad_vec[1],
        grad_mod,
    )


def solution(mesh):
    n_row, n_col = mesh.shape["row"], mesh.shape["col"]
    split = Mesh(mesh.devices.reshape(n_row // 2, 2, 2, 4, n_col // 8), AXES)
    tokens = P(None, ROW, COL, None)
    matrix = P(ROW + COL, None)
    vector = P(ROW + COL)
    return jax.shard_map(
        local,
        mesh=split,
        in_specs=(tokens, tokens) + (P(),) * 12,
        out_specs=(
            tokens,
            tokens,
            matrix,
            matrix,
            matrix,
            matrix,
            vector,
            matrix,
            vector,
            matrix,
        ),
        check_vma=False,
    )
```

```python
import functools
import math

import jax
import jax.numpy as jnp
from jax import lax
from jax.experimental import pallas as pl
from jax.experimental.pallas import tpu as pltpu
from jax.sharding import Mesh
from jax.sharding import PartitionSpec as P

BF = jnp.bfloat16
F32 = jnp.float32
LANES = 128
GROUP = 6
EIGHT = 9
LOG2E = math.log2(math.e)
MEGA = 1024 * 1024
VMEM_ALL = 60
PIECES = 4
SLOT = 16
AXES = ("xl", "core", "xh", "y", "z")
ROW = ("xl", "core")
COL = ("xh", "y", "z")
NEAR = ("y", "z")
FAR = ("xl", "core", "xh")
FAR_SIZE = 8
NT = (((1,), (1,)), ((), ()))
TN = (((0,), (0,)), ((), ()))


def time_features(step_index, width):
    halfway = width // 2
    frequency = jnp.exp(-math.log(10000.0) * jnp.arange(halfway, dtype=jnp.float32) / halfway)
    angles = step_index.astype(jnp.float32)[0] * frequency
    return jnp.concatenate([jnp.cos(angles), jnp.sin(angles)])


def total(terms):
    return functools.reduce(lambda a, b: a + b, terms)


def call(kernel, name, out_shape, scratch, vmem, flops, args, smem=(), late=(), pieces=None, choose=None, early=()):
    moved = [i for i in range(len(args)) if i not in smem]
    pieces, choose = pieces or {}, choose or {}
    held_shape = {
        i: args[i].shape[:1] + args[i].shape[2:] if i in choose else args[i].shape for i in moved
    }
    cuts = []
    for i in moved:
        size = args[i].shape[0] // pieces.get(i, 1)
        cuts += [(i, n, pl.ds(n * size, size)) for n in range(pieces.get(i, 1))]

    def body(*refs):
        given, out = refs[: len(args)], refs[len(args) : len(args) + len(out_shape)]
        rest = refs[len(args) + len(out_shape) :]
        held, rest = rest[: len(moved)], rest[len(moved) :]
        made, rest = rest[: len(out_shape)], rest[len(out_shape) :]
        in_sem, out_sem = rest[-2:]
        views = [given[i] if i in smem else held[moved.index(i)] for i in range(len(args))]
        copies = {
            (i, n): pltpu.make_async_copy(
                given[i].at[at, choose[i]] if i in choose else given[i].at[at],
                views[i].at[at],
                in_sem.at[place],
            )
            for place, (i, n, at) in enumerate(cuts)
        }
        for copy in copies.values():
            copy.start()
        for (i, _), copy in copies.items():
            if i not in late:
                copy.wait()
        waits = (lambda i, n=0: copies[i, n].wait(),) if late else ()
        sent = []

        def send(n, plane=None):
            at = (slice(None), plane) if plane is not None else (slice(None),)
            place = 2 * n + (plane or 0)
            copy = pltpu.make_async_copy(made[n].at[at], out[n].at[at], out_sem.at[place])
            copy.start()
            sent.append(copy)

        kernel(*waits, *((send,) if early else ()), *views, *made, *rest[:-2])
        for n in range(len(out_shape)):
            if n not in early:
                send(n)
        for copy in sent:
            copy.wait()

    spaces = [
        pl.BlockSpec(memory_space=pltpu.SMEM if i in smem else pltpu.HBM) for i in range(len(args))
    ]
    return pl.pallas_call(
        body,
        out_shape=tuple(jax.ShapeDtypeStruct(s, d) for s, d in out_shape),
        in_specs=spaces,
        out_specs=(pl.BlockSpec(memory_space=pltpu.HBM),) * len(out_shape),
        scratch_shapes=[pltpu.VMEM(held_shape[i], args[i].dtype) for i in moved]
        + [pltpu.VMEM(s, d) for s, d in out_shape]
        + [pltpu.VMEM(s, d) for s, d in scratch]
        + [pltpu.SemaphoreType.DMA((len(cuts),)), pltpu.SemaphoreType.DMA((2 * len(out_shape),))],
        compiler_params=pltpu.CompilerParams(vmem_limit_bytes=vmem * MEGA),
        cost_estimate=cost(flops, args),
        name=name,
    )(*args)


def cost(flops, args):
    return pl.CostEstimate(
        flops=int(flops),
        bytes_accessed=sum(a.size * a.dtype.itemsize for a in args),
        transcendentals=0,
    )


def plain_call(kernel, name, out_shape, scratch, vmem, flops, args, smem=()):
    spaces = [
        pl.BlockSpec(memory_space=pltpu.SMEM if i in smem else pltpu.VMEM) for i in range(len(args))
    ]
    return pl.pallas_call(
        kernel,
        out_shape=tuple(jax.ShapeDtypeStruct(s, d) for s, d in out_shape),
        in_specs=spaces,
        out_specs=(pl.BlockSpec(memory_space=pltpu.VMEM),) * len(out_shape),
        scratch_shapes=[pltpu.VMEM(s, d) for s, d in scratch],
        compiler_params=pltpu.CompilerParams(vmem_limit_bytes=vmem * MEGA),
        cost_estimate=cost(flops, args),
        name=name,
    )(*args)


def cut(j):
    return slice(LANES * j, LANES * j + LANES)


def to_flat(ref, j, value, tiles):
    ref[pl.ds(j, value.shape[0], stride=tiles), :] = value


def from_flat(ref, j, tokens, tiles):
    return ref[pl.ds(j, tokens, stride=tiles), :]


def normalise(latent):
    wide = latent.astype(F32)
    inverse = lax.rsqrt(jnp.mean(wide * wide, axis=-1, keepdims=True) + 1e-06)
    return wide * inverse, inverse


def pre_kernel(
    wait,
    send,
    place_ref,
    w_mod_ref,
    feature_ref,
    latent_ref,
    w_in_ref,
    grad_ref,
    w_out_ref,
    own_ref,
    wide_ref,
    slot_0_ref,
    slot_1_ref,
    slot_2_ref,
    slot_3_ref,
    both_ref,
    pre_ref,
    mod_ref,
    cot_ref,
    rows_ref,
    flat_ref,
):
    tokens, width = rows_ref.shape
    tiles = w_in_ref.shape[1] // LANES
    modulation = lax.dot_general(
        feature_ref[...], w_mod_ref[...], NT, preferred_element_type=F32
    )
    mod_ref[...] = modulation
    send(8)
    wait(3)
    latent = latent_ref[...].astype(F32).reshape(tokens, width)
    rows_ref[...] = latent.astype(BF)
    send(10)
    normed, _ = normalise(latent)
    shifted = (normed * (1.0 + modulation[:1, width:]) + modulation[:1, :width]).astype(BF)
    both_ref[0] = shifted
    wait(4)
    pre_act = jnp.dot(shifted, w_in_ref[...], preferred_element_type=F32)
    pre_ref[...] = pre_act
    send(7)
    wait(5)
    both_ref[1] = grad_ref[...].astype(F32).reshape(tokens, width).astype(BF)
    send(6)
    activ = (pre_act * jax.nn.sigmoid(pre_act)).astype(BF)

    def pack(which, value):
        wide = value.astype(F32)
        for j in range(tiles):
            to_flat(flat_ref, j, wide[:, cut(j)], tiles)
        flat = flat_ref[...].astype(BF)
        own_ref[0, which] = flat
        wide_ref[:, which] = flat.reshape(wide_ref.shape[0], wide_ref.shape[2], LANES)
        for k, ref in enumerate((slot_0_ref, slot_1_ref, slot_2_ref, slot_3_ref)):
            chunk = ref.shape[2]
            begin = pl.multiple_of((place_ref[0] ^ k) * chunk, chunk)
            ref[0, which] = flat_ref[pl.ds(begin, chunk), :].astype(BF)
        for n in range(6):
            send(n, which)

    pack(0, activ)
    wait(6)
    cot = lax.dot_general(both_ref[1], w_out_ref[...], NT, preferred_element_type=F32).astype(BF)
    cot_ref[...] = cot
    send(9)
    pack(1, cot)


def parts_of(refs):
    begin, found = 0, []
    for ref in refs:
        size = ref.shape[0] * ref.shape[2]
        found.append((ref, slice(begin, begin + size)))
        begin += size
    return found


def read_part(ref, which):
    return ref[:, which].reshape(ref.shape[0] * ref.shape[2], LANES).astype(F32)


def write_part(ref, which, value):
    ref[:, which] = value.astype(BF).reshape(ref.shape[0], ref.shape[2], LANES)


def scan_kernel(
    length,
    row_of,
    pieces,
    wait,
    send,
    order_ref,
    place_ref,
    *refs,
):
    data_refs, out_refs = refs[:pieces], refs[pieces + 4 : 2 * pieces + 4]
    scan_steps(
        length,
        row_of,
        order_ref,
        place_ref,
        data_refs,
        *refs[pieces : pieces + 4],
        out_refs,
        *refs[2 * pieces + 4 :],
        functools.partial(wait_for, wait, 2 + pieces),
        functools.partial(send_from, send, pieces),
    )


def wait_for(wait, first, n):
    wait(first + n)


def send_from(send, pieces, n):
    if n < 2:
        for k in range(pieces):
            send(k, n)
    else:
        send(pieces + n - 2)


def scan_steps(
    length,
    row_of,
    order_ref,
    place_ref,
    data_refs,
    wsel_ref,
    wdt_ref,
    bias_ref,
    alog_ref,
    out_refs,
    x_ref,
    grad_pre_ref,
    low_ref,
    grad_low_ref,
    gvec_ref,
    pre_ref,
    dt_ref,
    xf_ref,
    x_row_ref,
    dt_row_ref,
    dx_row_ref,
    dy_row_ref,
    bb_ref,
    cb_ref,
    gb_ref,
    gc_ref,
    hist_ref,
    keep_ref,
    y8_ref,
    u8_ref,
    v8_ref,
    rate2_ref,
    rate_ref,
    wait,
    send,
):
    tokens, inner = xf_ref.shape
    tiles = inner // LANES
    lines = tokens // length
    states = alog_ref.shape[0]
    rank = LANES - 2 * states
    for ref, at in parts_of(data_refs):
        x_row_ref[at, :] = read_part(ref, 0)
        dy_row_ref[at, :] = read_part(ref, 1)
    for j in range(tiles):
        xf_ref[:, cut(j)] = from_flat(x_row_ref, j, tokens, tiles)
    x = xf_ref[...].astype(BF)
    x_ref[...] = x
    send(2)
    wait(0)
    select = jnp.dot(x, wsel_ref[...], preferred_element_type=F32)
    lane = lax.broadcasted_iota(jnp.int32, (tokens, LANES), 1)
    low = jnp.where(lane < rank, select, 0.0).astype(BF)
    low_ref[...] = low
    send(4)
    wait(1)
    wait(2)
    w_dt = jnp.concatenate([wdt_ref[...], jnp.zeros((2 * states, inner), BF)], axis=0)
    pre = jnp.dot(low, w_dt, preferred_element_type=F32) + bias_ref[:1, :]
    pre_ref[...] = pre
    spacing = jnp.maximum(pre, 0.0) + jnp.log1p(jnp.exp(-jnp.abs(pre)))
    dt_ref[...] = spacing
    for j in range(tiles):
        at = slice(j * tokens, (j + 1) * tokens)
        dt_row_ref[at, :] = spacing[:, cut(j)]
        dx_row_ref[at, :] = spacing[:, cut(j)] * xf_ref[:, cut(j)]
    wait(3)
    rates = -jnp.exp(alog_ref[...])
    rate_ref[...] = rates
    rate2_ref[...] = rates * LOG2E
    turned = select.T
    for token in range(tokens):
        at = pl.ds(token * states, states)
        column = slice(token, token + 1)
        bb_ref[at, :] = jnp.broadcast_to(turned[rank : rank + states, column], (states, LANES))
        cb_ref[at, :] = jnp.broadcast_to(turned[rank + states :, column], (states, LANES))
    gb_ref[...] = jnp.zeros_like(gb_ref)
    gc_ref[...] = jnp.zeros_like(gc_ref)
    zero = jnp.zeros((states, LANES), F32)
    hist_ref[pl.ds(0, states), :] = jnp.zeros((states, GROUP * LANES), F32)
    unroll = min(length, 8)

    def fold(value):
        return value[:8] + value[8:]

    for group in range(tiles // GROUP):
        first = group * GROUP
        cuts = [cut(first + j) for j in range(GROUP)]
        rate2 = [rate2_ref[:, c] for c in cuts]
        rate1 = [rate_ref[:, c] for c in cuts]

        def one_line(line, grads):
            def places(step):
                row = row_of(order_ref[step], line, place_ref[0])
                at = pl.ds(pl.multiple_of(row * states, states), states)
                slot = pl.ds(pl.multiple_of((step + 1) * states, states), states)
                return row, row * EIGHT, at, slot

            def forward(step, carry):
                row, at_8, at, slot = places(step)
                bb, cb = bb_ref[at, :], cb_ref[at, :]
                new = []
                for j in range(GROUP):
                    dt = dt_row_ref[pl.ds(row + (first + j) * tokens, 1), :]
                    dx = dx_row_ref[pl.ds(row + (first + j) * tokens, 1), :]
                    decay = jnp.exp2(rate2[j] * dt)
                    keep_ref[slot, cut(j)] = decay
                    h = decay * carry[j] + bb * dx
                    hist_ref[slot, cut(j)] = h
                    y8_ref[pl.ds(at_8 + EIGHT * tokens * j, 8), :] = fold(h * cb)
                    new.append(h)
                return tuple(new)

            lax.fori_loop(0, length, forward, (zero,) * GROUP, unroll=unroll)

            def backward(back_step, carry):
                step = length - 1 - back_step
                row, at_8, at, slot = places(step)
                prev = pl.ds(pl.multiple_of(step * states, states), states)
                bb, cb = bb_ref[at, :], cb_ref[at, :]
                pend, acc = carry
                gb = gb_ref[at, :]
                gc = gc_ref[at, :]
                new, acc_new = [], []
                for j in range(GROUP):
                    dt = dt_row_ref[pl.ds(row + (first + j) * tokens, 1), :]
                    dx = dx_row_ref[pl.ds(row + (first + j) * tokens, 1), :]
                    dy = dy_row_ref[pl.ds(row * tiles + first + j, 1), :]
                    g = pend[j] + cb * dy
                    gc = gc + hist_ref[slot, cut(j)] * dy
                    u8_ref[pl.ds(at_8 + EIGHT * tokens * j, 8), :] = fold(g * bb)
                    gb = gb + g * dx
                    p = keep_ref[slot, cut(j)] * g
                    w = p * hist_ref[prev, cut(j)]
                    v8_ref[pl.ds(at_8 + EIGHT * tokens * j, 8), :] = fold(w * rate1[j])
                    acc_new.append(acc[j] + w * dt)
                    new.append(p)
                gb_ref[at, :] = gb
                gc_ref[at, :] = gc
                return tuple(new), tuple(acc_new)

            start = ((zero,) * GROUP, grads)
            return lax.fori_loop(0, length, backward, start, unroll=unroll)[1]

        grads = lax.fori_loop(0, lines, one_line, (zero,) * GROUP)
        for j in range(GROUP):
            gvec_ref[:states, cuts[j]] = grads[j] * rate1[j]

        def gather(block, carry):
            rows = pl.ds(pl.multiple_of(block * 8, 8), 8)

            def summed(ref, j):
                begin = block * (8 * EIGHT) + EIGHT * tokens * j
                return total([ref[pl.ds(begin + r, 8, stride=EIGHT), :] for r in range(8)])

            for j in range(GROUP):
                c = cuts[j]
                u = summed(u8_ref, j)
                x_row_ref[pl.ds(block * 8 * tiles + first + j, 8, stride=tiles), :] = summed(y8_ref, j)
                grad_spacing = summed(v8_ref, j) + xf_ref[rows, c] * u
                pre_ref[rows, c] = grad_spacing * jax.nn.sigmoid(pre_ref[rows, c])
                dt_ref[rows, c] = dt_ref[rows, c] * u
            return carry

        lax.fori_loop(0, tokens // 8, gather, 0, unroll=2)

    for ref, at in parts_of(out_refs):
        write_part(ref, 0, x_row_ref[at, :])
    send(0)
    grad_pre = pre_ref[...]
    gvec_ref[states:, :] = jnp.broadcast_to(
        jnp.sum(grad_pre, axis=0, keepdims=True), (8, inner)
    )
    send(6)
    grad_pre_b = grad_pre.astype(BF)
    grad_pre_ref[...] = grad_pre_b
    send(3)
    shape = (2 * LANES, LANES)
    half = lax.broadcasted_iota(jnp.int32, shape, 0) // LANES
    lane_at = lax.broadcasted_iota(jnp.int32, shape, 1)
    spread = jnp.where((lane_at - rank) // states == half, 1.0, 0.0).astype(BF)
    shape = (tokens * states, LANES)
    state_at = lax.broadcasted_iota(jnp.int32, shape, 0) % states
    lane_at = lax.broadcasted_iota(jnp.int32, shape, 1)
    both = jnp.concatenate([gb_ref[...], gc_ref[...]], axis=1)
    lanes = halves_product(both, spread, False)
    kept = jnp.where((lane_at >= rank) & ((lane_at - rank) % states == state_at), lanes, 0.0)
    shape = (tokens, tokens * states)
    collect = lax.broadcasted_iota(jnp.int32, shape, 1) // states == lax.broadcasted_iota(
        jnp.int32, shape, 0
    )
    grad_maps = halves_product(kept, jnp.where(collect, 1.0, 0.0).astype(BF), True)
    grad_low = lax.dot_general(grad_pre_b, w_dt, NT, preferred_element_type=F32)
    grad_select_out = (grad_low + grad_maps).astype(BF)
    grad_low_ref[...] = grad_select_out
    send(5)
    back = dt_ref[...] + lax.dot_general(
        grad_select_out, wsel_ref[...], NT, preferred_element_type=F32
    )
    for j in range(tiles):
        to_flat(dy_row_ref, j, back[:, cut(j)], tiles)
    for ref, at in parts_of(out_refs):
        write_part(ref, 1, dy_row_ref[at, :])
    send(1)


def halves_product(value, other, other_first):
    top = value.astype(BF)
    rest = (value - top.astype(F32)).astype(BF)
    if other_first:
        return jnp.dot(other, top, preferred_element_type=F32) + jnp.dot(
            other, rest, preferred_element_type=F32
        )
    return jnp.dot(top, other, preferred_element_type=F32) + jnp.dot(
        rest, other, preferred_element_type=F32
    )


def direction(name, length, row_of, order, place, data, params):
    inner = params[0].shape[0]
    tiles = inner // LANES
    tokens = sum(d.shape[0] * d.shape[2] for d in data) // tiles
    states = params[3].shape[0]
    plane = ((tokens, inner), F32)
    flat = ((tokens * tiles, LANES), F32)
    maps = ((tokens * states, LANES), F32)
    eights = ((tokens * EIGHT * GROUP, LANES), F32)
    results = call(
        functools.partial(scan_kernel, length, row_of, len(data)),
        name,
        [(d.shape, BF) for d in data]
        + [((tokens, inner), BF)] * 2
        + [((tokens, LANES), BF)] * 2
        + [((states + 8, inner), F32)],
        [plane] * 3
        + [flat] * 4
        + [maps] * 4
        + [(((length + 1) * states, GROUP * LANES), F32)] * 2
        + [eights] * 3
        + [((states, inner), F32)] * 2,
        VMEM_ALL,
        2e10,
        (order, place, *data, *params),
        smem=(0, 1),
        late=tuple(2 + len(data) + i for i in range(4)),
        early=tuple(range(len(data) + 5)),
    )
    return results[: len(data)], results[len(data) :]


def small_kernel(own_ref, *refs):
    found, refs = [refs[5 * d : 5 * d + 5] for d in range(3)], refs[15:]
    send_ref, row_ref, turned_ref, held_ref = refs
    inner = found[0][0].shape[1]
    tiles = inner // LANES
    tokens = own_ref.shape[2] // tiles
    own = inner // send_ref.shape[0]
    states = found[0][4].shape[0] - 8
    rank = LANES - 2 * states
    row_ref[...] = own_ref[0, 0].astype(F32) * own_ref[0, 1].astype(F32)
    skips = jnp.concatenate(
        [
            jnp.sum(from_flat(row_ref, j, tokens, tiles), axis=0, keepdims=True)
            for j in range(tiles)
        ],
        axis=1,
    )
    x, grad_pre, low, grad_low = [
        jnp.concatenate([d[i][...] for d in found], axis=0) for i in range(4)
    ]
    summed = total([d[4][...] for d in found])
    at = lax.broadcasted_iota(jnp.int32, (LANES, inner), 0)
    vectors = jnp.concatenate(
        [jnp.zeros((rank, inner), F32), summed, jnp.zeros((states - 8, inner), F32)], axis=0
    )
    vectors = jnp.where(at > rank + states, 0.0, vectors) + jnp.where(
        at == rank + states + 1, jnp.broadcast_to(skips, at.shape), 0.0
    )
    turned_ref[0] = lax.dot_general(x, grad_low, TN, preferred_element_type=F32)
    turned_ref[1] = vectors.T + lax.dot_general(
        grad_pre, low, TN, preferred_element_type=F32
    )
    for d in range(send_ref.shape[0]):
        for which in (0, 1):
            begin = (2 * d + which) * own
            held_ref[begin : begin + own, :] = turned_ref[which, d * own : (d + 1) * own, :]
    send_ref[...] = held_ref[...].reshape(send_ref.shape).astype(BF)


def spread_rows(ref, which, own, near, held_ref):
    for m in range(near):
        for o in range(FAR_SIZE):
            begin = (o * near + m) * own
            at = (m * FAR_SIZE + o) * own
            held_ref[at : at + own, :] = ref[which, begin : begin + own, :]
    return held_ref[...].reshape(near, FAR_SIZE * own, LANES).astype(BF)


def post_kernel(
    send,
    place_ref,
    activ_ref,
    cot_ref,
    time_ref,
    wide_ref,
    slot_0_ref,
    slot_1_ref,
    slot_2_ref,
    slot_3_ref,
    pre_ref,
    skip_ref,
    mixed_out_ref,
    grad_act_ref,
    send_ref,
    sum_ref,
    turned_ref,
    held_ref,
):
    tokens, inner = pre_ref.shape
    tiles = inner // LANES
    flat_shape = (tokens * tiles, LANES)
    near = send_ref.shape[0]
    near_rows = inner // near
    own = near_rows // FAR_SIZE

    def summed(which, own_ref):
        sum_ref[...] = time_ref[0, which].astype(F32) + wide_ref[:, which].reshape(
            flat_shape
        ).astype(F32)
        for k, ref in enumerate((slot_0_ref, slot_1_ref, slot_2_ref, slot_3_ref)):
            chunk = ref.shape[2]
            at = pl.ds(pl.multiple_of((place_ref[0] ^ k) * chunk, chunk), chunk)
            sum_ref[at, :] += ref[0, which].astype(F32)
        scans = jnp.concatenate([from_flat(sum_ref, j, tokens, tiles) for j in range(tiles)], axis=1)
        return scans + skip_ref[1:, :] * own_ref[...].astype(F32)

    back = summed(1, cot_ref)
    pre_act = pre_ref[...]
    gate = jax.nn.sigmoid(pre_act)
    grad_act = (back * gate * (1.0 + pre_act * (1.0 - gate))).astype(BF)
    grad_act_ref[...] = grad_act
    send(1)
    turned_ref[1] = grad_act.astype(F32).T
    mixed = summed(0, activ_ref).astype(BF)
    mixed_out_ref[...] = mixed
    send(0)
    turned_ref[0] = mixed.astype(F32).T
    send_ref[:, :near_rows] = spread_rows(turned_ref, 0, own, near, held_ref)
    for m in range(near):
        send_ref[m, near_rows:] = turned_ref[1, pl.ds(m * near_rows, near_rows), :].astype(BF)


def finish_kernel(
    wait,
    mixed_ref,
    grad_act_ref,
    latent_ref,
    mod_ref,
    w_in_ref,
    w_out_ref,
    branch_ref,
    latent_grad_ref,
    vec_ref,
):
    tokens, width = latent_ref.shape
    normed, inverse = normalise(latent_ref[...])
    wait(4)
    grad_shifted = lax.dot_general(
        grad_act_ref[...], w_in_ref[...], NT, preferred_element_type=F32
    )
    grad_vec = jnp.concatenate(
        [
            jnp.sum(grad_shifted, axis=0, keepdims=True),
            jnp.sum(grad_shifted * normed, axis=0, keepdims=True),
        ],
        axis=1,
    )
    devices = vec_ref.shape[0]
    part = 2 * width // devices
    shape = (devices, 2 * width)
    block_at = lax.broadcasted_iota(jnp.int32, shape, 0) * part
    column_at = lax.broadcasted_iota(jnp.int32, shape, 1)
    mine = (column_at >= block_at) & (column_at < block_at + part)
    chosen = jnp.where(mine, jnp.broadcast_to(grad_vec, shape), 0.0)
    lane_at = lax.broadcasted_iota(jnp.int32, (2 * width, LANES), 1)
    place = lax.broadcasted_iota(jnp.int32, (2 * width, LANES), 0) % part
    choose = jnp.where(lane_at == place, 1.0, 0.0).astype(BF)
    vec_ref[...] = halves_product(chosen, choose, False)
    grad_normed = grad_shifted * (1.0 + mod_ref[:1, width:])
    product = jnp.mean(grad_normed * normed, axis=1, keepdims=True)
    result = inverse * (grad_normed - normed * product)
    latent_grad_ref[...] = result.reshape(latent_grad_ref.shape).astype(BF)
    wait(5)
    result = jnp.dot(mixed_ref[...], w_out_ref[...], preferred_element_type=F32)
    branch_ref[...] = result.reshape(branch_ref.shape).astype(BF)


def long_product(wait, at, left, right_ref):
    size = right_ref.shape[0] // PIECES
    tokens, width = right_ref.shape[1:]
    terms = []
    for n in range(PIECES):
        wait(at, n)
        rows = slice(n * size * tokens, (n + 1) * size * tokens)
        right = right_ref[n * size : (n + 1) * size].reshape(size * tokens, width)
        terms.append(jnp.dot(left[:, rows], right, preferred_element_type=F32))
    return total(terms)


def in_grad_kernel(wait, recv_ref, both_ref, small_ref, vec_ref, all_ref, right_ref, rows_ref):
    near = recv_ref.shape[0]
    rows = right_ref.shape[0]
    width = both_ref.shape[2]
    devices = all_ref.shape[0]
    own = rows // FAR_SIZE
    for s in range(near):
        right_ref[:, cut(s)] = recv_ref[s, rows:]
    product = long_product(wait, 1, right_ref, both_ref)
    wait(2)
    wait(3)
    all_ref[:, SLOT:] = small_ref[...]
    turned = jnp.concatenate([product, jnp.zeros((LANES - rows, width), F32)], axis=0).T
    for d in range(devices):
        rows_ref[d * SLOT : d * SLOT + own, :] = turned[d * own : (d + 1) * own]
    for n in range(own, SLOT):
        rows_ref[pl.ds(n, devices, stride=SLOT), :] = vec_ref[...]
    all_ref[:, :SLOT] = rows_ref[...].reshape(devices, SLOT, LANES).astype(BF)


def pair_place(place, core_flip, slot):
    return place ^ ((slot // 2) * 4 + core_flip * 2 + slot % 2)


def out_grad_kernel(
    wait, place_ref, recv_ref, both_ref, mine_ref, other_ref, left_ref, out_ref, half_ref
):
    near = recv_ref.shape[0]
    rows = left_ref.shape[0]
    far = FAR_SIZE
    tiles = both_ref.shape[2] // LANES
    own = rows // far
    for s in range(near):
        left_ref[:, cut(s)] = recv_ref[s, :rows]
    product = long_product(wait, 2, left_ref, both_ref)
    for j in range(tiles):
        half_ref[...] = product[:, cut(j)]
        for o in range(far):
            out_ref[o, pl.ds(j, own, stride=tiles), :] = half_ref[o * own : (o + 1) * own, :]
    for slot in range(far // 2):
        mine_ref[slot] = out_ref[pair_place(place_ref[0], 0, slot)]
        other_ref[slot] = out_ref[pair_place(place_ref[0], 1, slot)].astype(BF)


def pair_sum_kernel(mine_ref, other_ref, kept_ref, *slot_refs):
    kept_ref[...] = mine_ref[0] + other_ref[0].astype(F32)
    for slot, ref in enumerate(slot_refs, 1):
        ref[...] = (mine_ref[slot] + other_ref[slot].astype(F32)).astype(BF)


def last_kernel(all_ref, feature_ref, *refs):
    far_refs = refs[: FAR_SIZE // 2]
    gwo_ref, gwi_ref, gsel_ref, gdt_ref, galog_ref, gvec_ref, gmod_ref, sum_ref, rest_ref = refs[
        FAR_SIZE // 2 :
    ]
    far = FAR_SIZE
    own, width = gwo_ref.shape
    tiles = width // LANES
    near = all_ref.shape[0] // far
    part = width // near
    sum_ref[...] = total([ref[...].astype(F32) for ref in far_refs])
    for j in range(tiles):
        gwo_ref[:, cut(j)] = sum_ref[pl.ds(j, own, stride=tiles), :]
    rest = []
    for m in range(near):
        block = total([all_ref[o * near + m].astype(F32) for o in range(far)])
        gwi_ref[:, part * m : part * (m + 1)] = block[:own, :part]
        rest.append(block)
    rest_ref[...] = total(rest)
    vec = rest_ref[own : own + 1, :]
    turned = jnp.broadcast_to(vec, (LANES, LANES)).T
    gmod_ref[...] = turned[: 2 * own, :1] * feature_ref[:1, :].astype(F32)
    gsel_ref[...] = rest_ref[SLOT : SLOT + own, :]
    rank, states = gdt_ref.shape[1], galog_ref.shape[1]
    base = SLOT + own
    gdt_ref[...] = rest_ref[base : base + own, :rank]
    galog_ref[...] = rest_ref[base : base + own, rank : rank + states]
    turned = jnp.concatenate([rest_ref[base : base + own, :], jnp.zeros((LANES - own, LANES), F32)])
    gvec_ref[...] = turned.T[rank + states : rank + states + 8, :own]


def permute(value, axes, k):
    if k == 0:
        return value
    return lax.ppermute(value, axes, [(i, i ^ k) for i in range(lax.axis_size(axes))])


def exchange(value, axes):
    return lax.all_to_all(value, axes, split_axis=0, concat_axis=0, tiled=True)


def local(
    latent,
    out_grad,
    w_in,
    w_out,
    w_select,
    w_dt,
    dt_bias,
    a_log,
    d_skip,
    w_mod,
    t_index,
    frame_order,
    row_order,
    col_order,
):
    frames, rows, cols, width = latent.shape
    inner = w_in.shape[1]
    tokens = frames * rows * cols
    tiles = inner // LANES
    states = a_log.shape[1]
    n_row, n_col = lax.axis_size(ROW), lax.axis_size(COL)
    near, far = lax.axis_size(NEAR), lax.axis_size(FAR)
    own = width // (near * far)
    features = jax.nn.silu(time_features(t_index, w_mod.shape[1])).astype(BF)
    feature_rows = jnp.broadcast_to(features[None, :], (8, features.shape[0]))

    def packed(parts):
        return ((parts, 2, tokens * tiles // parts, LANES), BF)

    slot = ((1, 2, tokens * tiles // n_row, LANES), BF)
    place = lax.axis_index(ROW).astype(jnp.int32)[None]
    far_place = lax.axis_index(FAR).astype(jnp.int32)[None]
    data_own, data_wide, *slots, both, pre_act, modulation, cot, flat_latent = call(
        pre_kernel,
        "norm_project",
        [
            packed(1),
            packed(n_col),
            slot,
            slot,
            slot,
            slot,
            ((2, tokens, width), BF),
            ((tokens, inner), F32),
            ((8, 2 * width), F32),
            ((tokens, inner), BF),
            ((tokens, width), BF),
        ],
        [((tokens * tiles, LANES), F32)],
        VMEM_ALL,
        7e9,
        (place, w_mod, feature_rows, latent, w_in, out_grad, w_out),
        smem=(0,),
        late=(3, 4, 5, 6),
        early=tuple(range(11)),
    )
    data_wide = exchange(data_wide, COL)
    slots = [permute(value, ROW, k) for k, value in enumerate(slots)]
    both_near = lax.all_gather(both, NEAR, axis=0, tiled=False)
    vectors = jnp.stack([dt_bias, d_skip])
    params = (
        w_select,
        w_dt.T,
        vectors,
        a_log.T,
    )
    area = rows * cols

    def time_row(at, line, place):
        return at * area + line

    def wide_row(at, line, place):
        chunk = frames // n_col * area
        return (
            lax.div(at, cols) * chunk
            + lax.rem(at, cols)
            + lax.div(line, rows) * area
            + lax.rem(line, rows) * cols
        )

    def tall_row(at, line, place):
        chunk = frames // n_row * area
        return (
            (lax.div(at, rows) ^ place) * chunk
            + lax.rem(at, rows) * cols
            + lax.div(line, cols) * area
            + lax.rem(line, cols)
        )

    out_tall, grads_tall = direction(
        "scan_height", rows * n_row, tall_row, row_order, place, slots, params
    )
    out_slots = [permute(value, ROW, k) for k, value in enumerate(out_tall)]
    data_wide, _ = lax.optimization_barrier((data_wide, out_tall))
    (out_wide,), grads_wide = direction(
        "scan_width", cols * n_col, wide_row, col_order, place, [data_wide], params
    )
    data_time, out_slots, _ = lax.optimization_barrier((data_own, out_slots, out_wide))
    out_wide = exchange(out_wide, COL)
    (out_time,), grads_time = direction(
        "scan_time", frames, time_row, frame_order, place, [data_time], params
    )
    mixed, grad_act, near_send = call(
        post_kernel,
        "sum_directions",
        [
            ((tokens, inner), BF),
            ((tokens, inner), BF),
            ((near, 2 * inner // near, LANES), BF),
        ],
        [
            ((tokens * tiles, LANES), F32),
            ((2, inner, LANES), F32),
            ((inner, LANES), F32),
        ],
        VMEM_ALL,
        6e9,
        (place, grads_time[0], cot, out_time, out_wide, *out_slots, pre_act, vectors),
        smem=(0,),
        early=(0, 1),
    )
    near_recv = exchange(near_send, NEAR)
    data_own, _ = lax.optimization_barrier((data_own, near_send))
    small_send = call(
        small_kernel,
        "small_sums",
        [((near * far, 2 * own, LANES), BF)],
        [
            ((tokens * tiles, LANES), F32),
            ((2, inner, LANES), F32),
            ((2 * inner, LANES), F32),
        ],
        VMEM_ALL,
        3e9,
        (data_own, *grads_time, *grads_wide, *grads_tall),
    )[0]
    branch, latent_grad, vec = call(
        finish_kernel,
        "out_projections",
        [(latent.shape, BF), (latent.shape, BF), ((near * far, LANES), F32)],
        [],
        VMEM_ALL,
        6e9,
        (mixed, grad_act, flat_latent, modulation, w_in, w_out),
        late=(4, 5),
    )
    near_recv, vec, small_send = lax.optimization_barrier((near_recv, vec, small_send))
    piece = own * tiles
    all_send = call(
        in_grad_kernel,
        "in_weight_grad",
        [((near * far, SLOT + 2 * own, LANES), BF)],
        [((inner // near, near * tokens), BF), ((near * far * SLOT, LANES), F32)],
        VMEM_ALL,
        3e9,
        (near_recv, both_near, small_send, vec),
        late=(1, 2, 3),
        pieces={1: PIECES},
        choose={1: 0},
    )[0]
    all_recv = exchange(all_send, FAR + NEAR)
    mine, other = call(
        out_grad_kernel,
        "out_weight_grad",
        [((far // 2, piece, LANES), F32), ((far // 2, piece, LANES), BF)],
        [
            ((inner // near, near * tokens), BF),
            ((far, piece, LANES), F32),
            ((inner // near, LANES), F32),
        ],
        VMEM_ALL,
        4e9,
        (far_place, near_recv, both_near),
        smem=(0,),
        late=(2,),
        pieces={2: PIECES},
        choose={2: 1},
    )
    other = permute(other, FAR, 2)
    far_send = plain_call(
        pair_sum_kernel,
        "pair_sums",
        [((piece, LANES), F32)] + [((piece, LANES), BF)] * (far // 2 - 1),
        [],
        8,
        1e9,
        (mine, other),
    )
    far_recv = [permute(value, FAR, (0, 1, 4, 5)[slot]) for slot, value in enumerate(far_send)]
    rank = w_dt.shape[1]
    grad_w_out, grad_w_in, grad_select, grad_dt, grad_alog, grad_vec, grad_mod = plain_call(
        last_kernel,
        "weight_sums",
        [
            ((own, width), F32),
            ((own, width), F32),
            ((own, LANES), F32),
            ((own, rank), F32),
            ((own, states), F32),
            ((8, own), F32),
            ((2 * own, features.shape[0]), F32),
        ],
        [((piece, LANES), F32), ((SLOT + 2 * own, LANES), F32)],
        16,
        1e9,
        (all_recv, feature_rows, *far_recv),
    )
    return (
        branch,
        latent_grad,
        grad_w_in,
        grad_w_out,
        grad_select,
        grad_dt,
        grad_vec[0],
        grad_alog,
        grad_vec[1],
        grad_mod,
    )


def solution(mesh):
    n_row, n_col = mesh.shape["row"], mesh.shape["col"]
    split = Mesh(mesh.devices.reshape(n_row // 2, 2, 2, 4, n_col // 8), AXES)
    tokens = P(None, ROW, COL, None)
    matrix = P(ROW + COL, None)
    vector = P(ROW + COL)
    return jax.shard_map(
        local,
        mesh=split,
        in_specs=(tokens, tokens) + (P(),) * 12,
        out_specs=(
            tokens,
            tokens,
            matrix,
            matrix,
            matrix,
            matrix,
            vector,
            matrix,
            vector,
            matrix,
        ),
        check_vma=False,
    )
```

```python
import functools
import math

import jax
import jax.numpy as jnp
from jax import lax
from jax.experimental import pallas as pl
from jax.experimental.pallas import tpu as pltpu
from jax.sharding import Mesh
from jax.sharding import PartitionSpec as P

BF = jnp.bfloat16
F32 = jnp.float32
LANES = 128
GROUP = 6
EIGHT = 9
LOG2E = math.log2(math.e)
MEGA = 1024 * 1024
VMEM_ALL = 60
PIECES = 4
SLOT = 16
AXES = ("xl", "core", "xh", "y", "z")
ROW = ("xl", "core")
COL = ("xh", "y", "z")
NEAR = ("y", "z")
FAR = ("xl", "core", "xh")
FAR_SIZE = 8
NT = (((1,), (1,)), ((), ()))
TN = (((0,), (0,)), ((), ()))


def time_features(step_index, width):
    halfway = width // 2
    frequency = jnp.exp(-math.log(10000.0) * jnp.arange(halfway, dtype=jnp.float32) / halfway)
    angles = step_index.astype(jnp.float32)[0] * frequency
    return jnp.concatenate([jnp.cos(angles), jnp.sin(angles)])


def total(terms):
    return functools.reduce(lambda a, b: a + b, terms)


def call(kernel, name, out_shape, scratch, vmem, flops, args, smem=(), late=(), pieces=None, choose=None, early=()):
    moved = [i for i in range(len(args)) if i not in smem]
    pieces, choose = pieces or {}, choose or {}
    held_shape = {
        i: args[i].shape[:1] + args[i].shape[2:] if i in choose else args[i].shape for i in moved
    }
    cuts = []
    for i in moved:
        size = args[i].shape[0] // pieces.get(i, 1)
        cuts += [(i, n, pl.ds(n * size, size)) for n in range(pieces.get(i, 1))]

    def body(*refs):
        given, out = refs[: len(args)], refs[len(args) : len(args) + len(out_shape)]
        rest = refs[len(args) + len(out_shape) :]
        held, rest = rest[: len(moved)], rest[len(moved) :]
        made, rest = rest[: len(out_shape)], rest[len(out_shape) :]
        in_sem, out_sem = rest[-2:]
        views = [given[i] if i in smem else held[moved.index(i)] for i in range(len(args))]
        copies = {
            (i, n): pltpu.make_async_copy(
                given[i].at[at, choose[i]] if i in choose else given[i].at[at],
                views[i].at[at],
                in_sem.at[place],
            )
            for place, (i, n, at) in enumerate(cuts)
        }
        for copy in copies.values():
            copy.start()
        for (i, _), copy in copies.items():
            if i not in late:
                copy.wait()
        waits = (lambda i, n=0: copies[i, n].wait(),) if late else ()
        sent = []

        def send(n, plane=None):
            at = (slice(None), plane) if plane is not None else (slice(None),)
            place = 2 * n + (plane or 0)
            copy = pltpu.make_async_copy(made[n].at[at], out[n].at[at], out_sem.at[place])
            copy.start()
            sent.append(copy)

        kernel(*waits, *((send,) if early else ()), *views, *made, *rest[:-2])
        for n in range(len(out_shape)):
            if n not in early:
                send(n)
        for copy in sent:
            copy.wait()

    spaces = [
        pl.BlockSpec(memory_space=pltpu.SMEM if i in smem else pltpu.HBM) for i in range(len(args))
    ]
    return pl.pallas_call(
        body,
        out_shape=tuple(jax.ShapeDtypeStruct(s, d) for s, d in out_shape),
        in_specs=spaces,
        out_specs=(pl.BlockSpec(memory_space=pltpu.HBM),) * len(out_shape),
        scratch_shapes=[pltpu.VMEM(held_shape[i], args[i].dtype) for i in moved]
        + [pltpu.VMEM(s, d) for s, d in out_shape]
        + [pltpu.VMEM(s, d) for s, d in scratch]
        + [pltpu.SemaphoreType.DMA((len(cuts),)), pltpu.SemaphoreType.DMA((2 * len(out_shape),))],
        compiler_params=pltpu.CompilerParams(vmem_limit_bytes=vmem * MEGA),
        cost_estimate=cost(flops, args),
        name=name,
    )(*args)


def cost(flops, args):
    return pl.CostEstimate(
        flops=int(flops),
        bytes_accessed=sum(a.size * a.dtype.itemsize for a in args),
        transcendentals=0,
    )


def plain_call(kernel, name, out_shape, scratch, vmem, flops, args, smem=()):
    spaces = [
        pl.BlockSpec(memory_space=pltpu.SMEM if i in smem else pltpu.VMEM) for i in range(len(args))
    ]
    return pl.pallas_call(
        kernel,
        out_shape=tuple(jax.ShapeDtypeStruct(s, d) for s, d in out_shape),
        in_specs=spaces,
        out_specs=(pl.BlockSpec(memory_space=pltpu.VMEM),) * len(out_shape),
        scratch_shapes=[pltpu.VMEM(s, d) for s, d in scratch],
        compiler_params=pltpu.CompilerParams(vmem_limit_bytes=vmem * MEGA),
        cost_estimate=cost(flops, args),
        name=name,
    )(*args)


def cut(j):
    return slice(LANES * j, LANES * j + LANES)


def to_flat(ref, j, value, tiles):
    ref[pl.ds(j, value.shape[0], stride=tiles), :] = value


def from_flat(ref, j, tokens, tiles):
    return ref[pl.ds(j, tokens, stride=tiles), :]


def normalise(latent):
    wide = latent.astype(F32)
    inverse = lax.rsqrt(jnp.mean(wide * wide, axis=-1, keepdims=True) + 1e-06)
    return wide * inverse, inverse


def pre_kernel(
    wait,
    send,
    place_ref,
    w_mod_ref,
    feature_ref,
    latent_ref,
    w_in_ref,
    grad_ref,
    w_out_ref,
    own_ref,
    wide_ref,
    slot_0_ref,
    slot_1_ref,
    slot_2_ref,
    slot_3_ref,
    both_ref,
    pre_ref,
    mod_ref,
    cot_ref,
    rows_ref,
    flat_ref,
):
    tokens, width = rows_ref.shape
    tiles = w_in_ref.shape[1] // LANES
    modulation = lax.dot_general(
        jnp.broadcast_to(feature_ref[...].reshape(1, -1), (8, feature_ref.shape[0])),
        w_mod_ref[...],
        NT,
        preferred_element_type=F32,
    )
    mod_ref[...] = modulation
    send(8)
    wait(3)
    latent = latent_ref[...].astype(F32).reshape(tokens, width)
    rows_ref[...] = latent.astype(BF)
    send(10)
    normed, _ = normalise(latent)
    shifted = (normed * (1.0 + modulation[:1, width:]) + modulation[:1, :width]).astype(BF)
    both_ref[0] = shifted
    wait(4)
    pre_act = jnp.dot(shifted, w_in_ref[...], preferred_element_type=F32)
    pre_ref[...] = pre_act
    send(7)
    wait(5)
    both_ref[1] = grad_ref[...].astype(F32).reshape(tokens, width).astype(BF)
    send(6)
    activ = (pre_act * jax.nn.sigmoid(pre_act)).astype(BF)

    def pack(which, value):
        wide = value.astype(F32)
        for j in range(tiles):
            to_flat(flat_ref, j, wide[:, cut(j)], tiles)
        flat = flat_ref[...].astype(BF)
        own_ref[0, which] = flat
        wide_ref[:, which] = flat.reshape(wide_ref.shape[0], wide_ref.shape[2], LANES)
        for k, ref in enumerate((slot_0_ref, slot_1_ref, slot_2_ref, slot_3_ref)):
            chunk = ref.shape[2]
            begin = pl.multiple_of((place_ref[0] ^ k) * chunk, chunk)
            ref[0, which] = flat_ref[pl.ds(begin, chunk), :].astype(BF)
        for n in range(6):
            send(n, which)

    pack(0, activ)
    wait(6)
    cot = lax.dot_general(both_ref[1], w_out_ref[...], NT, preferred_element_type=F32).astype(BF)
    cot_ref[...] = cot
    send(9)
    pack(1, cot)


def parts_of(refs):
    begin, found = 0, []
    for ref in refs:
        size = ref.shape[0] * ref.shape[2]
        found.append((ref, slice(begin, begin + size)))
        begin += size
    return found


def read_part(ref, which):
    return ref[:, which].reshape(ref.shape[0] * ref.shape[2], LANES).astype(F32)


def write_part(ref, which, value):
    ref[:, which] = value.astype(BF).reshape(ref.shape[0], ref.shape[2], LANES)


def scan_kernel(
    length,
    row_of,
    pieces,
    wait,
    send,
    order_ref,
    place_ref,
    *refs,
):
    data_refs, out_refs = refs[:pieces], refs[pieces + 4 : 2 * pieces + 4]
    scan_steps(
        length,
        row_of,
        order_ref,
        place_ref,
        data_refs,
        *refs[pieces : pieces + 4],
        out_refs,
        *refs[2 * pieces + 4 :],
        functools.partial(wait_for, wait, 2 + pieces),
        functools.partial(send_from, send, pieces),
    )


def wait_for(wait, first, n):
    wait(first + n)


def send_from(send, pieces, n):
    if n < 2:
        for k in range(pieces):
            send(k, n)
    else:
        send(pieces + n - 2)


def scan_steps(
    length,
    row_of,
    order_ref,
    place_ref,
    data_refs,
    wsel_ref,
    wdt_ref,
    bias_ref,
    alog_ref,
    out_refs,
    x_ref,
    grad_pre_ref,
    low_ref,
    grad_low_ref,
    gvec_ref,
    pre_ref,
    dt_ref,
    xf_ref,
    x_row_ref,
    dt_row_ref,
    dx_row_ref,
    dy_row_ref,
    bb_ref,
    cb_ref,
    gb_ref,
    gc_ref,
    hist_ref,
    keep_ref,
    y8_ref,
    u8_ref,
    v8_ref,
    rate2_ref,
    rate_ref,
    wait,
    send,
):
    tokens, inner = xf_ref.shape
    tiles = inner // LANES
    lines = tokens // length
    states = alog_ref.shape[0]
    rank = LANES - 2 * states
    for ref, at in parts_of(data_refs):
        x_row_ref[at, :] = read_part(ref, 0)
        dy_row_ref[at, :] = read_part(ref, 1)
    for j in range(tiles):
        xf_ref[:, cut(j)] = from_flat(x_row_ref, j, tokens, tiles)
    x = xf_ref[...].astype(BF)
    x_ref[...] = x
    send(2)
    wait(0)
    select = jnp.dot(x, wsel_ref[...], preferred_element_type=F32)
    lane = lax.broadcasted_iota(jnp.int32, (tokens, LANES), 1)
    low = jnp.where(lane < rank, select, 0.0).astype(BF)
    low_ref[...] = low
    send(4)
    wait(1)
    wait(2)
    w_dt = jnp.concatenate([wdt_ref[...], jnp.zeros((2 * states, inner), BF)], axis=0)
    pre = jnp.dot(low, w_dt, preferred_element_type=F32) + bias_ref[...].reshape(1, inner)
    pre_ref[...] = pre
    spacing = jnp.maximum(pre, 0.0) + jnp.log1p(jnp.exp(-jnp.abs(pre)))
    dt_ref[...] = spacing
    for j in range(tiles):
        at = slice(j * tokens, (j + 1) * tokens)
        dt_row_ref[at, :] = spacing[:, cut(j)]
        dx_row_ref[at, :] = spacing[:, cut(j)] * xf_ref[:, cut(j)]
    wait(3)
    rates = -jnp.exp(alog_ref[...])
    rate_ref[...] = rates
    rate2_ref[...] = rates * LOG2E
    turned = select.T
    for token in range(tokens):
        at = pl.ds(token * states, states)
        column = slice(token, token + 1)
        bb_ref[at, :] = jnp.broadcast_to(turned[rank : rank + states, column], (states, LANES))
        cb_ref[at, :] = jnp.broadcast_to(turned[rank + states :, column], (states, LANES))
    gb_ref[...] = jnp.zeros_like(gb_ref)
    gc_ref[...] = jnp.zeros_like(gc_ref)
    zero = jnp.zeros((states, LANES), F32)
    hist_ref[pl.ds(0, states), :] = jnp.zeros((states, GROUP * LANES), F32)
    unroll = min(length, 8)

    def repeat(step, carry):
        def block(n, carry):
            for inside in range(unroll):
                carry = step(n, inside, carry)
            return carry

        if length == unroll:
            return block(0, carry)
        return lax.fori_loop(0, length // unroll, block, carry)

    def fold(value):
        return value[:8] + value[8:]

    for group in range(tiles // GROUP):
        first = group * GROUP
        cuts = [cut(first + j) for j in range(GROUP)]
        rate2 = [rate2_ref[:, c] for c in cuts]
        rate1 = [rate_ref[:, c] for c in cuts]

        def one_line(line, grads):
            def places(block, inside):
                row = row_of(order_ref[block * unroll + inside], line, place_ref[0])
                at = pl.ds(pl.multiple_of(row * states, states), states)
                base = pl.multiple_of(block * (unroll * states), unroll * states)
                slot = pl.ds(base + (inside + 1) * states, states)
                prev = pl.ds(base + inside * states, states)
                return row, row * EIGHT, at, slot, prev

            def forward(block, inside, carry):
                row, at_8, at, slot, _ = places(block, inside)
                bb, cb = bb_ref[at, :], cb_ref[at, :]
                new = []
                for j in range(GROUP):
                    dt = dt_row_ref[pl.ds(row + (first + j) * tokens, 1), :]
                    dx = dx_row_ref[pl.ds(row + (first + j) * tokens, 1), :]
                    decay = jnp.exp2(rate2[j] * dt)
                    keep_ref[slot, cut(j)] = decay
                    h = decay * carry[j] + bb * dx
                    hist_ref[slot, cut(j)] = h
                    y8_ref[pl.ds(at_8 + EIGHT * tokens * j, 8), :] = fold(h * cb)
                    new.append(h)
                return tuple(new)

            repeat(forward, (zero,) * GROUP)

            def backward(block, inside, carry):
                last = length // unroll - 1
                row, at_8, at, slot, prev = places(last - block, unroll - 1 - inside)
                bb, cb = bb_ref[at, :], cb_ref[at, :]
                pend, acc = carry
                gb = gb_ref[at, :]
                gc = gc_ref[at, :]
                new, acc_new = [], []
                for j in range(GROUP):
                    dt = dt_row_ref[pl.ds(row + (first + j) * tokens, 1), :]
                    dx = dx_row_ref[pl.ds(row + (first + j) * tokens, 1), :]
                    dy = dy_row_ref[pl.ds(row * tiles + first + j, 1), :]
                    g = pend[j] + cb * dy
                    gc = gc + hist_ref[slot, cut(j)] * dy
                    u8_ref[pl.ds(at_8 + EIGHT * tokens * j, 8), :] = fold(g * bb)
                    gb = gb + g * dx
                    p = keep_ref[slot, cut(j)] * g
                    w = p * hist_ref[prev, cut(j)]
                    v8_ref[pl.ds(at_8 + EIGHT * tokens * j, 8), :] = fold(w * rate1[j])
                    acc_new.append(acc[j] + w * dt)
                    new.append(p)
                gb_ref[at, :] = gb
                gc_ref[at, :] = gc
                return tuple(new), tuple(acc_new)

            start = ((zero,) * GROUP, grads)
            return repeat(backward, start)[1]

        grads = lax.fori_loop(0, lines, one_line, (zero,) * GROUP)
        for j in range(GROUP):
            gvec_ref[:states, cuts[j]] = grads[j] * rate1[j]

        def gather(block, carry):
            rows = pl.ds(pl.multiple_of(block * 8, 8), 8)

            def summed(ref, j):
                begin = block * (8 * EIGHT) + EIGHT * tokens * j
                return total([ref[pl.ds(begin + r, 8, stride=EIGHT), :] for r in range(8)])

            for j in range(GROUP):
                c = cuts[j]
                u = summed(u8_ref, j)
                x_row_ref[pl.ds(block * 8 * tiles + first + j, 8, stride=tiles), :] = summed(y8_ref, j)
                grad_spacing = summed(v8_ref, j) + xf_ref[rows, c] * u
                pre_ref[rows, c] = grad_spacing * jax.nn.sigmoid(pre_ref[rows, c])
                dt_ref[rows, c] = dt_ref[rows, c] * u
            return carry

        lax.fori_loop(0, tokens // 8, gather, 0, unroll=2)

    for ref, at in parts_of(out_refs):
        write_part(ref, 0, x_row_ref[at, :])
    send(0)
    grad_pre = pre_ref[...]
    gvec_ref[states:, :] = jnp.broadcast_to(
        jnp.sum(grad_pre, axis=0, keepdims=True), (8, inner)
    )
    send(6)
    grad_pre_b = grad_pre.astype(BF)
    grad_pre_ref[...] = grad_pre_b
    send(3)
    shape = (2 * LANES, LANES)
    half = lax.broadcasted_iota(jnp.int32, shape, 0) // LANES
    lane_at = lax.broadcasted_iota(jnp.int32, shape, 1)
    spread = jnp.where((lane_at - rank) // states == half, 1.0, 0.0).astype(BF)
    shape = (tokens * states, LANES)
    state_at = lax.broadcasted_iota(jnp.int32, shape, 0) % states
    lane_at = lax.broadcasted_iota(jnp.int32, shape, 1)
    both = jnp.concatenate([gb_ref[...], gc_ref[...]], axis=1)
    lanes = halves_product(both, spread, False)
    kept = jnp.where((lane_at >= rank) & ((lane_at - rank) % states == state_at), lanes, 0.0)
    shape = (tokens, tokens * states)
    collect = lax.broadcasted_iota(jnp.int32, shape, 1) // states == lax.broadcasted_iota(
        jnp.int32, shape, 0
    )
    grad_maps = halves_product(kept, jnp.where(collect, 1.0, 0.0).astype(BF), True)
    grad_low = lax.dot_general(grad_pre_b, w_dt, NT, preferred_element_type=F32)
    grad_select_out = (grad_low + grad_maps).astype(BF)
    grad_low_ref[...] = grad_select_out
    send(5)
    back = dt_ref[...] + lax.dot_general(
        grad_select_out, wsel_ref[...], NT, preferred_element_type=F32
    )
    for j in range(tiles):
        to_flat(dy_row_ref, j, back[:, cut(j)], tiles)
    for ref, at in parts_of(out_refs):
        write_part(ref, 1, dy_row_ref[at, :])
    send(1)


def halves_product(value, other, other_first):
    top = value.astype(BF)
    rest = (value - top.astype(F32)).astype(BF)
    if other_first:
        return jnp.dot(other, top, preferred_element_type=F32) + jnp.dot(
            other, rest, preferred_element_type=F32
        )
    return jnp.dot(top, other, preferred_element_type=F32) + jnp.dot(
        rest, other, preferred_element_type=F32
    )


def direction(name, length, row_of, order, place, data, params):
    inner = params[0].shape[0]
    tiles = inner // LANES
    tokens = sum(d.shape[0] * d.shape[2] for d in data) // tiles
    states = params[3].shape[0]
    plane = ((tokens, inner), F32)
    flat = ((tokens * tiles, LANES), F32)
    maps = ((tokens * states, LANES), F32)
    eights = ((tokens * EIGHT * GROUP, LANES), F32)
    results = call(
        functools.partial(scan_kernel, length, row_of, len(data)),
        name,
        [(d.shape, BF) for d in data]
        + [((tokens, inner), BF)] * 2
        + [((tokens, LANES), BF)] * 2
        + [((states + 8, inner), F32)],
        [plane] * 3
        + [flat] * 4
        + [maps] * 4
        + [(((length + 1) * states, GROUP * LANES), F32)] * 2
        + [eights] * 3
        + [((states, inner), F32)] * 2,
        VMEM_ALL,
        2e10,
        (order, place, *data, *params),
        smem=(0, 1),
        late=tuple(2 + len(data) + i for i in range(4)),
        early=tuple(range(len(data) + 5)),
    )
    return results[: len(data)], results[len(data) :]


def small_kernel(place_ref, own_ref, *refs):
    found, refs = [refs[5 * d : 5 * d + 5] for d in range(3)], refs[15:]
    mine_ref, other_ref, row_ref, turned_ref = refs
    inner = found[0][0].shape[1]
    tiles = inner // LANES
    tokens = own_ref.shape[2] // tiles
    states = found[0][4].shape[0] - 8
    rank = LANES - 2 * states
    row_ref[...] = own_ref[0, 0].astype(F32) * own_ref[0, 1].astype(F32)
    skips = jnp.concatenate(
        [
            jnp.sum(from_flat(row_ref, j, tokens, tiles), axis=0, keepdims=True)
            for j in range(tiles)
        ],
        axis=1,
    )
    x, grad_pre, low, grad_low = [
        jnp.concatenate([d[i][...] for d in found], axis=0) for i in range(4)
    ]
    summed = total([d[4][...] for d in found])
    at = lax.broadcasted_iota(jnp.int32, (LANES, inner), 0)
    vectors = jnp.concatenate(
        [jnp.zeros((rank, inner), F32), summed, jnp.zeros((states - 8, inner), F32)], axis=0
    )
    vectors = jnp.where(at > rank + states, 0.0, vectors) + jnp.where(
        at == rank + states + 1, jnp.broadcast_to(skips, at.shape), 0.0
    )
    turned_ref[0] = lax.dot_general(x, grad_low, TN, preferred_element_type=F32)
    turned_ref[1] = vectors.T + lax.dot_general(
        grad_pre, low, TN, preferred_element_type=F32
    )
    core = place_ref[0] & 1
    mine_ref[...] = turned_ref[core]
    other_ref[...] = turned_ref[1 - core].astype(BF)


def spread_rows(ref, which, own, near, held_ref):
    for m in range(near):
        for o in range(FAR_SIZE):
            begin = (o * near + m) * own
            at = (m * FAR_SIZE + o) * own
            held_ref[at : at + own, :] = ref[which, begin : begin + own, :]
    return held_ref[...].reshape(near, FAR_SIZE * own, LANES).astype(BF)


def post_kernel(
    send,
    place_ref,
    activ_ref,
    cot_ref,
    time_ref,
    wide_ref,
    slot_0_ref,
    slot_1_ref,
    slot_2_ref,
    slot_3_ref,
    pre_ref,
    skip_ref,
    mixed_out_ref,
    grad_act_ref,
    send_ref,
    sum_ref,
    turned_ref,
    held_ref,
):
    tokens, inner = pre_ref.shape
    tiles = inner // LANES
    flat_shape = (tokens * tiles, LANES)
    near = send_ref.shape[0]
    near_rows = inner // near
    own = near_rows // FAR_SIZE

    def summed(which, own_ref):
        sum_ref[...] = time_ref[0, which].astype(F32) + wide_ref[:, which].reshape(
            flat_shape
        ).astype(F32)
        for k, ref in enumerate((slot_0_ref, slot_1_ref, slot_2_ref, slot_3_ref)):
            chunk = ref.shape[2]
            at = pl.ds(pl.multiple_of((place_ref[0] ^ k) * chunk, chunk), chunk)
            sum_ref[at, :] += ref[0, which].astype(F32)
        scans = jnp.concatenate([from_flat(sum_ref, j, tokens, tiles) for j in range(tiles)], axis=1)
        return scans + skip_ref[...].reshape(1, inner) * own_ref[...].astype(F32)

    back = summed(1, cot_ref)
    pre_act = pre_ref[...]
    gate = jax.nn.sigmoid(pre_act)
    grad_act = (back * gate * (1.0 + pre_act * (1.0 - gate))).astype(BF)
    grad_act_ref[...] = grad_act
    send(1)
    turned_ref[1] = grad_act.astype(F32).T
    mixed = summed(0, activ_ref).astype(BF)
    mixed_out_ref[...] = mixed
    send(0)
    turned_ref[0] = mixed.astype(F32).T
    send_ref[:, :near_rows] = spread_rows(turned_ref, 0, own, near, held_ref)
    for m in range(near):
        send_ref[m, near_rows:] = turned_ref[1, pl.ds(m * near_rows, near_rows), :].astype(BF)


def finish_kernel(
    wait,
    mixed_ref,
    grad_act_ref,
    latent_ref,
    mod_ref,
    w_in_ref,
    w_out_ref,
    branch_ref,
    latent_grad_ref,
    vec_ref,
):
    tokens, width = latent_ref.shape
    normed, inverse = normalise(latent_ref[...])
    wait(4)
    grad_shifted = lax.dot_general(
        grad_act_ref[...], w_in_ref[...], NT, preferred_element_type=F32
    )
    grad_vec = jnp.concatenate(
        [
            jnp.sum(grad_shifted, axis=0, keepdims=True),
            jnp.sum(grad_shifted * normed, axis=0, keepdims=True),
        ],
        axis=1,
    )
    devices = vec_ref.shape[0]
    part = 2 * width // devices
    shape = (devices, 2 * width)
    block_at = lax.broadcasted_iota(jnp.int32, shape, 0) * part
    column_at = lax.broadcasted_iota(jnp.int32, shape, 1)
    mine = (column_at >= block_at) & (column_at < block_at + part)
    chosen = jnp.where(mine, jnp.broadcast_to(grad_vec, shape), 0.0)
    lane_at = lax.broadcasted_iota(jnp.int32, (2 * width, LANES), 1)
    place = lax.broadcasted_iota(jnp.int32, (2 * width, LANES), 0) % part
    choose = jnp.where(lane_at == place, 1.0, 0.0).astype(BF)
    vec_ref[...] = halves_product(chosen, choose, False)
    grad_normed = grad_shifted * (1.0 + mod_ref[:1, width:])
    product = jnp.mean(grad_normed * normed, axis=1, keepdims=True)
    result = inverse * (grad_normed - normed * product)
    latent_grad_ref[...] = result.reshape(latent_grad_ref.shape).astype(BF)
    wait(5)
    result = jnp.dot(mixed_ref[...], w_out_ref[...], preferred_element_type=F32)
    branch_ref[...] = result.reshape(branch_ref.shape).astype(BF)


def long_product(wait, at, left, right_ref):
    size = right_ref.shape[0] // PIECES
    tokens, width = right_ref.shape[1:]
    terms = []
    for n in range(PIECES):
        wait(at, n)
        rows = slice(n * size * tokens, (n + 1) * size * tokens)
        right = right_ref[n * size : (n + 1) * size].reshape(size * tokens, width)
        terms.append(jnp.dot(left[:, rows], right, preferred_element_type=F32))
    return total(terms)


def in_grad_kernel(
    wait, recv_ref, both_ref, mine_ref, other_ref, vec_ref, all_ref, right_ref, rows_ref
):
    near = recv_ref.shape[0]
    rows = right_ref.shape[0]
    width = both_ref.shape[2]
    devices = all_ref.shape[0]
    own = rows // FAR_SIZE
    for s in range(near):
        right_ref[:, cut(s)] = recv_ref[s, rows:]
    product = long_product(wait, 1, right_ref, both_ref)
    for n in (2, 3, 4):
        wait(n)
    mine_ref[...] += other_ref[...].astype(F32)
    turned = jnp.concatenate([product, jnp.zeros((LANES - rows, width), F32)], axis=0).T
    step = 2 * SLOT
    for d in range(devices):
        begin = d * step
        rows_ref[begin : begin + own, :] = turned[d * own : (d + 1) * own]
        rows_ref[begin + SLOT : begin + SLOT + own, :] = mine_ref[d * own : (d + 1) * own, :]
    for n in range(own, SLOT):
        rows_ref[pl.ds(n, devices, stride=step), :] = vec_ref[...]
        rows_ref[pl.ds(SLOT + n, devices, stride=step), :] = jnp.zeros((devices, LANES), F32)
    all_ref[...] = rows_ref[...].reshape(devices, step, LANES).astype(BF)


def pair_place(place, core_flip, slot):
    return place ^ ((slot // 2) * 4 + core_flip * 2 + slot % 2)


def out_grad_kernel(
    wait, place_ref, recv_ref, both_ref, mine_ref, other_ref, left_ref, out_ref, half_ref
):
    near = recv_ref.shape[0]
    rows = left_ref.shape[0]
    far = FAR_SIZE
    tiles = both_ref.shape[2] // LANES
    own = rows // far
    for s in range(near):
        left_ref[:, cut(s)] = recv_ref[s, :rows]
    product = long_product(wait, 2, left_ref, both_ref)
    for j in range(tiles):
        half_ref[...] = product[:, cut(j)]
        for o in range(far):
            out_ref[o, pl.ds(j, own, stride=tiles), :] = half_ref[o * own : (o + 1) * own, :]
    for slot in range(far // 2):
        mine_ref[slot] = out_ref[pair_place(place_ref[0], 0, slot)]
        other_ref[slot] = out_ref[pair_place(place_ref[0], 1, slot)].astype(BF)


def pair_sum_kernel(mine_ref, other_ref, kept_ref, *slot_refs):
    kept_ref[...] = mine_ref[0] + other_ref[0].astype(F32)
    for slot, ref in enumerate(slot_refs, 1):
        ref[...] = (mine_ref[slot] + other_ref[slot].astype(F32)).astype(BF)


def last_kernel(all_ref, feature_ref, *refs):
    far_refs = refs[: FAR_SIZE // 2]
    gwo_ref, gwi_ref, gsel_ref, gdt_ref, galog_ref, gvec_ref, gmod_ref, sum_ref, rest_ref = refs[
        FAR_SIZE // 2 :
    ]
    far = FAR_SIZE
    own, width = gwo_ref.shape
    tiles = width // LANES
    near = all_ref.shape[0] // far
    part = width // near
    sum_ref[...] = total([ref[...].astype(F32) for ref in far_refs])
    for j in range(tiles):
        gwo_ref[:, cut(j)] = sum_ref[pl.ds(j, own, stride=tiles), :]
    rest = []
    for m in range(near):
        cores = [
            total([all_ref[o * near + m].astype(F32) for o in range(far) if o // 2 % 2 == core])
            for core in (0, 1)
        ]
        gwi_ref[:, part * m : part * (m + 1)] = (cores[0] + cores[1])[:own, :part]
        rest.append(cores)
    rest_ref[: 2 * SLOT, :] = total([c[0] for c in rest])
    rest_ref[2 * SLOT :, :] = total([c[1] for c in rest])
    vec = rest_ref[own : own + 1, :] + rest_ref[2 * SLOT + own : 2 * SLOT + own + 1, :]
    turned = jnp.broadcast_to(vec, (LANES, LANES)).T
    gmod_ref[...] = turned[: 2 * own, :1] * feature_ref[...].reshape(1, -1).astype(F32)
    gsel_ref[...] = rest_ref[SLOT : SLOT + own, :]
    rank, states = gdt_ref.shape[1], galog_ref.shape[1]
    base = 3 * SLOT
    gdt_ref[...] = rest_ref[base : base + own, :rank]
    galog_ref[...] = rest_ref[base : base + own, rank : rank + states]
    turned = jnp.concatenate([rest_ref[base : base + own, :], jnp.zeros((LANES - own, LANES), F32)])
    gvec_ref[...] = turned.T[rank + states : rank + states + 8, :own]


def permute(value, axes, k):
    if k == 0:
        return value
    return lax.ppermute(value, axes, [(i, i ^ k) for i in range(lax.axis_size(axes))])


def exchange(value, axes):
    return lax.all_to_all(value, axes, split_axis=0, concat_axis=0, tiled=True)


def local(
    latent,
    out_grad,
    w_in,
    w_out,
    w_select,
    w_dt,
    dt_bias,
    a_log,
    d_skip,
    w_mod,
    t_index,
    frame_order,
    row_order,
    col_order,
):
    frames, rows, cols, width = latent.shape
    inner = w_in.shape[1]
    tokens = frames * rows * cols
    tiles = inner // LANES
    states = a_log.shape[1]
    n_row, n_col = lax.axis_size(ROW), lax.axis_size(COL)
    near, far = lax.axis_size(NEAR), lax.axis_size(FAR)
    own = width // (near * far)
    features = jax.nn.silu(time_features(t_index, w_mod.shape[1])).astype(BF)

    def packed(parts):
        return ((parts, 2, tokens * tiles // parts, LANES), BF)

    slot = ((1, 2, tokens * tiles // n_row, LANES), BF)
    place = lax.axis_index(ROW).astype(jnp.int32)[None]
    far_place = lax.axis_index(FAR).astype(jnp.int32)[None]
    data_own, data_wide, *slots, both, pre_act, modulation, cot, flat_latent = call(
        pre_kernel,
        "norm_project",
        [
            packed(1),
            packed(n_col),
            slot,
            slot,
            slot,
            slot,
            ((2, tokens, width), BF),
            ((tokens, inner), F32),
            ((8, 2 * width), F32),
            ((tokens, inner), BF),
            ((tokens, width), BF),
        ],
        [((tokens * tiles, LANES), F32)],
        VMEM_ALL,
        7e9,
        (place, w_mod, features, latent, w_in, out_grad, w_out),
        smem=(0,),
        late=(3, 4, 5, 6),
        early=tuple(range(11)),
    )
    data_wide = exchange(data_wide, COL)
    slots = [permute(value, ROW, k) for k, value in enumerate(slots)]
    both_near = lax.all_gather(both, NEAR, axis=0, tiled=False)
    params = (
        w_select,
        w_dt.T,
        dt_bias,
        a_log.T,
    )
    area = rows * cols

    def time_row(at, line, place):
        return at * area + line

    def wide_row(at, line, place):
        chunk = frames // n_col * area
        return (
            lax.div(at, cols) * chunk
            + lax.rem(at, cols)
            + lax.div(line, rows) * area
            + lax.rem(line, rows) * cols
        )

    def tall_row(at, line, place):
        chunk = frames // n_row * area
        return (
            (lax.div(at, rows) ^ place) * chunk
            + lax.rem(at, rows) * cols
            + lax.div(line, cols) * area
            + lax.rem(line, cols)
        )

    out_tall, grads_tall = direction(
        "scan_height", rows * n_row, tall_row, row_order, place, slots, params
    )
    out_slots = [permute(value, ROW, k) for k, value in enumerate(out_tall)]
    data_wide, _ = lax.optimization_barrier((data_wide, out_tall))
    (out_wide,), grads_wide = direction(
        "scan_width", cols * n_col, wide_row, col_order, place, [data_wide], params
    )
    data_time, out_slots, _ = lax.optimization_barrier((data_own, out_slots, out_wide))
    out_wide = exchange(out_wide, COL)
    (out_time,), grads_time = direction(
        "scan_time", frames, time_row, frame_order, place, [data_time], params
    )
    mixed, grad_act, near_send = call(
        post_kernel,
        "sum_directions",
        [
            ((tokens, inner), BF),
            ((tokens, inner), BF),
            ((near, 2 * inner // near, LANES), BF),
        ],
        [
            ((tokens * tiles, LANES), F32),
            ((2, inner, LANES), F32),
            ((inner, LANES), F32),
        ],
        VMEM_ALL,
        6e9,
        (place, grads_time[0], cot, out_time, out_wide, *out_slots, pre_act, d_skip),
        smem=(0,),
        early=(0, 1),
    )
    near_recv = exchange(near_send, NEAR)
    data_own, _ = lax.optimization_barrier((data_own, near_send))
    mine, other = call(
        small_kernel,
        "small_sums",
        [((inner, LANES), F32), ((inner, LANES), BF)],
        [((tokens * tiles, LANES), F32), ((2, inner, LANES), F32)],
        VMEM_ALL,
        3e9,
        (place, data_own, *grads_time, *grads_wide, *grads_tall),
        smem=(0,),
    )
    other = permute(other, ROW, 1)
    branch, latent_grad, vec = call(
        finish_kernel,
        "out_projections",
        [(latent.shape, BF), (latent.shape, BF), ((near * far, LANES), F32)],
        [],
        VMEM_ALL,
        6e9,
        (mixed, grad_act, flat_latent, modulation, w_in, w_out),
        late=(4, 5),
    )
    near_recv, vec, mine, other = lax.optimization_barrier((near_recv, vec, mine, other))
    piece = own * tiles
    all_send = call(
        in_grad_kernel,
        "in_weight_grad",
        [((near * far, 2 * SLOT, LANES), BF)],
        [((inner // near, near * tokens), BF), ((near * far * 2 * SLOT, LANES), F32)],
        VMEM_ALL,
        3e9,
        (near_recv, both_near, mine, other, vec),
        late=(1, 2, 3, 4),
        pieces={1: PIECES},
        choose={1: 0},
    )[0]
    all_recv = exchange(all_send, FAR + NEAR)
    mine, other = call(
        out_grad_kernel,
        "out_weight_grad",
        [((far // 2, piece, LANES), F32), ((far // 2, piece, LANES), BF)],
        [
            ((inner // near, near * tokens), BF),
            ((far, piece, LANES), F32),
            ((inner // near, LANES), F32),
        ],
        VMEM_ALL,
        4e9,
        (far_place, near_recv, both_near),
        smem=(0,),
        late=(2,),
        pieces={2: PIECES},
        choose={2: 1},
    )
    other = permute(other, FAR, 2)
    far_send = plain_call(
        pair_sum_kernel,
        "pair_sums",
        [((piece, LANES), F32)] + [((piece, LANES), BF)] * (far // 2 - 1),
        [],
        8,
        1e9,
        (mine, other),
    )
    far_recv = [permute(value, FAR, (0, 1, 4, 5)[slot]) for slot, value in enumerate(far_send)]
    rank = w_dt.shape[1]
    grad_w_out, grad_w_in, grad_select, grad_dt, grad_alog, grad_vec, grad_mod = plain_call(
        last_kernel,
        "weight_sums",
        [
            ((own, width), F32),
            ((own, width), F32),
            ((own, LANES), F32),
            ((own, rank), F32),
            ((own, states), F32),
            ((8, own), F32),
            ((2 * own, features.shape[0]), F32),
        ],
        [((piece, LANES), F32), ((4 * SLOT, LANES), F32)],
        16,
        1e9,
        (all_recv, features, *far_recv),
    )
    return (
        branch,
        latent_grad,
        grad_w_in,
        grad_w_out,
        grad_select,
        grad_dt,
        grad_vec[0],
        grad_alog,
        grad_vec[1],
        grad_mod,
    )


def solution(mesh):
    n_row, n_col = mesh.shape["row"], mesh.shape["col"]
    split = Mesh(mesh.devices.reshape(n_row // 2, 2, 2, 4, n_col // 8), AXES)
    tokens = P(None, ROW, COL, None)
    matrix = P(ROW + COL, None)
    vector = P(ROW + COL)
    return jax.shard_map(
        local,
        mesh=split,
        in_specs=(tokens, tokens) + (P(),) * 12,
        out_specs=(
            tokens,
            tokens,
            matrix,
            matrix,
            matrix,
            matrix,
            vector,
            matrix,
            vector,
            matrix,
        ),
        check_vma=False,
    )
```

```python
import functools
import math

import jax
import jax.numpy as jnp
from jax import lax
from jax.experimental import pallas as pl
from jax.experimental.pallas import tpu as pltpu
from jax.sharding import Mesh
from jax.sharding import PartitionSpec as P

BF = jnp.bfloat16
F32 = jnp.float32
LANES = 128
GROUP = 6
EIGHT = 9
LOG2E = math.log2(math.e)
MEGA = 1024 * 1024
VMEM_ALL = 60
PIECES = 8
SLOT = 16
AXES = ("xl", "core", "xh", "y", "z")
ROW = ("xl", "core")
COL = ("xh", "y", "z")
NEAR = ("y", "z")
FAR = ("xl", "core", "xh")
FAR_SIZE = 8
NT = (((1,), (1,)), ((), ()))
TN = (((0,), (0,)), ((), ()))


def time_features(step_index, width):
    halfway = width // 2
    frequency = jnp.exp(-math.log(10000.0) * jnp.arange(halfway, dtype=jnp.float32) / halfway)
    angles = step_index.astype(jnp.float32)[0] * frequency
    return jnp.concatenate([jnp.cos(angles), jnp.sin(angles)])


def total(terms):
    return functools.reduce(lambda a, b: a + b, terms)


def call(kernel, name, out_shape, scratch, vmem, flops, args, smem=(), late=(), pieces=None, choose=None, early=()):
    moved = [i for i in range(len(args)) if i not in smem]
    pieces, choose = pieces or {}, choose or {}
    held_shape = {
        i: args[i].shape[:1] + args[i].shape[2:] if i in choose else args[i].shape for i in moved
    }
    cuts = []
    for i in moved:
        size = args[i].shape[0] // pieces.get(i, 1)
        cuts += [(i, n, pl.ds(n * size, size)) for n in range(pieces.get(i, 1))]

    def body(*refs):
        given, out = refs[: len(args)], refs[len(args) : len(args) + len(out_shape)]
        rest = refs[len(args) + len(out_shape) :]
        held, rest = rest[: len(moved)], rest[len(moved) :]
        made, rest = rest[: len(out_shape)], rest[len(out_shape) :]
        in_sem, out_sem = rest[-2:]
        views = [given[i] if i in smem else held[moved.index(i)] for i in range(len(args))]
        copies = {
            (i, n): pltpu.make_async_copy(
                given[i].at[at, choose[i]] if i in choose else given[i].at[at],
                views[i].at[at],
                in_sem.at[place],
            )
            for place, (i, n, at) in enumerate(cuts)
        }
        for copy in copies.values():
            copy.start()
        for (i, _), copy in copies.items():
            if i not in late:
                copy.wait()
        waits = (lambda i, n=0: copies[i, n].wait(),) if late else ()
        sent = []

        def send(n, plane=None):
            at = (slice(None), plane) if plane is not None else (slice(None),)
            place = 2 * n + (plane or 0)
            copy = pltpu.make_async_copy(made[n].at[at], out[n].at[at], out_sem.at[place])
            copy.start()
            sent.append(copy)

        kernel(*waits, *((send,) if early else ()), *views, *made, *rest[:-2])
        for n in range(len(out_shape)):
            if n not in early:
                send(n)
        for copy in sent:
            copy.wait()

    spaces = [
        pl.BlockSpec(memory_space=pltpu.SMEM if i in smem else pltpu.HBM) for i in range(len(args))
    ]
    return pl.pallas_call(
        body,
        out_shape=tuple(jax.ShapeDtypeStruct(s, d) for s, d in out_shape),
        in_specs=spaces,
        out_specs=(pl.BlockSpec(memory_space=pltpu.HBM),) * len(out_shape),
        scratch_shapes=[pltpu.VMEM(held_shape[i], args[i].dtype) for i in moved]
        + [pltpu.VMEM(s, d) for s, d in out_shape]
        + [pltpu.VMEM(s, d) for s, d in scratch]
        + [pltpu.SemaphoreType.DMA((len(cuts),)), pltpu.SemaphoreType.DMA((2 * len(out_shape),))],
        compiler_params=pltpu.CompilerParams(vmem_limit_bytes=vmem * MEGA),
        cost_estimate=cost(flops, args),
        name=name,
    )(*args)


def cost(flops, args):
    return pl.CostEstimate(
        flops=int(flops),
        bytes_accessed=sum(a.size * a.dtype.itemsize for a in args),
        transcendentals=0,
    )


def plain_call(kernel, name, out_shape, scratch, vmem, flops, args, smem=()):
    spaces = [
        pl.BlockSpec(memory_space=pltpu.SMEM if i in smem else pltpu.VMEM) for i in range(len(args))
    ]
    return pl.pallas_call(
        kernel,
        out_shape=tuple(jax.ShapeDtypeStruct(s, d) for s, d in out_shape),
        in_specs=spaces,
        out_specs=(pl.BlockSpec(memory_space=pltpu.VMEM),) * len(out_shape),
        scratch_shapes=[pltpu.VMEM(s, d) for s, d in scratch],
        compiler_params=pltpu.CompilerParams(vmem_limit_bytes=vmem * MEGA),
        cost_estimate=cost(flops, args),
        name=name,
    )(*args)


def cut(j):
    return slice(LANES * j, LANES * j + LANES)


def to_flat(ref, j, value, tiles):
    ref[pl.ds(j, value.shape[0], stride=tiles), :] = value


def from_flat(ref, j, tokens, tiles):
    return ref[pl.ds(j, tokens, stride=tiles), :]


def normalise(latent):
    wide = latent.astype(F32)
    inverse = lax.rsqrt(jnp.mean(wide * wide, axis=-1, keepdims=True) + 1e-06)
    return wide * inverse, inverse


def pre_kernel(
    wait,
    send,
    place_ref,
    w_mod_ref,
    feature_ref,
    latent_ref,
    w_in_ref,
    grad_ref,
    w_out_ref,
    own_ref,
    wide_ref,
    slot_0_ref,
    slot_1_ref,
    slot_2_ref,
    slot_3_ref,
    both_ref,
    pre_ref,
    mod_ref,
    cot_ref,
    rows_ref,
    flat_ref,
):
    tokens, width = rows_ref.shape
    tiles = w_in_ref.shape[1] // LANES
    modulation = lax.dot_general(
        jnp.broadcast_to(feature_ref[...].reshape(1, -1), (8, feature_ref.shape[0])),
        w_mod_ref[...],
        NT,
        preferred_element_type=F32,
    )
    mod_ref[...] = modulation
    send(8)
    wait(3)
    latent = latent_ref[...].astype(F32).reshape(tokens, width)
    rows_ref[...] = latent.astype(BF)
    send(10)
    normed, _ = normalise(latent)
    shifted = (normed * (1.0 + modulation[:1, width:]) + modulation[:1, :width]).astype(BF)
    both_ref[0] = shifted
    wait(4)
    pre_act = jnp.dot(shifted, w_in_ref[...], preferred_element_type=F32)
    pre_ref[...] = pre_act
    send(7)
    wait(5)
    both_ref[1] = grad_ref[...].astype(F32).reshape(tokens, width).astype(BF)
    send(6)
    activ = (pre_act * jax.nn.sigmoid(pre_act)).astype(BF)

    def pack(which, value):
        wide = value.astype(F32)
        for j in range(tiles):
            to_flat(flat_ref, j, wide[:, cut(j)], tiles)
        flat = flat_ref[...].astype(BF)
        own_ref[0, which] = flat
        wide_ref[:, which] = flat.reshape(wide_ref.shape[0], wide_ref.shape[2], LANES)
        for k, ref in enumerate((slot_0_ref, slot_1_ref, slot_2_ref, slot_3_ref)):
            chunk = ref.shape[2]
            begin = pl.multiple_of((place_ref[0] ^ k) * chunk, chunk)
            ref[0, which] = flat_ref[pl.ds(begin, chunk), :].astype(BF)
        for n in range(6):
            send(n, which)

    pack(0, activ)
    wait(6)
    cot = lax.dot_general(both_ref[1], w_out_ref[...], NT, preferred_element_type=F32).astype(BF)
    cot_ref[...] = cot
    send(9)
    pack(1, cot)


def parts_of(refs):
    begin, found = 0, []
    for ref in refs:
        size = ref.shape[0] * ref.shape[2]
        found.append((ref, slice(begin, begin + size)))
        begin += size
    return found


def read_part(ref, which):
    return ref[:, which].reshape(ref.shape[0] * ref.shape[2], LANES).astype(F32)


def write_part(ref, which, value):
    ref[:, which] = value.astype(BF).reshape(ref.shape[0], ref.shape[2], LANES)


def scan_kernel(
    length,
    row_of,
    pieces,
    wait,
    send,
    order_ref,
    place_ref,
    *refs,
):
    data_refs, out_refs = refs[:pieces], refs[pieces + 4 : 2 * pieces + 4]
    scan_steps(
        length,
        row_of,
        order_ref,
        place_ref,
        data_refs,
        *refs[pieces : pieces + 4],
        out_refs,
        *refs[2 * pieces + 4 :],
        functools.partial(wait_for, wait, 2 + pieces),
        functools.partial(send_from, send, pieces),
    )


def wait_for(wait, first, n):
    wait(first + n)


def send_from(send, pieces, n):
    if n < 2:
        for k in range(pieces):
            send(k, n)
    else:
        send(pieces + n - 2)


def scan_steps(
    length,
    row_of,
    order_ref,
    place_ref,
    data_refs,
    wsel_ref,
    wdt_ref,
    bias_ref,
    alog_ref,
    out_refs,
    x_ref,
    grad_pre_ref,
    low_ref,
    grad_low_ref,
    gvec_ref,
    pre_ref,
    dt_ref,
    xf_ref,
    x_row_ref,
    dt_row_ref,
    dx_row_ref,
    dy_row_ref,
    bb_ref,
    cb_ref,
    gb_ref,
    gc_ref,
    hist_ref,
    keep_ref,
    y8_ref,
    u8_ref,
    v8_ref,
    rate2_ref,
    rate_ref,
    wait,
    send,
):
    tokens, inner = xf_ref.shape
    tiles = inner // LANES
    lines = tokens // length
    states = alog_ref.shape[0]
    rank = LANES - 2 * states
    for ref, at in parts_of(data_refs):
        x_row_ref[at, :] = read_part(ref, 0)
        dy_row_ref[at, :] = read_part(ref, 1)
    for j in range(tiles):
        xf_ref[:, cut(j)] = from_flat(x_row_ref, j, tokens, tiles)
    x = xf_ref[...].astype(BF)
    x_ref[...] = x
    send(2)
    wait(0)
    select = jnp.dot(x, wsel_ref[...], preferred_element_type=F32)
    lane = lax.broadcasted_iota(jnp.int32, (tokens, LANES), 1)
    low = jnp.where(lane < rank, select, 0.0).astype(BF)
    low_ref[...] = low
    send(4)
    wait(1)
    wait(2)
    w_dt = jnp.concatenate([wdt_ref[...], jnp.zeros((2 * states, inner), BF)], axis=0)
    pre = jnp.dot(low, w_dt, preferred_element_type=F32) + bias_ref[...].reshape(1, inner)
    pre_ref[...] = pre
    spacing = jnp.maximum(pre, 0.0) + jnp.log1p(jnp.exp(-jnp.abs(pre)))
    dt_ref[...] = spacing
    for j in range(tiles):
        at = slice(j * tokens, (j + 1) * tokens)
        dt_row_ref[at, :] = spacing[:, cut(j)]
        dx_row_ref[at, :] = spacing[:, cut(j)] * xf_ref[:, cut(j)]
    wait(3)
    rates = -jnp.exp(alog_ref[...])
    rate_ref[...] = rates
    rate2_ref[...] = rates * LOG2E
    turned = select.T
    for token in range(tokens):
        at = pl.ds(token * states, states)
        column = slice(token, token + 1)
        bb_ref[at, :] = jnp.broadcast_to(turned[rank : rank + states, column], (states, LANES))
        cb_ref[at, :] = jnp.broadcast_to(turned[rank + states :, column], (states, LANES))
    gb_ref[...] = jnp.zeros_like(gb_ref)
    gc_ref[...] = jnp.zeros_like(gc_ref)
    zero = jnp.zeros((states, LANES), F32)
    hist_ref[pl.ds(0, states), :] = jnp.zeros((states, GROUP * LANES), F32)
    unroll = min(length, 8)

    def repeat(step, carry):
        def block(n, carry):
            for inside in range(unroll):
                carry = step(n, inside, carry)
            return carry

        if length == unroll:
            return block(0, carry)
        return lax.fori_loop(0, length // unroll, block, carry)

    def fold(value):
        return value[:8] + value[8:]

    for group in range(tiles // GROUP):
        first = group * GROUP
        cuts = [cut(first + j) for j in range(GROUP)]
        rate2 = [rate2_ref[:, c] for c in cuts]
        rate1 = [rate_ref[:, c] for c in cuts]

        def one_line(line, grads):
            def places(block, inside):
                row = row_of(order_ref[block * unroll + inside], line, place_ref[0])
                at = pl.ds(pl.multiple_of(row * states, states), states)
                base = pl.multiple_of(block * (unroll * states), unroll * states)
                slot = pl.ds(base + (inside + 1) * states, states)
                prev = pl.ds(base + inside * states, states)
                return row, row * EIGHT, at, slot, prev

            def forward(block, inside, carry):
                row, at_8, at, slot, _ = places(block, inside)
                bb, cb = bb_ref[at, :], cb_ref[at, :]
                new = []
                for j in range(GROUP):
                    dt = dt_row_ref[pl.ds(row + (first + j) * tokens, 1), :]
                    dx = dx_row_ref[pl.ds(row + (first + j) * tokens, 1), :]
                    decay = jnp.exp2(rate2[j] * dt)
                    keep_ref[slot, cut(j)] = decay
                    h = decay * carry[j] + bb * dx
                    hist_ref[slot, cut(j)] = h
                    y8_ref[pl.ds(at_8 + EIGHT * tokens * j, 8), :] = fold(h * cb)
                    new.append(h)
                return tuple(new)

            repeat(forward, (zero,) * GROUP)

            def backward(block, inside, carry):
                last = length // unroll - 1
                row, at_8, at, slot, prev = places(last - block, unroll - 1 - inside)
                bb, cb = bb_ref[at, :], cb_ref[at, :]
                pend, acc = carry
                gb = gb_ref[at, :]
                gc = gc_ref[at, :]
                new, acc_new = [], []
                for j in range(GROUP):
                    dt = dt_row_ref[pl.ds(row + (first + j) * tokens, 1), :]
                    dx = dx_row_ref[pl.ds(row + (first + j) * tokens, 1), :]
                    dy = dy_row_ref[pl.ds(row * tiles + first + j, 1), :]
                    g = pend[j] + cb * dy
                    gc = gc + hist_ref[slot, cut(j)] * dy
                    u8_ref[pl.ds(at_8 + EIGHT * tokens * j, 8), :] = fold(g * bb)
                    gb = gb + g * dx
                    p = keep_ref[slot, cut(j)] * g
                    w = p * hist_ref[prev, cut(j)]
                    v8_ref[pl.ds(at_8 + EIGHT * tokens * j, 8), :] = fold(w * rate1[j])
                    acc_new.append(acc[j] + w * dt)
                    new.append(p)
                gb_ref[at, :] = gb
                gc_ref[at, :] = gc
                return tuple(new), tuple(acc_new)

            start = ((zero,) * GROUP, grads)
            return repeat(backward, start)[1]

        grads = lax.fori_loop(0, lines, one_line, (zero,) * GROUP)
        for j in range(GROUP):
            gvec_ref[:states, cuts[j]] = grads[j] * rate1[j]

        def gather(block, carry):
            rows = pl.ds(pl.multiple_of(block * 8, 8), 8)

            def summed(ref, j):
                begin = block * (8 * EIGHT) + EIGHT * tokens * j
                return total([ref[pl.ds(begin + r, 8, stride=EIGHT), :] for r in range(8)])

            for j in range(GROUP):
                c = cuts[j]
                u = summed(u8_ref, j)
                x_row_ref[pl.ds(block * 8 * tiles + first + j, 8, stride=tiles), :] = summed(y8_ref, j)
                grad_spacing = summed(v8_ref, j) + xf_ref[rows, c] * u
                pre_ref[rows, c] = grad_spacing * jax.nn.sigmoid(pre_ref[rows, c])
                dt_ref[rows, c] = dt_ref[rows, c] * u
            return carry

        lax.fori_loop(0, tokens // 8, gather, 0, unroll=2)

    for ref, at in parts_of(out_refs):
        write_part(ref, 0, x_row_ref[at, :])
    send(0)
    grad_pre = pre_ref[...]
    gvec_ref[states:, :] = jnp.broadcast_to(
        jnp.sum(grad_pre, axis=0, keepdims=True), (8, inner)
    )
    send(6)
    grad_pre_b = grad_pre.astype(BF)
    grad_pre_ref[...] = grad_pre_b
    send(3)
    shape = (2 * LANES, LANES)
    half = lax.broadcasted_iota(jnp.int32, shape, 0) // LANES
    lane_at = lax.broadcasted_iota(jnp.int32, shape, 1)
    spread = jnp.where((lane_at - rank) // states == half, 1.0, 0.0).astype(BF)
    shape = (tokens * states, LANES)
    state_at = lax.broadcasted_iota(jnp.int32, shape, 0) % states
    lane_at = lax.broadcasted_iota(jnp.int32, shape, 1)
    both = jnp.concatenate([gb_ref[...], gc_ref[...]], axis=1)
    lanes = halves_product(both, spread, False)
    kept = jnp.where((lane_at >= rank) & ((lane_at - rank) % states == state_at), lanes, 0.0)
    shape = (tokens, tokens * states)
    collect = lax.broadcasted_iota(jnp.int32, shape, 1) // states == lax.broadcasted_iota(
        jnp.int32, shape, 0
    )
    grad_maps = halves_product(kept, jnp.where(collect, 1.0, 0.0).astype(BF), True)
    grad_low = lax.dot_general(grad_pre_b, w_dt, NT, preferred_element_type=F32)
    grad_select_out = (grad_low + grad_maps).astype(BF)
    grad_low_ref[...] = grad_select_out
    send(5)
    back = dt_ref[...] + lax.dot_general(
        grad_select_out, wsel_ref[...], NT, preferred_element_type=F32
    )
    for j in range(tiles):
        to_flat(dy_row_ref, j, back[:, cut(j)], tiles)
    for ref, at in parts_of(out_refs):
        write_part(ref, 1, dy_row_ref[at, :])
    send(1)


def halves_product(value, other, other_first):
    top = value.astype(BF)
    rest = (value - top.astype(F32)).astype(BF)
    if other_first:
        return jnp.dot(other, top, preferred_element_type=F32) + jnp.dot(
            other, rest, preferred_element_type=F32
        )
    return jnp.dot(top, other, preferred_element_type=F32) + jnp.dot(
        rest, other, preferred_element_type=F32
    )


def direction(name, length, row_of, order, place, data, params):
    inner = params[0].shape[0]
    tiles = inner // LANES
    tokens = sum(d.shape[0] * d.shape[2] for d in data) // tiles
    states = params[3].shape[0]
    plane = ((tokens, inner), F32)
    flat = ((tokens * tiles, LANES), F32)
    maps = ((tokens * states, LANES), F32)
    eights = ((tokens * EIGHT * GROUP, LANES), F32)
    results = call(
        functools.partial(scan_kernel, length, row_of, len(data)),
        name,
        [(d.shape, BF) for d in data]
        + [((tokens, inner), BF)] * 2
        + [((tokens, LANES), BF)] * 2
        + [((states + 8, inner), F32)],
        [plane] * 3
        + [flat] * 4
        + [maps] * 4
        + [(((length + 1) * states, GROUP * LANES), F32)] * 2
        + [eights] * 3
        + [((states, inner), F32)] * 2,
        VMEM_ALL,
        2e10,
        (order, place, *data, *params),
        smem=(0, 1),
        late=tuple(2 + len(data) + i for i in range(4)),
        early=tuple(range(len(data) + 5)),
    )
    return results[: len(data)], results[len(data) :]


def small_kernel(place_ref, own_ref, *refs):
    found, refs = [refs[5 * d : 5 * d + 5] for d in range(3)], refs[15:]
    mine_ref, other_ref, row_ref, turned_ref = refs
    inner = found[0][0].shape[1]
    tiles = inner // LANES
    tokens = own_ref.shape[2] // tiles
    states = found[0][4].shape[0] - 8
    rank = LANES - 2 * states
    row_ref[...] = own_ref[0, 0].astype(F32) * own_ref[0, 1].astype(F32)
    skips = jnp.concatenate(
        [
            jnp.sum(from_flat(row_ref, j, tokens, tiles), axis=0, keepdims=True)
            for j in range(tiles)
        ],
        axis=1,
    )
    x, grad_pre, low, grad_low = [
        jnp.concatenate([d[i][...] for d in found], axis=0) for i in range(4)
    ]
    summed = total([d[4][...] for d in found])
    at = lax.broadcasted_iota(jnp.int32, (LANES, inner), 0)
    vectors = jnp.concatenate(
        [jnp.zeros((rank, inner), F32), summed, jnp.zeros((states - 8, inner), F32)], axis=0
    )
    vectors = jnp.where(at > rank + states, 0.0, vectors) + jnp.where(
        at == rank + states + 1, jnp.broadcast_to(skips, at.shape), 0.0
    )
    turned_ref[0] = lax.dot_general(x, grad_low, TN, preferred_element_type=F32)
    turned_ref[1] = vectors.T + lax.dot_general(
        grad_pre, low, TN, preferred_element_type=F32
    )
    core = place_ref[0] & 1
    mine_ref[...] = turned_ref[core]
    other_ref[...] = turned_ref[1 - core].astype(BF)


def spread_rows(ref, which, own, near, held_ref):
    for m in range(near):
        for o in range(FAR_SIZE):
            begin = (o * near + m) * own
            at = (m * FAR_SIZE + o) * own
            held_ref[at : at + own, :] = ref[which, begin : begin + own, :]
    return held_ref[...].reshape(near, FAR_SIZE * own, LANES).astype(BF)


def post_kernel(
    send,
    place_ref,
    activ_ref,
    cot_ref,
    time_ref,
    wide_ref,
    slot_0_ref,
    slot_1_ref,
    slot_2_ref,
    slot_3_ref,
    pre_ref,
    skip_ref,
    mixed_out_ref,
    grad_act_ref,
    send_ref,
    sum_ref,
    turned_ref,
    held_ref,
):
    tokens, inner = pre_ref.shape
    tiles = inner // LANES
    flat_shape = (tokens * tiles, LANES)
    near = send_ref.shape[0]
    near_rows = inner // near
    own = near_rows // FAR_SIZE

    def summed(which, own_ref):
        sum_ref[...] = time_ref[0, which].astype(F32) + wide_ref[:, which].reshape(
            flat_shape
        ).astype(F32)
        for k, ref in enumerate((slot_0_ref, slot_1_ref, slot_2_ref, slot_3_ref)):
            chunk = ref.shape[2]
            at = pl.ds(pl.multiple_of((place_ref[0] ^ k) * chunk, chunk), chunk)
            sum_ref[at, :] += ref[0, which].astype(F32)
        scans = jnp.concatenate([from_flat(sum_ref, j, tokens, tiles) for j in range(tiles)], axis=1)
        return scans + skip_ref[...].reshape(1, inner) * own_ref[...].astype(F32)

    back = summed(1, cot_ref)
    pre_act = pre_ref[...]
    gate = jax.nn.sigmoid(pre_act)
    grad_act = (back * gate * (1.0 + pre_act * (1.0 - gate))).astype(BF)
    grad_act_ref[...] = grad_act
    send(1)
    turned_ref[1] = grad_act.astype(F32).T
    mixed = summed(0, activ_ref).astype(BF)
    mixed_out_ref[...] = mixed
    send(0)
    turned_ref[0] = mixed.astype(F32).T
    send_ref[:, :near_rows] = spread_rows(turned_ref, 0, own, near, held_ref)
    for m in range(near):
        send_ref[m, near_rows:] = turned_ref[1, pl.ds(m * near_rows, near_rows), :].astype(BF)


def finish_kernel(
    wait,
    mixed_ref,
    grad_act_ref,
    latent_ref,
    mod_ref,
    w_in_ref,
    w_out_ref,
    branch_ref,
    latent_grad_ref,
    vec_ref,
):
    tokens, width = latent_ref.shape
    normed, inverse = normalise(latent_ref[...])
    wait(4)
    grad_shifted = lax.dot_general(
        grad_act_ref[...], w_in_ref[...], NT, preferred_element_type=F32
    )
    grad_vec = jnp.concatenate(
        [
            jnp.sum(grad_shifted, axis=0, keepdims=True),
            jnp.sum(grad_shifted * normed, axis=0, keepdims=True),
        ],
        axis=1,
    )
    devices = vec_ref.shape[0]
    part = 2 * width // devices
    shape = (devices, 2 * width)
    block_at = lax.broadcasted_iota(jnp.int32, shape, 0) * part
    column_at = lax.broadcasted_iota(jnp.int32, shape, 1)
    mine = (column_at >= block_at) & (column_at < block_at + part)
    chosen = jnp.where(mine, jnp.broadcast_to(grad_vec, shape), 0.0)
    lane_at = lax.broadcasted_iota(jnp.int32, (2 * width, LANES), 1)
    place = lax.broadcasted_iota(jnp.int32, (2 * width, LANES), 0) % part
    choose = jnp.where(lane_at == place, 1.0, 0.0).astype(BF)
    vec_ref[...] = halves_product(chosen, choose, False)
    grad_normed = grad_shifted * (1.0 + mod_ref[:1, width:])
    product = jnp.mean(grad_normed * normed, axis=1, keepdims=True)
    result = inverse * (grad_normed - normed * product)
    latent_grad_ref[...] = result.reshape(latent_grad_ref.shape).astype(BF)
    wait(5)
    result = jnp.dot(mixed_ref[...], w_out_ref[...], preferred_element_type=F32)
    branch_ref[...] = result.reshape(branch_ref.shape).astype(BF)


def long_product(wait, at, left, right_ref):
    size = right_ref.shape[0] // PIECES
    tokens, width = right_ref.shape[1:]
    terms = []
    for n in range(PIECES):
        wait(at, n)
        rows = slice(n * size * tokens, (n + 1) * size * tokens)
        right = right_ref[n * size : (n + 1) * size].reshape(size * tokens, width)
        terms.append(jnp.dot(left[:, rows], right, preferred_element_type=F32))
    return total(terms)


def in_grad_kernel(
    wait, recv_ref, both_ref, mine_ref, other_ref, vec_ref, all_ref, right_ref, rows_ref
):
    near = recv_ref.shape[0]
    rows = right_ref.shape[0]
    width = both_ref.shape[2]
    devices = all_ref.shape[0]
    own = rows // FAR_SIZE
    for s in range(near):
        right_ref[:, cut(s)] = recv_ref[s, rows:]
    product = long_product(wait, 1, right_ref, both_ref)
    for n in (2, 3, 4):
        wait(n)
    mine_ref[...] += other_ref[...].astype(F32)
    turned = jnp.concatenate([product, jnp.zeros((LANES - rows, width), F32)], axis=0).T
    step = 2 * SLOT
    for d in range(devices):
        begin = d * step
        rows_ref[begin : begin + own, :] = turned[d * own : (d + 1) * own]
        rows_ref[begin + SLOT : begin + SLOT + own, :] = mine_ref[d * own : (d + 1) * own, :]
    for n in range(own, SLOT):
        rows_ref[pl.ds(n, devices, stride=step), :] = vec_ref[...]
        rows_ref[pl.ds(SLOT + n, devices, stride=step), :] = jnp.zeros((devices, LANES), F32)
    all_ref[...] = rows_ref[...].reshape(devices, step, LANES).astype(BF)


def pair_place(place, core_flip, slot):
    return place ^ ((slot // 2) * 4 + core_flip * 2 + slot % 2)


def out_grad_kernel(
    wait, place_ref, recv_ref, both_ref, mine_ref, other_ref, left_ref, out_ref, half_ref
):
    near = recv_ref.shape[0]
    rows = left_ref.shape[0]
    far = FAR_SIZE
    tiles = both_ref.shape[2] // LANES
    own = rows // far
    for s in range(near):
        left_ref[:, cut(s)] = recv_ref[s, :rows]
    product = long_product(wait, 2, left_ref, both_ref)
    for j in range(tiles):
        half_ref[...] = product[:, cut(j)]
        for o in range(far):
            out_ref[o, pl.ds(j, own, stride=tiles), :] = half_ref[o * own : (o + 1) * own, :]
    for slot in range(far // 2):
        mine_ref[slot] = out_ref[pair_place(place_ref[0], 0, slot)]
        other_ref[slot] = out_ref[pair_place(place_ref[0], 1, slot)].astype(BF)


def pair_sum_kernel(mine_ref, other_ref, kept_ref, *slot_refs):
    kept_ref[...] = mine_ref[0] + other_ref[0].astype(F32)
    for slot, ref in enumerate(slot_refs, 1):
        ref[...] = (mine_ref[slot] + other_ref[slot].astype(F32)).astype(BF)


def last_kernel(all_ref, feature_ref, *refs):
    far_refs = refs[: FAR_SIZE // 2]
    gwo_ref, gwi_ref, gsel_ref, gdt_ref, galog_ref, gvec_ref, gmod_ref, sum_ref, rest_ref = refs[
        FAR_SIZE // 2 :
    ]
    far = FAR_SIZE
    own, width = gwo_ref.shape
    tiles = width // LANES
    near = all_ref.shape[0] // far
    part = width // near
    sum_ref[...] = total([ref[...].astype(F32) for ref in far_refs])
    for j in range(tiles):
        gwo_ref[:, cut(j)] = sum_ref[pl.ds(j, own, stride=tiles), :]
    rest = []
    for m in range(near):
        cores = [
            total([all_ref[o * near + m].astype(F32) for o in range(far) if o // 2 % 2 == core])
            for core in (0, 1)
        ]
        gwi_ref[:, part * m : part * (m + 1)] = (cores[0] + cores[1])[:own, :part]
        rest.append(cores)
    rest_ref[: 2 * SLOT, :] = total([c[0] for c in rest])
    rest_ref[2 * SLOT :, :] = total([c[1] for c in rest])
    vec = rest_ref[own : own + 1, :] + rest_ref[2 * SLOT + own : 2 * SLOT + own + 1, :]
    turned = jnp.broadcast_to(vec, (LANES, LANES)).T
    gmod_ref[...] = turned[: 2 * own, :1] * feature_ref[...].reshape(1, -1).astype(F32)
    gsel_ref[...] = rest_ref[SLOT : SLOT + own, :]
    rank, states = gdt_ref.shape[1], galog_ref.shape[1]
    base = 3 * SLOT
    gdt_ref[...] = rest_ref[base : base + own, :rank]
    galog_ref[...] = rest_ref[base : base + own, rank : rank + states]
    turned = jnp.concatenate([rest_ref[base : base + own, :], jnp.zeros((LANES - own, LANES), F32)])
    gvec_ref[...] = turned.T[rank + states : rank + states + 8, :own]


def permute(value, axes, k):
    if k == 0:
        return value
    return lax.ppermute(value, axes, [(i, i ^ k) for i in range(lax.axis_size(axes))])


def exchange(value, axes):
    return lax.all_to_all(value, axes, split_axis=0, concat_axis=0, tiled=True)


def local(
    latent,
    out_grad,
    w_in,
    w_out,
    w_select,
    w_dt,
    dt_bias,
    a_log,
    d_skip,
    w_mod,
    t_index,
    frame_order,
    row_order,
    col_order,
):
    frames, rows, cols, width = latent.shape
    inner = w_in.shape[1]
    tokens = frames * rows * cols
    tiles = inner // LANES
    states = a_log.shape[1]
    n_row, n_col = lax.axis_size(ROW), lax.axis_size(COL)
    near, far = lax.axis_size(NEAR), lax.axis_size(FAR)
    own = width // (near * far)
    features = jax.nn.silu(time_features(t_index, w_mod.shape[1])).astype(BF)

    def packed(parts):
        return ((parts, 2, tokens * tiles // parts, LANES), BF)

    slot = ((1, 2, tokens * tiles // n_row, LANES), BF)
    place = lax.axis_index(ROW).astype(jnp.int32)[None]
    far_place = lax.axis_index(FAR).astype(jnp.int32)[None]
    data_own, data_wide, *slots, both, pre_act, modulation, cot, flat_latent = call(
        pre_kernel,
        "norm_project",
        [
            packed(1),
            packed(n_col),
            slot,
            slot,
            slot,
            slot,
            ((2, tokens, width), BF),
            ((tokens, inner), F32),
            ((8, 2 * width), F32),
            ((tokens, inner), BF),
            ((tokens, width), BF),
        ],
        [((tokens * tiles, LANES), F32)],
        VMEM_ALL,
        7e9,
        (place, w_mod, features, latent, w_in, out_grad, w_out),
        smem=(0,),
        late=(3, 4, 5, 6),
        early=tuple(range(11)),
    )
    data_wide = exchange(data_wide, COL)
    slots = [permute(value, ROW, k) for k, value in enumerate(slots)]
    both_near = lax.all_gather(both, NEAR, axis=0, tiled=False)
    params = (
        w_select,
        w_dt.T,
        dt_bias,
        a_log.T,
    )
    area = rows * cols

    def time_row(at, line, place):
        return at * area + line

    def wide_row(at, line, place):
        chunk = frames // n_col * area
        return (
            lax.div(at, cols) * chunk
            + lax.rem(at, cols)
            + lax.div(line, rows) * area
            + lax.rem(line, rows) * cols
        )

    def tall_row(at, line, place):
        chunk = frames // n_row * area
        return (
            (lax.div(at, rows) ^ place) * chunk
            + lax.rem(at, rows) * cols
            + lax.div(line, cols) * area
            + lax.rem(line, cols)
        )

    out_tall, grads_tall = direction(
        "scan_height", rows * n_row, tall_row, row_order, place, slots, params
    )
    out_slots = [permute(value, ROW, k) for k, value in enumerate(out_tall)]
    data_wide, _ = lax.optimization_barrier((data_wide, out_tall))
    (out_wide,), grads_wide = direction(
        "scan_width", cols * n_col, wide_row, col_order, place, [data_wide], params
    )
    data_time, out_slots, _ = lax.optimization_barrier((data_own, out_slots, out_wide))
    out_wide = exchange(out_wide, COL)
    (out_time,), grads_time = direction(
        "scan_time", frames, time_row, frame_order, place, [data_time], params
    )
    mixed, grad_act, near_send = call(
        post_kernel,
        "sum_directions",
        [
            ((tokens, inner), BF),
            ((tokens, inner), BF),
            ((near, 2 * inner // near, LANES), BF),
        ],
        [
            ((tokens * tiles, LANES), F32),
            ((2, inner, LANES), F32),
            ((inner, LANES), F32),
        ],
        VMEM_ALL,
        6e9,
        (place, grads_time[0], cot, out_time, out_wide, *out_slots, pre_act, d_skip),
        smem=(0,),
        early=(0, 1),
    )
    near_recv = exchange(near_send, NEAR)
    data_own, _ = lax.optimization_barrier((data_own, near_send))
    mine, other = call(
        small_kernel,
        "small_sums",
        [((inner, LANES), F32), ((inner, LANES), BF)],
        [((tokens * tiles, LANES), F32), ((2, inner, LANES), F32)],
        VMEM_ALL,
        3e9,
        (place, data_own, *grads_time, *grads_wide, *grads_tall),
        smem=(0,),
    )
    other = permute(other, ROW, 1)
    branch, latent_grad, vec = call(
        finish_kernel,
        "out_projections",
        [(latent.shape, BF), (latent.shape, BF), ((near * far, LANES), F32)],
        [],
        VMEM_ALL,
        6e9,
        (mixed, grad_act, flat_latent, modulation, w_in, w_out),
        late=(4, 5),
    )
    near_recv, vec, mine, other = lax.optimization_barrier((near_recv, vec, mine, other))
    piece = own * tiles
    all_send = call(
        in_grad_kernel,
        "in_weight_grad",
        [((near * far, 2 * SLOT, LANES), BF)],
        [((inner // near, near * tokens), BF), ((near * far * 2 * SLOT, LANES), F32)],
        VMEM_ALL,
        3e9,
        (near_recv, both_near, mine, other, vec),
        late=(1, 2, 3, 4),
        pieces={1: PIECES},
        choose={1: 0},
    )[0]
    all_recv = exchange(all_send, FAR + NEAR)
    mine, other = call(
        out_grad_kernel,
        "out_weight_grad",
        [((far // 2, piece, LANES), F32), ((far // 2, piece, LANES), BF)],
        [
            ((inner // near, near * tokens), BF),
            ((far, piece, LANES), F32),
            ((inner // near, LANES), F32),
        ],
        VMEM_ALL,
        4e9,
        (far_place, near_recv, both_near),
        smem=(0,),
        late=(2,),
        pieces={2: PIECES},
        choose={2: 1},
    )
    other = permute(other, FAR, 2)
    far_send = plain_call(
        pair_sum_kernel,
        "pair_sums",
        [((piece, LANES), F32)] + [((piece, LANES), BF)] * (far // 2 - 1),
        [],
        8,
        1e9,
        (mine, other),
    )
    far_recv = [permute(value, FAR, (0, 1, 4, 5)[slot]) for slot, value in enumerate(far_send)]
    rank = w_dt.shape[1]
    grad_w_out, grad_w_in, grad_select, grad_dt, grad_alog, grad_vec, grad_mod = plain_call(
        last_kernel,
        "weight_sums",
        [
            ((own, width), F32),
            ((own, width), F32),
            ((own, LANES), F32),
            ((own, rank), F32),
            ((own, states), F32),
            ((8, own), F32),
            ((2 * own, features.shape[0]), F32),
        ],
        [((piece, LANES), F32), ((4 * SLOT, LANES), F32)],
        16,
        1e9,
        (all_recv, features, *far_recv),
    )
    return (
        branch,
        latent_grad,
        grad_w_in,
        grad_w_out,
        grad_select,
        grad_dt,
        grad_vec[0],
        grad_alog,
        grad_vec[1],
        grad_mod,
    )


def solution(mesh):
    n_row, n_col = mesh.shape["row"], mesh.shape["col"]
    split = Mesh(mesh.devices.reshape(n_row // 2, 2, 2, 4, n_col // 8), AXES)
    tokens = P(None, ROW, COL, None)
    matrix = P(ROW + COL, None)
    vector = P(ROW + COL)
    return jax.shard_map(
        local,
        mesh=split,
        in_specs=(tokens, tokens) + (P(),) * 12,
        out_specs=(
            tokens,
            tokens,
            matrix,
            matrix,
            matrix,
            matrix,
            vector,
            matrix,
            vector,
            matrix,
        ),
        check_vma=False,
    )
```
